32 devices in a mesh: dp: 8 (over z, y), blk: 4 (over x, core).
Axes of the slice: x: 2, y: 2, z: 4, core: 2. Of those that a mesh axis runs over, the one named last changes fastest.
Arguments:
- tokens: bfloat16 [8, 1024, 512], P('dp', 'blk'), may hold values from -6 to 6
- segments: int32 [8, 1024], P('dp', 'blk'), may hold values from 0 to 4, as said below
- memory_init: float32 [20, 512], P(None, ('dp', 'blk')), may hold values from -6 to 6
- attn_weights: float32 [2, 12, 512, 512], P(None, None, ('dp', 'blk'))
- ffn_in: float32 [2, 512, 2048], P(None, ('dp', 'blk')), may hold values from -0.25 to 0.25
- ffn_out: float32 [2, 2048, 512], P(None, ('dp', 'blk')), may hold values from -0.125 to 0.125
- ffn_bias: float32 [2, 2048], P(None, ('dp', 'blk')), may hold values from -3 to 3
- norm_gain: float32 [2, 4, 512], P(None, None, ('dp', 'blk')), may hold values from 0.5 to 1.5
- norm_shift: float32 [2, 5, 512], P(None, None, ('dp', 'blk')), may hold values from -1.8 to 1.8
- out_grad: bfloat16 [8, 1024, 512], P('dp', 'blk'), may hold values from -6 to 6
- memory_cot: bfloat16 [8, 20, 512], P('dp'), may hold values from -6 to 6
Outputs:
- result: bfloat16 [8, 1024, 512], P('dp', 'blk')
- memory_out: float32 [8, 20, 512], P('dp')
- tokens_grad: float32 [8, 1024, 512], P('dp', 'blk')
- memory_init_grad: float32 [20, 512], P(None, ('dp', 'blk'))
- attn_weights_grad: float32 [2, 12, 512, 512], P(None, None, ('dp', 'blk'))
- ffn_in_grad: float32 [2, 512, 2048], P(None, ('dp', 'blk'))
- ffn_out_grad: float32 [2, 2048, 512], P(None, ('dp', 'blk'))
- ffn_bias_grad: float32 [2, 2048], P(None, ('dp', 'blk'))
- norm_gain_grad: float32 [2, 4, 512], P(None, None, ('dp', 'blk'))
- norm_shift_grad: float32 [2, 5, 512], P(None, None, ('dp', 'blk'))
The draws below stay inside these ranges and needn't reach their ends.
Inputs may be any that keep to these rules, and one draw needn't show every extreme that they name: `segments`: in each row the document numbers start at 0 at position 0 and rise by one at exactly four positions: one in 1 to 63, one in 64 to 127, one in 896 to 959, and one in 960 to 1023.
All inputs are finite; a program needn't handle non-finite values.
Results may differ from the reference program's by a relative error of at most 0.03.
Values may be sent and summed in bfloat16 or wider, within the bound.
No kernel may reach another device: no remote copies, remote signals or barrier semaphores. Data moves between devices by JAX's collectives and lax.ppermute only.
A program may use at most 192 MiB of HBM per device.

```python
import math
import jax
import jax.numpy as jnp
from jax import lax

D = 512
FF = 2048
HEADS = 8
HEAD = 64
MEM = 20
LAYERS = 2
TOK_DEV = 256
LENGTH = 1024
ROWS = 8


def draw_segments(key, part):
    key = jax.random.fold_in(key, 11)
    quarter = max(TOK_DEV // 4, 2)
    first_key, second_key, third_key, fourth_key = jax.random.split(key, 4)
    shape = (ROWS, 1)
    cuts = [jax.random.randint(first_key, shape, 1, quarter), jax.random.randint(second_key, shape, quarter, 2 * quarter), jax.random.randint(third_key, shape, LENGTH - 2 * quarter, LENGTH - quarter), jax.random.randint(fourth_key, shape, LENGTH - quarter, LENGTH)]
    place = jnp.arange(LENGTH, dtype=jnp.int32)[None, :]
    ids = jnp.zeros((ROWS, LENGTH), jnp.int32)
    for cut in cuts:
        ids = ids + (place >= cut).astype(jnp.int32)
    return ids


def draw_attn_weights(key, part):
    key = jax.random.fold_in(key, 7)
    shape = (LAYERS, 12, D, D)
    base = jax.random.normal(key, shape, jnp.float32)
    slot = jnp.arange(12)
    factor = jnp.where(slot == 11, 2.0, jnp.where(slot % 4 == 3, math.sqrt(LENGTH / 4.0), 1.0)).astype(jnp.float32)
    return base * factor[None, :, None, None] / math.sqrt(D)


def shard_levels(own_key, shape, pieces, smallest, largest):
    loudness = 1.0
    for dim, shards_of in pieces:
        steps = jax.random.uniform(jax.random.fold_in(jax.random.fold_in(own_key, 6), dim), (shards_of,), jnp.float32, smallest / len(pieces), largest / len(pieces))
        loudness = loudness * jnp.repeat(jnp.exp(steps), shape[dim] // shards_of).reshape((-1,) + (1,) * (len(shape) - 1 - dim))
    return loudness


def centred(rng, shape, deviation, reach, cuts=(), held_as=jnp.bfloat16):
    array = jax.random.normal(rng, shape, jnp.float32) * deviation
    if len(cuts) > 0:
        array = shard_levels(rng, shape, cuts, -0.22, 0.18) * array
    return jnp.clip(array, min=-reach, max=reach).astype(held_as)


def setup_inputs(seed: int = 0) -> dict:
    splits = jax.random.split(jax.random.key(seed), 12)
    tokens = centred(splits[0], (ROWS, LENGTH, D), 1.0, 6.0, ((0, 8), (1, 4)))
    segments = draw_segments(jax.random.fold_in(splits[11], 71), 0)
    memory_init = centred(splits[2], (MEM, D), 1.0, 6.0, ((1, 32),), jnp.float32)
    attn_weights = draw_attn_weights(jax.random.fold_in(splits[11], 71), 0)
    ffn_in = centred(splits[4], (LAYERS, D, FF), D ** -0.5, 0.25, ((1, 32),), jnp.float32)
    ffn_out = centred(splits[5], (LAYERS, FF, D), FF ** -0.5, 0.125, ((1, 32),), jnp.float32)
    ffn_bias = centred(splits[6], (LAYERS, FF), 0.5, 3.0, ((1, 32),), jnp.float32)
    norm_gain = jnp.clip(1.0 + 0.1 * jax.random.normal(splits[7], (LAYERS, 4, D), jnp.float32), 0.5, 1.5)
    norm_shift = centred(splits[8], (LAYERS, 5, D), 0.3, 1.8, ((2, 32),), jnp.float32)
    out_grad = centred(splits[9], (ROWS, LENGTH, D), 1.0, 6.0, ((0, 8), (1, 4)))
    memory_cot = centred(splits[10], (ROWS, MEM, D), 1.0, 6.0, ((0, 8),))
    return {"tokens": tokens, "segments": segments, "memory_init": memory_init, "attn_weights": attn_weights, "ffn_in": ffn_in, "ffn_out": ffn_out, "ffn_bias": ffn_bias, "norm_gain": norm_gain, "norm_shift": norm_shift, "out_grad": out_grad, "memory_cot": memory_cot}


@jax.custom_vjp
def low(v):
    return lax.optimization_barrier(v.astype(jnp.bfloat16)).astype(jnp.float32)

@jax.custom_vjp
def low_back(v):
    return v

def low_keep(v):
    return (low(v), None)

def low_pass(kept, grad):
    return (grad,)

def back_keep(v):
    return (v, None)

def back_low(kept, grad):
    return (low(grad),)
low.defvjp(low_keep, low_pass)
low_back.defvjp(back_keep, back_low)
NEG = -1000000000.0
EPS = 1e-05
HIGH = lax.Precision.HIGHEST

def rounded(value):
    return low(low_back(value))

def product(left, right):
    return jnp.dot(left, right, precision=HIGH, preferred_element_type=jnp.float32)

def stacked_product(inputs, weights):
    return jnp.einsum('nd,jde->jne', inputs, weights, precision=HIGH)

def heads(matrix):
    return matrix.reshape(matrix.shape[0], HEADS, HEAD).transpose(1, 0, 2)

def unheads(tensor):
    return tensor.transpose(1, 0, 2).reshape(tensor.shape[1], HEADS * HEAD)

def normalize(values, gain, shift):
    center = values - lax.optimization_barrier(jnp.mean(values, -1, keepdims=True))
    spread = lax.optimization_barrier(jnp.mean(center * center, -1, keepdims=True))
    return center * lax.rsqrt(spread + EPS) * gain + shift

def attend(query, keys, values, allowed):
    raw = jnp.einsum('hqe,hke->hqk', query, keys, precision=HIGH)
    scores = low_back(raw * HEAD ** (-0.5))
    if allowed is not None:
        scores = jnp.where(allowed[None], scores, NEG)
    highest = lax.optimization_barrier(jnp.max(scores, -1, keepdims=True))
    expo = jnp.exp(scores - highest)
    probs = low(expo / lax.optimization_barrier(jnp.sum(expo, -1, keepdims=True)))
    return jnp.einsum('hqk,hke->hqe', probs, values, precision=HIGH)

def layer(seq_in, mem_in, segs, matrices, ffn_up, ffn_down, up_bias, gains, shifts):
    joint = jnp.concatenate([mem_in, seq_in], 0)
    joint_low = low(joint)
    qkv = rounded(stacked_product(joint_low, matrices[0:3]))
    query, keys, values = (heads(qkv[0]), heads(qkv[1]), heads(qkv[2]))
    mem_att = attend(query[:, :MEM], keys, values, None)
    length = seq_in.shape[0]
    blocks = length // TOK_DEV
    seq_query = query[:, MEM:].reshape(HEADS, blocks, TOK_DEV, HEAD).transpose(1, 0, 2, 3)
    seg_blocks = segs.reshape(blocks, TOK_DEV)

    def one_block(inputs):
        block_query, block_segs = inputs
        allowed = jnp.concatenate([jnp.zeros((TOK_DEV, MEM), jnp.int32) == 0, block_segs[:, None] == segs[None, :]], 1)
        return attend(block_query, keys, values, allowed)
    seq_att = lax.map(jax.checkpoint(one_block), (seq_query, seg_blocks))
    seq_att = seq_att.transpose(1, 0, 2, 3).reshape(HEADS, length, HEAD)
    att = rounded(unheads(jnp.concatenate([mem_att, seq_att], 1)))
    joint_one = normalize(joint + low_back(product(att, matrices[3])), gains[0], shifts[0])
    mem_one, seq_one = (joint_one[:MEM], joint_one[MEM:])
    mem_one_low, seq_one_low = (low(mem_one), low(seq_one))
    read_query = heads(rounded(product(mem_one_low, matrices[4])))
    read_kv = rounded(stacked_product(seq_one_low, matrices[5:7]))
    read_att = rounded(unheads(attend(read_query, heads(read_kv[0]), heads(read_kv[1]), None)))
    mem_two = normalize(mem_one + low_back(product(read_att, matrices[7])), gains[1], shifts[1])
    mem_two_low = low(mem_two)
    write_query = heads(rounded(product(seq_one_low, matrices[8])))
    write_kv = rounded(stacked_product(mem_two_low, matrices[9:11]))
    write_att = rounded(unheads(attend(write_query, heads(write_kv[0]), heads(write_kv[1]), None)))
    seq_two = normalize(seq_one + low_back(product(write_att, matrices[11])), gains[2], shifts[2])
    feed_low = jnp.concatenate([mem_two_low, low(seq_two)], 0)
    hidden = low(jax.nn.gelu(low_back(product(feed_low, ffn_up) + up_bias)))
    joint_two = jnp.concatenate([mem_two, seq_two], 0)
    joint_three = normalize(joint_two + low_back(product(hidden, ffn_down) + shifts[4]), gains[3], shifts[3])
    return (joint_three[MEM:], joint_three[:MEM])

def forward(params, row_tokens, segs):
    memory, matrices, ffn_up, ffn_down, up_bias, gains, shifts = [low(part) for part in params]
    seq_state, mem_state = (row_tokens, memory)
    for index in range(LAYERS):
        seq_state, mem_state = layer(seq_state, mem_state, segs, matrices[index], ffn_up[index], ffn_down[index], up_bias[index], gains[index], shifts[index])
    return (seq_state, mem_state)

def reference(tokens, segments, memory_init, attn_weights, ffn_in, ffn_out, ffn_bias, norm_gain, norm_shift, out_grad, memory_cot):
    params = (memory_init, attn_weights, ffn_in, ffn_out, ffn_bias, norm_gain, norm_shift)

    def one_row(carry, inputs):
        row_tokens, row_segs, row_cot, row_mem_cot = inputs
        outputs, pull = jax.vjp(lambda weights, start: forward(weights, start, row_segs), params, row_tokens.astype(jnp.float32))
        param_grads, token_grad = pull((row_cot.astype(jnp.float32), row_mem_cot.astype(jnp.float32)))
        carry = jax.tree.map(jnp.add, carry, param_grads)
        return (carry, (outputs[0].astype(jnp.bfloat16), outputs[1], token_grad))
    zeros = jax.tree.map(jnp.zeros_like, params)
    grads, outs = lax.scan(one_row, zeros, (tokens, segments, out_grad, memory_cot))
    return (outs[0], outs[1], outs[2], grads[0], grads[1], grads[2], grads[3], grads[4], grads[5], grads[6])
```

```python
import jax
import jax.numpy as jnp
from jax import lax
from jax.sharding import PartitionSpec as P

HEADS = 8
HEAD = 64
MEM = 20


NEG = -1000000000.0
EPS = 1e-05


def combined_all(array, axis, join):
    highest, total, accum = array
    packed = jnp.concatenate([accum, highest[..., None], total[..., None]], -1)
    gathered = lax.all_gather(packed, axis)
    width = accum.shape[-1]
    state = None
    for source in range(lax.axis_size(axis)):
        part = gathered[source]
        part = (part[..., width], part[..., width + 1], part[..., :width])
        state = part if state is None else join(state, part)
    return state


def for_sending(array):

    def short(part):
        return part.astype(jnp.bfloat16) if part.dtype == jnp.float32 else part

    return jax.tree.map(short, array)


def passed_along(value, axis, steps):
    count = lax.axis_size(axis)
    pairs = [(source, (source + steps) % count) for source in range(count)]
    return lax.ppermute(value, axis, pairs)


def split_heads(matrix):
    return matrix.reshape(matrix.shape[0], HEADS, HEAD).transpose(1, 0, 2)


def join_heads(tensor):
    return tensor.transpose(1, 0, 2).reshape(tensor.shape[1], HEADS * HEAD)


def normalize(values, gain, shift):
    center = values - jnp.mean(values, -1, keepdims=True)
    spread = jnp.mean(center * center, -1, keepdims=True)
    return center * lax.rsqrt(spread + EPS) * gain + shift


def norm_back(values, gain, shift, grad):
    output, pull = jax.vjp(normalize, values, gain, shift)
    return pull(grad)


def linear(inputs, weight):
    return jnp.dot(inputs, weight, preferred_element_type=jnp.float32)


def stacked_linear(inputs, weights):
    return jnp.einsum("nd,jde->jne", inputs, weights, preferred_element_type=jnp.float32).astype(
        jnp.bfloat16
    )


def weight_grad(inputs, grads):
    return jnp.einsum("nd,ne->de", inputs, grads, preferred_element_type=jnp.float32)


def input_grad(grads, weight):
    return jnp.einsum("ne,de->nd", grads, weight, preferred_element_type=jnp.float32)


def mixed_grad(inputs, grads, share):
    return share * weight_grad(inputs[:MEM], grads[:MEM]) + weight_grad(inputs[MEM:], grads[MEM:])


def row_total(grads, share):
    values = grads.astype(jnp.float32)
    return share * jnp.sum(values[:MEM], 0) + jnp.sum(values[MEM:], 0)


def scores_of(query, keys, allowed):
    raw = jnp.einsum("hqe,hke->hqk", query, keys, preferred_element_type=jnp.float32) * HEAD ** (
        -0.5
    )
    if allowed is None:
        return raw
    return jnp.where(allowed[None], raw, NEG)


def fresh(query):
    count, rows, width = query.shape
    return (
        jnp.full((count, rows), -1e30, jnp.float32),
        jnp.zeros((count, rows), jnp.float32),
        jnp.zeros((count, rows, width), jnp.float32),
    )


def absorb(state, query, keys, values, allowed):
    highest, total, accum = state
    scores = scores_of(query, keys, allowed)
    summit = jnp.maximum(highest, jnp.max(scores, -1))
    weights = jnp.exp(scores - summit[..., None])
    fade = jnp.exp(highest - summit)
    total = total * fade + jnp.sum(weights, -1)
    accum = accum * fade[..., None] + jnp.einsum(
        "hqk,hke->hqe", weights.astype(jnp.bfloat16), values, preferred_element_type=jnp.float32
    )
    return (summit, total, accum)


def combine_parts(first, second):
    summit = jnp.maximum(first[0], second[0])
    fade_one = jnp.exp(first[0] - summit)
    fade_two = jnp.exp(second[0] - summit)
    return (
        summit,
        first[1] * fade_one + second[1] * fade_two,
        first[2] * fade_one[..., None] + second[2] * fade_two[..., None],
    )


def finish(state):
    highest, total, accum = state
    return (accum / total[..., None], highest + jnp.log(total))


def memory_over_sequence(query, keys, values):
    part = absorb(fresh(query), query, keys, values, None)
    return combined_all(part, "blk", combine_parts)


def memory_total(parts):
    return jax.tree.map(lambda part: part.astype(jnp.float32), lax.psum(for_sending(parts), "blk"))


def attend_back(query, keys, values, allowed, log_total, out_low, delta):
    scores = scores_of(query, keys, allowed)
    probs = jnp.exp(scores - log_total[..., None])
    prob_grad = jnp.einsum("hqe,hke->hqk", out_low, values, preferred_element_type=jnp.float32)
    score_grad = (probs * (prob_grad - delta[..., None])).astype(jnp.bfloat16)
    query_grad = jnp.einsum(
        "hqk,hke->hqe", score_grad, keys, preferred_element_type=jnp.float32
    ) * HEAD ** (-0.5)
    key_grad = jnp.einsum(
        "hqk,hqe->hke", score_grad, query, preferred_element_type=jnp.float32
    ) * HEAD ** (-0.5)
    value_grad = jnp.einsum(
        "hqk,hqe->hke", probs.astype(jnp.bfloat16), out_low, preferred_element_type=jnp.float32
    )
    return (query_grad, key_grad, value_grad)


def layer_forward(seq_in, mem_in, seg_float, params):
    matrices, ffn_up, ffn_down, up_bias, gains, shifts = params
    gains = gains.astype(jnp.float32)
    shifts = shifts.astype(jnp.float32)
    seq_low = seq_in.astype(jnp.bfloat16)
    mem_low = mem_in.astype(jnp.bfloat16)
    seq_qkv = stacked_linear(seq_low, matrices[0:3])
    mem_qkv = stacked_linear(mem_low, matrices[0:3])
    seq_query, seq_keys, seq_values = (
        split_heads(seq_qkv[0]),
        split_heads(seq_qkv[1]),
        split_heads(seq_qkv[2]),
    )
    mem_query, mem_keys, mem_values = (
        split_heads(mem_qkv[0]),
        split_heads(mem_qkv[1]),
        split_heads(mem_qkv[2]),
    )
    state = absorb(fresh(seq_query), seq_query, mem_keys, mem_values, None)
    travel = (seq_keys, seq_values, seg_float)
    for step in range(lax.axis_size("blk")):
        allowed = seg_float[:, None] == travel[2][None, :]
        state = absorb(state, seq_query, travel[0], travel[1], allowed)
        if step + 1 < lax.axis_size("blk"):
            travel = passed_along((travel[0], travel[1], travel[2]), "blk", 1)
    seq_out, seq_lse = finish(state)
    mem_state = memory_over_sequence(mem_query, seq_keys, seq_values)
    mem_state = absorb(mem_state, mem_query, mem_keys, mem_values, None)
    mem_out, mem_lse = finish(mem_state)
    full_low = jnp.concatenate([join_heads(mem_out), join_heads(seq_out)], 0).astype(jnp.bfloat16)
    joint_pre = jnp.concatenate([mem_in, seq_in], 0) + linear(full_low, matrices[3])
    joint_one = normalize(joint_pre, gains[0], shifts[0])
    mem_one, seq_one = (joint_one[:MEM], joint_one[MEM:])
    mem_one_low = mem_one.astype(jnp.bfloat16)
    seq_one_low = seq_one.astype(jnp.bfloat16)
    read_query = split_heads(linear(mem_one_low, matrices[4]).astype(jnp.bfloat16))
    read_kv = stacked_linear(seq_one_low, matrices[5:7])
    read_keys, read_values = (split_heads(read_kv[0]), split_heads(read_kv[1]))
    read_out, read_lse = finish(memory_over_sequence(read_query, read_keys, read_values))
    read_low = join_heads(read_out).astype(jnp.bfloat16)
    mem_pre = mem_one + linear(read_low, matrices[7])
    mem_two = normalize(mem_pre, gains[1], shifts[1])
    mem_two_low = mem_two.astype(jnp.bfloat16)
    write_query = split_heads(linear(seq_one_low, matrices[8]).astype(jnp.bfloat16))
    write_kv = stacked_linear(mem_two_low, matrices[9:11])
    write_keys, write_values = (split_heads(write_kv[0]), split_heads(write_kv[1]))
    write_out, write_lse = finish(
        absorb(fresh(write_query), write_query, write_keys, write_values, None)
    )
    write_low = join_heads(write_out).astype(jnp.bfloat16)
    seq_pre = seq_one + linear(write_low, matrices[11])
    seq_two = normalize(seq_pre, gains[2], shifts[2])
    feed_low = jnp.concatenate([mem_two_low, seq_two.astype(jnp.bfloat16)], 0)
    hidden_pre = linear(feed_low, ffn_up) + up_bias.astype(jnp.float32)
    hidden_low = jax.nn.gelu(hidden_pre).astype(jnp.bfloat16)
    feed_pre = jnp.concatenate([mem_two, seq_two], 0) + linear(hidden_low, ffn_down) + shifts[4]
    joint_three = normalize(feed_pre, gains[3], shifts[3])
    saved = dict(
        seq_low=seq_low,
        mem_low=mem_low,
        seq_query=seq_query,
        seq_keys=seq_keys,
        seq_values=seq_values,
        mem_query=mem_query,
        mem_keys=mem_keys,
        mem_values=mem_values,
        seq_out=seq_out,
        seq_lse=seq_lse,
        mem_out=mem_out,
        mem_lse=mem_lse,
        full_low=full_low,
        joint_pre=joint_pre,
        mem_one_low=mem_one_low,
        seq_one_low=seq_one_low,
        read_query=read_query,
        read_keys=read_keys,
        read_values=read_values,
        read_out=read_out,
        read_lse=read_lse,
        read_low=read_low,
        mem_pre=mem_pre,
        mem_two_low=mem_two_low,
        write_query=write_query,
        write_keys=write_keys,
        write_values=write_values,
        write_out=write_out,
        write_lse=write_lse,
        write_low=write_low,
        seq_pre=seq_pre,
        feed_low=feed_low,
        hidden_pre=hidden_pre,
        hidden_low=hidden_low,
        feed_pre=feed_pre,
    )
    return (joint_three[MEM:], joint_three[:MEM], saved)


def layer_backward(seq_grad, mem_grad, seg_float, params, saved):
    matrices, ffn_up, ffn_down, up_bias, gains, shifts = params
    gains = gains.astype(jnp.float32)
    shifts = shifts.astype(jnp.float32)
    share = 1.0 / lax.axis_size("blk")
    matrix_grads = [None] * 12
    feed_pre = saved["feed_pre"]
    mem_feed, gain_three_mem, shift_three_mem = norm_back(
        feed_pre[:MEM], gains[3], shifts[3], mem_grad
    )
    seq_feed, gain_three_seq, shift_three_seq = norm_back(
        feed_pre[MEM:], gains[3], shifts[3], seq_grad
    )
    feed_grad_low = jnp.concatenate([mem_feed, seq_feed], 0).astype(jnp.bfloat16)
    down_bias_grad = row_total(feed_grad_low, share)
    down_grad = mixed_grad(saved["hidden_low"], feed_grad_low, share)
    hidden_grad = input_grad(feed_grad_low, ffn_down)
    gelu_out, gelu_pull = jax.vjp(jax.nn.gelu, saved["hidden_pre"])
    pre_grad_low = gelu_pull(hidden_grad)[0].astype(jnp.bfloat16)
    bias_grad = row_total(pre_grad_low, share)
    up_grad = mixed_grad(saved["feed_low"], pre_grad_low, share)
    feed_in_grad = input_grad(pre_grad_low, ffn_up)
    mem_two_grad = mem_feed + feed_in_grad[:MEM]
    seq_two_grad = seq_feed + feed_in_grad[MEM:]
    seq_pre_grad, gain_two, shift_two = norm_back(
        saved["seq_pre"], gains[2], shifts[2], seq_two_grad
    )
    write_grad_low = seq_pre_grad.astype(jnp.bfloat16)
    matrix_grads[11] = weight_grad(saved["write_low"], write_grad_low)
    write_out_low = split_heads(input_grad(write_grad_low, matrices[11]).astype(jnp.bfloat16))
    delta = jnp.sum(write_out_low.astype(jnp.float32) * saved["write_out"], -1)
    query_grad, key_grad, value_grad = attend_back(
        saved["write_query"],
        saved["write_keys"],
        saved["write_values"],
        None,
        saved["write_lse"],
        write_out_low,
        delta,
    )
    key_grad, value_grad = memory_total((key_grad, value_grad))
    query_low = join_heads(query_grad).astype(jnp.bfloat16)
    key_low = join_heads(key_grad).astype(jnp.bfloat16)
    value_low = join_heads(value_grad).astype(jnp.bfloat16)
    matrix_grads[8] = weight_grad(saved["seq_one_low"], query_low)
    matrix_grads[9] = share * weight_grad(saved["mem_two_low"], key_low)
    matrix_grads[10] = share * weight_grad(saved["mem_two_low"], value_low)
    seq_one_grad = seq_pre_grad + input_grad(query_low, matrices[8])
    mem_two_grad = (
        mem_two_grad + input_grad(key_low, matrices[9]) + input_grad(value_low, matrices[10])
    )
    mem_pre_grad, gain_one, shift_one = norm_back(
        saved["mem_pre"], gains[1], shifts[1], mem_two_grad
    )
    read_grad_low = mem_pre_grad.astype(jnp.bfloat16)
    matrix_grads[7] = share * weight_grad(saved["read_low"], read_grad_low)
    read_out_low = split_heads(input_grad(read_grad_low, matrices[7]).astype(jnp.bfloat16))
    delta = jnp.sum(read_out_low.astype(jnp.float32) * saved["read_out"], -1)
    query_grad, key_grad, value_grad = attend_back(
        saved["read_query"],
        saved["read_keys"],
        saved["read_values"],
        None,
        saved["read_lse"],
        read_out_low,
        delta,
    )
    query_grad = memory_total((query_grad,))[0]
    query_low = join_heads(query_grad).astype(jnp.bfloat16)
    key_low = join_heads(key_grad).astype(jnp.bfloat16)
    value_low = join_heads(value_grad).astype(jnp.bfloat16)
    matrix_grads[4] = share * weight_grad(saved["mem_one_low"], query_low)
    matrix_grads[5] = weight_grad(saved["seq_one_low"], key_low)
    matrix_grads[6] = weight_grad(saved["seq_one_low"], value_low)
    mem_one_grad = mem_pre_grad + input_grad(query_low, matrices[4])
    seq_one_grad = (
        seq_one_grad + input_grad(key_low, matrices[5]) + input_grad(value_low, matrices[6])
    )
    joint_pre = saved["joint_pre"]
    mem_joint, gain_zero_mem, shift_zero_mem = norm_back(
        joint_pre[:MEM], gains[0], shifts[0], mem_one_grad
    )
    seq_joint, gain_zero_seq, shift_zero_seq = norm_back(
        joint_pre[MEM:], gains[0], shifts[0], seq_one_grad
    )
    joint_grad_low = jnp.concatenate([mem_joint, seq_joint], 0).astype(jnp.bfloat16)
    matrix_grads[3] = mixed_grad(saved["full_low"], joint_grad_low, share)
    attn_grad = input_grad(joint_grad_low, matrices[3]).astype(jnp.bfloat16)
    mem_out_low = split_heads(attn_grad[:MEM])
    seq_out_low = split_heads(attn_grad[MEM:])
    mem_delta = jnp.sum(mem_out_low.astype(jnp.float32) * saved["mem_out"], -1)
    seq_delta = jnp.sum(seq_out_low.astype(jnp.float32) * saved["seq_out"], -1)
    seq_query, seq_keys, seq_values = (saved["seq_query"], saved["seq_keys"], saved["seq_values"])
    mem_query, mem_keys, mem_values = (saved["mem_query"], saved["mem_keys"], saved["mem_values"])
    seq_q_grad, mem_k_part, mem_v_part = attend_back(
        seq_query, mem_keys, mem_values, None, saved["seq_lse"], seq_out_low, seq_delta
    )
    travel = (seq_keys, seq_values, seg_float)
    moving = (jnp.zeros(seq_keys.shape, jnp.float32), jnp.zeros(seq_values.shape, jnp.float32))
    for step in range(lax.axis_size("blk")):
        allowed = seg_float[:, None] == travel[2][None, :]
        query_grad, key_grad, value_grad = attend_back(
            seq_query, travel[0], travel[1], allowed, saved["seq_lse"], seq_out_low, seq_delta
        )
        seq_q_grad = seq_q_grad + query_grad
        moving = (moving[0] + key_grad, moving[1] + value_grad)
        if step + 1 < lax.axis_size("blk"):
            travel = passed_along(
                (for_sending(travel[0]), for_sending(travel[1]), travel[2]), "blk", 1
            )
        moving = (
            passed_along(moving[0].astype(jnp.bfloat16), "blk", 1).astype(jnp.float32),
            passed_along(moving[1].astype(jnp.bfloat16), "blk", 1).astype(jnp.float32),
        )
    mem_q_part, key_grad, value_grad = attend_back(
        mem_query, seq_keys, seq_values, None, saved["mem_lse"], mem_out_low, mem_delta
    )
    seq_k_grad = moving[0] + key_grad
    seq_v_grad = moving[1] + value_grad
    mem_q_part, mem_k_part, mem_v_part = memory_total((mem_q_part, mem_k_part, mem_v_part))
    query_grad, key_grad, value_grad = attend_back(
        mem_query, mem_keys, mem_values, None, saved["mem_lse"], mem_out_low, mem_delta
    )
    mem_qkv_low = jnp.stack(
        [
            join_heads(mem_q_part + query_grad),
            join_heads(mem_k_part + key_grad),
            join_heads(mem_v_part + value_grad),
        ]
    ).astype(jnp.bfloat16)
    seq_qkv_low = jnp.stack(
        [join_heads(seq_q_grad), join_heads(seq_k_grad), join_heads(seq_v_grad)]
    ).astype(jnp.bfloat16)
    first_grads = share * jnp.einsum(
        "nd,jne->jde", saved["mem_low"], mem_qkv_low, preferred_element_type=jnp.float32
    )
    first_grads = first_grads + jnp.einsum(
        "nd,jne->jde", saved["seq_low"], seq_qkv_low, preferred_element_type=jnp.float32
    )
    matrix_grads[0], matrix_grads[1], matrix_grads[2] = (
        first_grads[0],
        first_grads[1],
        first_grads[2],
    )
    mem_in_grad = mem_joint + jnp.einsum(
        "jne,jde->nd", mem_qkv_low, matrices[0:3], preferred_element_type=jnp.float32
    )
    seq_in_grad = seq_joint + jnp.einsum(
        "jne,jde->nd", seq_qkv_low, matrices[0:3], preferred_element_type=jnp.float32
    )
    gain_grads = jnp.stack(
        [
            share * gain_zero_mem + gain_zero_seq,
            share * gain_one,
            gain_two,
            share * gain_three_mem + gain_three_seq,
        ]
    )
    shift_grads = jnp.stack(
        [
            share * shift_zero_mem + shift_zero_seq,
            share * shift_one,
            shift_two,
            share * shift_three_mem + shift_three_seq,
            down_bias_grad,
        ]
    )
    layer_grads = (jnp.stack(matrix_grads), up_grad, down_grad, bias_grad, gain_grads, shift_grads)
    return (seq_in_grad, mem_in_grad, layer_grads)


def local(
    tokens,
    segments,
    memory_init,
    attn_weights,
    ffn_in,
    ffn_out,
    ffn_bias,
    norm_gain,
    norm_shift,
    out_grad,
    memory_cot,
):
    layers, count, rows, width = attn_weights.shape
    per = ffn_in.shape[2] // width
    small = [ffn_bias, norm_gain, norm_shift, memory_init]
    sizes = [part.size for part in small]
    flat = jnp.concatenate([part.astype(jnp.bfloat16).reshape(-1) for part in small])
    blocks = -(-flat.size // (rows * width))
    flat = jnp.pad(flat, (0, blocks * rows * width - flat.size))
    packed = jnp.concatenate(
        [
            attn_weights.astype(jnp.bfloat16).reshape(layers * count, rows, width),
            ffn_in.astype(jnp.bfloat16).reshape(layers, rows, per, width).transpose(0, 2, 1, 3).reshape(-1, rows, width),
            ffn_out.astype(jnp.bfloat16).reshape(-1, rows, width),
            flat.reshape(blocks, rows, width),
        ]
    )
    everyone = lax.axis_size("dp") * lax.axis_size("blk")
    whole = lax.all_gather(packed, ("dp", "blk"), axis=1, tiled=True)
    one, two, three = (layers * count, layers * (count + per), layers * (count + 2 * per))
    full_small = whole[three:].reshape(blocks, everyone, rows * width).transpose(1, 0, 2).reshape(everyone, -1)
    starts = [sum(sizes[:k]) for k in range(5)]
    pieces = [full_small[:, starts[k] : starts[k + 1]].reshape((everyone,) + small[k].shape) for k in range(4)]
    full_pieces = [jnp.moveaxis(piece, 0, -2).reshape(piece.shape[1:-1] + (-1,)) for piece in pieces]
    gathered = (
        whole[:one].reshape(layers, count, width, width),
        whole[one:two].reshape(layers, per, width, width).transpose(0, 2, 1, 3).reshape(layers, width, per * width),
        whole[two:three].reshape(layers, per, everyone, rows, width).transpose(0, 2, 1, 3, 4).reshape(layers, per * width, width),
        full_pieces[0],
        full_pieces[1],
        full_pieces[2],
        full_pieces[3],
    )
    seg_float = segments[0].astype(jnp.bfloat16)
    seq_state = tokens[0].astype(jnp.float32)
    mem_state = gathered[6].astype(jnp.float32)
    kept = []
    for index in range(layers):
        params = tuple((member[index] for member in gathered[:6]))
        seq_state, mem_state, saved = layer_forward(seq_state, mem_state, seg_float, params)
        kept.append(saved)
    seq_grad = out_grad[0].astype(jnp.float32)
    mem_grad = memory_cot[0].astype(jnp.float32)
    share = 1.0 / lax.axis_size("blk")
    grads_list = [None] * layers
    for index in reversed(range(layers)):
        params = tuple((member[index] for member in gathered[:6]))
        seq_grad, mem_grad, layer_grads = layer_backward(
            seq_grad, mem_grad, seg_float, params, kept[index]
        )
        grads_list[index] = layer_grads
    stacked = [
        jnp.stack([grads_list[index][member] for index in range(layers)]) for member in range(6)
    ]
    tiny = [stacked[3], stacked[4], stacked[5], mem_grad * share]
    tiny = [
        jnp.moveaxis(part.reshape(part.shape[:-1] + (everyone, -1)), -2, 0).reshape(everyone, -1) for part in tiny
    ]
    tiny = jnp.concatenate(tiny, 1)
    tiny = jnp.pad(tiny, ((0, 0), (0, blocks * rows * width - tiny.shape[1])))
    outgoing = jnp.concatenate(
        [
            stacked[0].reshape(layers * count, width, width),
            stacked[1].reshape(layers, width, per, width).transpose(0, 2, 1, 3).reshape(-1, width, width),
            stacked[2].reshape(layers, everyone, per, rows, width).transpose(0, 2, 1, 3, 4).reshape(-1, width, width),
            tiny.reshape(everyone, blocks, rows, width).transpose(1, 0, 2, 3).reshape(blocks, width, width),
        ]
    ).astype(jnp.bfloat16)
    mine = lax.psum_scatter(outgoing, ("dp", "blk"), scatter_dimension=1, tiled=True).astype(jnp.float32)
    mine_small = mine[three:].reshape(-1)
    back = [mine_small[starts[k] : starts[k + 1]].reshape(small[k].shape) for k in range(4)]
    summed = (
        mine[:one].reshape(layers, count, rows, width),
        mine[one:two].reshape(layers, per, rows, width).transpose(0, 2, 1, 3).reshape(layers, rows, per * width),
        mine[two:three].reshape(layers, per * rows, width),
        back[0],
        back[1],
        back[2],
        back[3],
    )
    return (
        seq_state.astype(jnp.bfloat16)[None],
        mem_state[None],
        seq_grad[None],
        summed[6],
        summed[0],
        summed[1],
        summed[2],
        summed[3],
        summed[4],
        summed[5],
    )


def solution(mesh):
    in_specs = (
        P("dp", "blk", None),
        P("dp", "blk"),
        P(None, ("dp", "blk")),
        P(None, None, ("dp", "blk"), None),
        P(None, ("dp", "blk"), None),
        P(None, ("dp", "blk"), None),
        P(None, ("dp", "blk")),
        P(None, None, ("dp", "blk")),
        P(None, None, ("dp", "blk")),
        P("dp", "blk", None),
        P("dp", None, None),
    )
    out_specs = (
        P("dp", "blk", None),
        P("dp", None, None),
        P("dp", "blk", None),
        P(None, ("dp", "blk")),
        P(None, None, ("dp", "blk"), None),
        P(None, ("dp", "blk"), None),
        P(None, ("dp", "blk"), None),
        P(None, ("dp", "blk")),
        P(None, None, ("dp", "blk")),
        P(None, None, ("dp", "blk")),
    )
    return jax.shard_map(local, mesh=mesh, in_specs=in_specs, out_specs=out_specs, check_vma=False)
```

```python
import functools

import jax
import jax.numpy as jnp
from jax import lax
from jax.experimental import pallas as pl
from jax.experimental.pallas import tpu as pltpu
from jax.sharding import PartitionSpec as P

HEADS = 8
HEAD = 64
MEM = 20
PAD = 32
NEG = -1000000000.0
BIG = 3.0e38
EPS = 1e-05
SCALE = HEAD**-0.5
ALL = ("dp", "blk")
LOW = jnp.bfloat16
F32 = jnp.float32
VMEM_LIMIT = 56 * 1024 * 1024


def dot(a, b):
    return jnp.dot(a, b, preferred_element_type=F32)


def dot_nt(a, b):
    return lax.dot_general(a, b, (((1,), (1,)), ((), ())), preferred_element_type=F32)


def dot_tn(a, b):
    return lax.dot_general(a, b, (((0,), (0,)), ((), ())), preferred_element_type=F32)


def hat(x):
    center = x - jnp.mean(x, -1, keepdims=True)
    spread = jnp.mean(center * center, -1, keepdims=True)
    inv = lax.rsqrt(spread + EPS)
    return center * inv, inv


def norm(x, gain, shift):
    return hat(x)[0] * gain + shift


def norm_back(x, gain, grad):
    unit, inv = hat(x)
    scaled = grad * gain
    mean_one = jnp.mean(scaled, -1, keepdims=True)
    mean_two = jnp.mean(scaled * unit, -1, keepdims=True)
    return inv * (scaled - mean_one - unit * mean_two), grad * unit


def total(x):
    return jnp.sum(x, 0, keepdims=True)


def gelu_parts(u):
    k = 0.7978845608028654
    t = jnp.tanh(k * (u + 0.044715 * u * u * u))
    half = 0.5 * (1.0 + t)
    slope = half + 0.5 * u * (1.0 - t * t) * (k * (1.0 + 0.134145 * u * u))
    return u * half, slope


def head_mask(width):
    lanes = lax.broadcasted_iota(jnp.int32, (HEADS, 1, width), 2) // HEAD
    return lanes == lax.broadcasted_iota(jnp.int32, (HEADS, 1, width), 0)


def spread_heads(x):
    rows, width = x.shape
    full = jnp.where(head_mask(width), x.astype(F32)[None], 0.0)
    return full.reshape(HEADS * rows, width).astype(x.dtype)


def fold_heads(x):
    rows, width = x.shape
    full = x.reshape(HEADS, rows // HEADS, width)
    return jnp.sum(jnp.where(head_mask(width), full, 0.0), 0)


def two_heads(x):
    first = lax.broadcasted_iota(jnp.int32, x.shape, 1) < HEAD
    zero = jnp.zeros_like(x)
    return jnp.concatenate([jnp.where(first, x, zero), jnp.where(first, zero, x)], 0)


def pick_heads(x):
    width, rows = x.shape
    mine = (lax.broadcasted_iota(jnp.int32, x.shape, 0) < HEAD) == (
        lax.broadcasted_iota(jnp.int32, x.shape, 1) < rows // 2
    )
    both = jnp.where(mine, x, 0.0).T
    return both[: rows // 2] + both[rows // 2 :]


def bound_of(seg_keys, seg_queries):
    same = seg_keys == seg_queries
    allowed = (same | (seg_keys == -2.0) | (seg_queries == -1.0)) & (seg_keys != -3.0)
    return jnp.where(allowed, BIG, NEG)


def place_keys(keys_ref, own_ref, core_ref, chip_ref, both_ref):
    rows = core_ref.shape[0]
    me = lax.axis_index("blk")
    pieces = ((me, own_ref), (me ^ 1, core_ref), (me ^ 2, chip_ref), (me ^ 3, both_ref))
    for place, piece in pieces:
        keys_ref[pl.ds(pl.multiple_of(place * rows, rows), rows), :] = piece[0:rows, :]
    keys_ref[4 * rows :, :] = own_ref[rows:, :]


def project(z, weight, q_ref, kv_ref):
    low = z.astype(LOW)
    width = low.shape[1]
    q_ref[...] = dot(low, weight(0)).astype(LOW)
    kv_ref[:, :width] = dot(low, weight(1)).astype(LOW)
    kv_ref[:, width:] = dot(low, weight(2)).astype(LOW)


def first_kernel(weight, tokens_ref, memory_ref, z_ref, q_ref, kv_ref):
    rows = tokens_ref.shape[0]
    z_ref[:rows, :] = tokens_ref[...].astype(F32)
    z_ref[rows:, :] = memory_ref[...]
    project(z_ref[...], weight, q_ref, kv_ref)


def attend_kernel(
    weight, z_ref, q_ref, own_ref, core_ref, chip_ref, both_ref, segk_ref, segq_ref, gain_ref, shift_ref,
    att_ref, pre_ref, one_ref, rq_ref, rkv_ref, wq_ref, part_ref,
    keys_ref, bound_ref,
):
    rows = core_ref.shape[0]
    width = z_ref.shape[1]
    place_keys(keys_ref, own_ref, core_ref, chip_ref, both_ref)
    bound_ref[...] = bound_of(segk_ref[...], segq_ref[...])

    def pair(step, carry):
        lanes = pl.ds(pl.multiple_of(step * 128, 128), 128)
        more = pl.ds(pl.multiple_of(width + step * 128, 128), 128)
        query = two_heads(q_ref[:, lanes]) * jnp.asarray(SCALE, LOW)
        keys = keys_ref[:, lanes]
        values = keys_ref[:, more]
        scores = jnp.minimum(dot_nt(keys, query), bound_ref[...])
        expo = jnp.exp(scores - jnp.max(scores, 0, keepdims=True))
        probs = expo * (1.0 / jnp.sum(expo, 0, keepdims=True))
        att_ref[:, lanes] = pick_heads(dot_tn(values, probs.astype(LOW))).astype(LOW)
        return carry

    lax.fori_loop(0, width // 128, pair, 0)
    pre = z_ref[...] + dot(att_ref[...], weight(3))
    pre_ref[...] = pre
    one = norm(pre, gain_ref[0:1, :], shift_ref[0:1, :])
    one_ref[...] = one
    low = one.astype(LOW)
    seq_low, mem_low = low[:rows], low[rows:]
    wq_ref[...] = dot(seq_low, weight(8)).astype(LOW)
    rq = dot(mem_low, weight(4)).astype(LOW)
    rk = dot(seq_low, weight(5)).astype(LOW)
    rv = dot(seq_low, weight(6)).astype(LOW)
    rq_ref[...] = rq
    rkv_ref[:, :width] = rk
    rkv_ref[:, width:] = rv
    scores = dot_nt(spread_heads(rq * jnp.asarray(SCALE, LOW)), rk)
    top = jnp.max(scores, -1, keepdims=True)
    expo = jnp.exp(scores - top)
    summed = jnp.sum(expo, -1, keepdims=True)
    part_ref[0:PAD, :] = fold_heads(dot(expo.astype(LOW), rv))
    wide = (HEADS * PAD, width)
    part_ref[PAD : 2 * PAD, :] = fold_heads(jnp.broadcast_to(top, wide))
    part_ref[2 * PAD :, :] = fold_heads(jnp.broadcast_to(summed, wide))


def write_probs(wk, wq):
    scores = dot_nt(spread_heads(wk * jnp.asarray(SCALE, LOW)), wq)
    scores = scores.reshape(HEADS, PAD, scores.shape[1])
    real = lax.broadcasted_iota(jnp.int32, scores.shape, 1) < MEM
    scores = jnp.where(real, scores, NEG)
    expo = jnp.exp(scores - jnp.max(scores, 1, keepdims=True))
    return expo * (1.0 / jnp.sum(expo, 1, keepdims=True))


def finish_kernel(
    last, weight, one_ref, parts_ref, wq_ref, bias_ref, gain_ref, shift_ref, *rest
):
    if last:
        (z_ref, rout_ref, rlse_ref, mempre_ref, two_ref, wkv_ref, wlow_ref, seqpre_ref, x_ref, feedpre_ref) = rest
    else:
        (z_ref, q_ref, kv_ref,
         rout_ref, rlse_ref, mempre_ref, two_ref, wkv_ref, wlow_ref, seqpre_ref, x_ref, feedpre_ref) = rest
    rows, width = wq_ref.shape
    count = parts_ref.shape[0]
    top = parts_ref[0, PAD : 2 * PAD, :]
    for source in range(1, count):
        top = jnp.maximum(top, parts_ref[source, PAD : 2 * PAD, :])
    accum = jnp.zeros((PAD, width), F32)
    summed = jnp.zeros((PAD, width), F32)
    for source in range(count):
        fade = jnp.exp(parts_ref[source, PAD : 2 * PAD, :] - top)
        accum = accum + fade * parts_ref[source, 0:PAD, :]
        summed = summed + fade * parts_ref[source, 2 * PAD :, :]
    rout = accum / summed
    rout_ref[...] = rout
    rlse_ref[...] = top + jnp.log(summed)
    mempre = one_ref[rows:, :] + dot(rout.astype(LOW), weight(7))
    mempre_ref[...] = mempre
    memtwo = norm(mempre, gain_ref[1:2, :], shift_ref[1:2, :])
    memlow = memtwo.astype(LOW)
    wk = dot(memlow, weight(9)).astype(LOW)
    wv = dot(memlow, weight(10)).astype(LOW)
    wkv_ref[:, :width] = wk
    wkv_ref[:, width:] = wv
    probs = write_probs(wk, wq_ref[...]).reshape(HEADS * PAD, rows)
    wlow = dot_tn(probs.astype(LOW), spread_heads(wv)).astype(LOW)
    wlow_ref[...] = wlow
    seqpre = one_ref[:rows, :] + dot(wlow, weight(11))
    seqpre_ref[...] = seqpre
    seqtwo = norm(seqpre, gain_ref[2:3, :], shift_ref[2:3, :])
    two_ref[:rows, :] = seqtwo
    two_ref[rows:, :] = memtwo
    two = two_ref[...]
    x = two.astype(LOW)
    x_ref[...] = x
    feed = two + shift_ref[4:5, :]
    for part in range(bias_ref.shape[0]):
        u = dot(x, weight(("up", part))) + bias_ref[part : part + 1, :]
        feed = feed + dot(gelu_parts(u)[0].astype(LOW), weight(("down", part)))
    feedpre_ref[...] = feed
    z_ref[...] = norm(feed, gain_ref[3:4, :], shift_ref[3:4, :])
    if not last:
        project(z_ref[...], weight, q_ref, kv_ref)


def feed_back_kernel(
    share, weight, grad_ref, feedpre_ref, x_ref, seqpre_ref, wlow_ref, wq_ref, wkv_ref, one_ref,
    bias_ref, gain_ref,
    gup_ref, gdown_ref, g11_ref, g8_ref, gbias_ref, gsmall_ref, mem_ref, seq_ref, part_ref,
):
    rows, width = wq_ref.shape
    full = grad_ref.shape[0]
    balance = jnp.where(lax.broadcasted_iota(jnp.int32, (full, 1), 0) < rows, 1.0, share)
    grad = grad_ref[...]
    feed, by_unit = norm_back(feedpre_ref[...], gain_ref[3:4, :], grad)
    gsmall_ref[0:1, :] = total(by_unit * balance)
    gsmall_ref[1:2, :] = total(grad * balance)
    low = feed.astype(LOW)
    low_share = (low.astype(F32) * balance).astype(LOW)
    gsmall_ref[2:3, :] = total(low_share.astype(F32))
    x = x_ref[...]
    two = feed
    for part in range(bias_ref.shape[0]):
        u = dot(x, weight(("up", part))) + bias_ref[part : part + 1, :]
        value, slope = gelu_parts(u)
        gdown_ref[part] = dot_tn(value.astype(LOW), low_share).astype(LOW)
        pre = (dot_nt(low, weight(("down", part))) * slope).astype(LOW)
        pre_share = (pre.astype(F32) * balance).astype(LOW)
        gbias_ref[part : part + 1, :] = total(pre_share.astype(F32))
        gup_ref[part] = dot_tn(x, pre_share).astype(LOW)
        two = two + dot_nt(pre, weight(("up", part)))
    mem_ref[...] = two[rows:]
    grad = two[:rows]
    seq, by_unit = norm_back(seqpre_ref[...], gain_ref[2:3, :], grad)
    gsmall_ref[3:4, :] = total(by_unit)
    gsmall_ref[4:5, :] = total(grad)
    low = seq.astype(LOW)
    g11_ref[...] = dot_tn(wlow_ref[...], low).astype(LOW)
    out_low = dot_nt(low, weight(11)).astype(LOW)
    wk, wv = wkv_ref[:, :width], wkv_ref[:, width:]
    wq = wq_ref[...]
    probs = write_probs(wk, wq)
    prob_grad = dot_nt(spread_heads(wv), out_low).reshape(probs.shape)
    delta = jnp.sum(probs * prob_grad, 1, keepdims=True)
    score_grad = (probs * (prob_grad - delta)).reshape(HEADS * PAD, rows).astype(LOW)
    wq_low = (dot_tn(score_grad, spread_heads(wk)) * SCALE).astype(LOW)
    part_ref[:PAD, :] = fold_heads(dot(score_grad, wq)) * SCALE
    part_ref[PAD:, :] = fold_heads(dot(probs.reshape(HEADS * PAD, rows).astype(LOW), out_low))
    g8_ref[...] = dot_tn(one_ref[:rows, :].astype(LOW), wq_low).astype(LOW)
    seq_ref[...] = seq + dot_nt(wq_low, weight(8))


def read_back_kernel(
    share, weight, parts_ref, mem_ref, seq_ref, two_ref, mempre_ref, rout_ref, rlse_ref, rq_ref, rkv_ref, one_ref,
    pre_ref, gain_ref,
    g5_ref, g6_ref, g7_ref, g9_ref, g10_ref, gsmall_ref, memgrad_ref, seqjoint_ref, part_ref,
):
    rows, width = seq_ref.shape
    both = parts_ref[0]
    for source in range(1, parts_ref.shape[0]):
        both = both + parts_ref[source]
    k_low = both[:PAD].astype(LOW)
    v_low = both[PAD:].astype(LOW)
    mem_low = two_ref[rows:, :].astype(LOW)
    g9_ref[...] = (dot_tn(mem_low, k_low) * share).astype(LOW)
    g10_ref[...] = (dot_tn(mem_low, v_low) * share).astype(LOW)
    grad = mem_ref[...] + dot_nt(k_low, weight(9)) + dot_nt(v_low, weight(10))
    mem, by_unit = norm_back(mempre_ref[...], gain_ref[1:2, :], grad)
    gsmall_ref[0:1, :] = total(by_unit) * share
    gsmall_ref[1:2, :] = total(grad) * share
    low = mem.astype(LOW)
    rout = rout_ref[...]
    g7_ref[...] = (dot_tn(rout.astype(LOW), low) * share).astype(LOW)
    out_low = dot_nt(low, weight(7)).astype(LOW)
    memgrad_ref[...] = mem
    rk, rv = rkv_ref[:, :width], rkv_ref[:, width:]
    rq = spread_heads(rq_ref[...] * jnp.asarray(SCALE, LOW))
    out_wide = spread_heads(out_low)
    delta = jnp.sum(spread_heads(out_low.astype(F32) * rout), -1, keepdims=True)
    mask = head_mask(width)
    lse = jnp.max(jnp.where(mask, rlse_ref[...][None], -BIG).reshape(HEADS * PAD, width), -1, keepdims=True)
    probs = jnp.exp(dot_nt(rq, rk) - lse)
    score_grad = (probs * (dot_nt(out_wide, rv) - delta)).astype(LOW)
    part_ref[...] = fold_heads(dot(score_grad, rk)) * SCALE
    key_low = dot_tn(score_grad, rq).astype(LOW)
    value_low = dot_tn(probs.astype(LOW), out_wide).astype(LOW)
    seq_low = one_ref[:rows, :].astype(LOW)
    g5_ref[...] = dot_tn(seq_low, key_low).astype(LOW)
    g6_ref[...] = dot_tn(seq_low, value_low).astype(LOW)
    grad = seq_ref[...] + dot_nt(key_low, weight(5)) + dot_nt(value_low, weight(6))
    joint, by_unit = norm_back(pre_ref[:rows, :], gain_ref[0:1, :], grad)
    gsmall_ref[2:3, :] = total(by_unit)
    gsmall_ref[3:4, :] = total(grad)
    seqjoint_ref[...] = joint


def attend_back_kernel(
    share, weight, parts_ref, memgrad_ref, seqjoint_ref, one_ref, pre_ref, att_ref,
    q_ref, own_ref, core_ref, chip_ref, both_ref, segk_ref, segq_ref, gain_ref,
    g3_ref, g4_ref, gsmall_ref, joint_ref, qgrad_ref, kvgrad_ref,
    keys_ref, bound_ref, out_ref,
):
    rows, width = seqjoint_ref.shape
    full = att_ref.shape[0]
    place_keys(keys_ref, own_ref, core_ref, chip_ref, both_ref)
    bound_ref[...] = bound_of(segk_ref[...], segq_ref[...])
    part = parts_ref[0]
    for source in range(1, parts_ref.shape[0]):
        part = part + parts_ref[source]
    q_low = part.astype(LOW)
    g4_ref[...] = (dot_tn(one_ref[rows:, :].astype(LOW), q_low) * share).astype(LOW)
    grad = memgrad_ref[...] + dot_nt(q_low, weight(4))
    mem, by_unit = norm_back(pre_ref[rows:, :], gain_ref[0:1, :], grad)
    gsmall_ref[0:1, :] = total(by_unit) * share
    gsmall_ref[1:2, :] = total(grad) * share
    joint_ref[:rows, :] = seqjoint_ref[...]
    joint_ref[rows:, :] = mem
    low = joint_ref[...].astype(LOW)
    balance = jnp.where(lax.broadcasted_iota(jnp.int32, (full, 1), 0) < rows, 1.0, share)
    g3_ref[...] = dot_tn(att_ref[...], (low.astype(F32) * balance).astype(LOW)).astype(LOW)
    out_ref[...] = dot_nt(low, weight(3)).astype(LOW)

    def pair(step, carry):
        lanes = pl.ds(pl.multiple_of(step * 128, 128), 128)
        more = pl.ds(pl.multiple_of(width + step * 128, 128), 128)
        query = q_ref[:, lanes] * jnp.asarray(SCALE, LOW)
        out = out_ref[:, lanes]
        low_balance = jnp.concatenate([balance, balance], 0)
        query = two_heads(query)
        out = two_heads(out)
        keys = keys_ref[:, lanes]
        values = keys_ref[:, more]
        scores = jnp.minimum(dot_nt(keys, query), bound_ref[...])
        expo = jnp.exp(scores - jnp.max(scores, 0, keepdims=True))
        probs = expo * (1.0 / jnp.sum(expo, 0, keepdims=True))
        prob_grad = dot_nt(values, out)
        delta = jnp.sum(probs * prob_grad, 0, keepdims=True)
        score_grad = (probs * (prob_grad - delta)).astype(LOW)
        qgrad_ref[:, lanes] = (pick_heads(dot_tn(keys, score_grad)) * SCALE).astype(LOW)
        query_share = (query.astype(F32) * low_balance).astype(LOW)
        out_share = (out.astype(F32) * low_balance).astype(LOW)
        kvgrad_ref[:, lanes] = dot(score_grad, query_share).astype(LOW)
        kvgrad_ref[:, more] = dot(probs.astype(LOW), out_share).astype(LOW)
        return carry

    lax.fori_loop(0, width // 128, pair, 0)


def input_back_kernel(share, weight, z_ref, joint_ref, qgrad_ref, kvgrad_ref, g0_ref, g1_ref, g2_ref, zgrad_ref):
    full, width = z_ref.shape
    rows = full - PAD
    balance = jnp.where(lax.broadcasted_iota(jnp.int32, (full, 1), 0) < rows, 1.0, share)
    low = z_ref[...].astype(LOW)
    grads = (qgrad_ref[...], kvgrad_ref[:, :width], kvgrad_ref[:, width:])
    grad = joint_ref[...]
    for part, (value, out_ref) in enumerate(zip(grads, (g0_ref, g1_ref, g2_ref))):
        out_ref[...] = dot_tn(low, (value.astype(F32) * balance).astype(LOW)).astype(LOW)
        grad = grad + dot_nt(value, weight(part))
    zgrad_ref[...] = grad


def call(kernel, name, ins, outs, weights, scratch=()):
    sources = []
    for array, _ in weights.values():
        if not any(array is source for source in sources):
            sources.append(array)
    places = {
        key: ([array is source for source in sources].index(True), index) for key, (array, index) in weights.items()
    }
    shape = sources[0].shape[1:]

    def body(*refs):
        in_refs, refs = refs[: len(ins)], refs[len(ins) :]
        source_refs, refs = refs[: len(sources)], refs[len(sources) :]
        *refs, buffer, sems = refs
        copies = {}
        for slot, (key, (source, index)) in enumerate(places.items()):
            copies[key] = pltpu.make_async_copy(source_refs[source].at[index], buffer.at[slot], sems.at[slot])
            copies[key].start()
        slots = {key: slot for slot, key in enumerate(places)}
        arrived = set()

        def weight(key):
            if key not in arrived:
                copies[key].wait()
                arrived.add(key)
            return buffer[slots[key]]

        kernel(weight, *in_refs, *refs)

    inside = pl.BlockSpec(memory_space=pltpu.VMEM)
    return pl.pallas_call(
        body,
        out_shape=[jax.ShapeDtypeStruct(shape, kind) for shape, kind in outs],
        in_specs=[inside] * len(ins) + [pl.BlockSpec(memory_space=pl.ANY)] * len(sources),
        out_specs=[inside] * len(outs),
        scratch_shapes=list(scratch)
        + [pltpu.VMEM((len(weights),) + shape, LOW), pltpu.SemaphoreType.DMA((len(weights),))],
        compiler_params=pltpu.CompilerParams(vmem_limit_bytes=VMEM_LIMIT),
        name=name,
    )(*ins, *sources)


def flipped(value, bit):
    size = lax.axis_size("blk")
    return lax.ppermute(value, "blk", [(source, source ^ bit) for source in range(size)])


def everyone_of(value):
    return lax.all_gather(value, "blk")


def local(
    tokens, segments, memory_init, attn_weights, ffn_in, ffn_out, ffn_bias, norm_gain, norm_shift, out_grad, memory_cot
):
    layers, count, rows, width = attn_weights.shape
    hidden = ffn_in.shape[2]
    per = hidden // width
    small = [ffn_bias, norm_gain, norm_shift, memory_init]
    sizes = [part.size for part in small]
    starts = [sum(sizes[:k]) for k in range(5)]
    flat = jnp.concatenate([part.astype(LOW).reshape(-1) for part in small])
    blocks = -(-flat.size // (rows * width))
    flat = jnp.pad(flat, (0, blocks * rows * width - flat.size))
    packed = jnp.concatenate(
        [
            attn_weights.astype(LOW).reshape(layers * count, rows, width),
            ffn_in.astype(LOW).reshape(layers, rows, per, width).transpose(0, 2, 1, 3).reshape(-1, rows, width),
            ffn_out.astype(LOW).reshape(-1, rows, width),
            flat.reshape(blocks, rows, width),
        ]
    )
    everyone = lax.axis_size("dp") * lax.axis_size("blk")
    whole = lax.all_gather(packed, ALL, axis=1, tiled=True)
    one, two, three = (layers * count, layers * (count + per), layers * (count + 2 * per))
    full_small = whole[three:].reshape(blocks, everyone, rows * width).transpose(1, 0, 2).reshape(everyone, -1)
    pieces = [full_small[:, starts[k] : starts[k + 1]].reshape((everyone,) + small[k].shape) for k in range(4)]
    bias, gains, shifts, memory = [
        jnp.moveaxis(piece, 0, -2).reshape(piece.shape[1:-1] + (-1,)).astype(F32) for piece in pieces
    ]
    down_all = (
        whole[two:three].reshape(layers, per, everyone, rows, width).transpose(0, 2, 1, 3, 4)
    ).reshape(layers * per, width, width)
    bias = bias.reshape(layers, per, width)

    def attn(index, *keys):
        return {key: (whole, index * count + key) for key in keys}

    def feed(index):
        pairs = {}
        for part in range(per):
            pairs["up", part] = (whole, one + index * per + part)
            pairs["down", part] = (down_all, index * per + part)
        return pairs

    length = tokens.shape[1]
    full = length + PAD
    size = lax.axis_size("blk")
    share = 1.0 / size
    seg = segments[0].astype(F32)
    seg_all = lax.all_gather(segments[0], "blk", tiled=True).astype(F32)
    seg_keys = jnp.concatenate(
        [seg_all, jnp.full((MEM,), -2.0, F32), jnp.full((PAD - MEM,), -3.0, F32)]
    ).reshape(-1, 1)
    seg_row = jnp.concatenate([seg, jnp.full((PAD,), -1.0, F32)])
    seg_queries = jnp.concatenate([seg_row, seg_row]).reshape(1, -1)
    every = size * length + PAD
    memory = jnp.pad(memory, ((0, PAD - MEM), (0, 0)))
    keys_scratch = pltpu.VMEM((every, 2 * width), LOW)
    bound_scratch = pltpu.VMEM((every, 2 * full), F32)

    z, q, kv = call(
        first_kernel,
        "first",
        [tokens[0], memory],
        [((full, width), F32), ((full, width), LOW), ((full, 2 * width), LOW)],
        attn(0, 0, 1, 2),
    )
    kept = []
    for index in range(layers):
        own = kv[:length]
        core = flipped(own, 1)
        chip = flipped(own, 2)
        both = flipped(chip, 1)
        att, pre, first, rq, rkv, wq, part = call(
            attend_kernel,
            f"attend_{index}",
            [z, q, kv, core, chip, both, seg_keys, seg_queries, gains[index], shifts[index]],
            [
                ((full, width), LOW), ((full, width), F32), ((full, width), F32), ((PAD, width), LOW),
                ((length, 2 * width), LOW), ((length, width), LOW), ((3 * PAD, width), F32),
            ],
            attn(index, 3, 8, 4, 5, 6),
            [keys_scratch, bound_scratch],
        )
        parts = everyone_of(part)
        last = index + 1 == layers
        results = call(
            functools.partial(finish_kernel, last),
            f"finish_{index}",
            [first, parts, wq, bias[index], gains[index], shifts[index]],
            [((full, width), F32)]
            + ([] if last else [((full, width), LOW), ((full, 2 * width), LOW)])
            + [
                ((PAD, width), F32), ((PAD, width), F32), ((PAD, width), F32), ((full, width), F32),
                ((PAD, 2 * width), LOW), ((length, width), LOW), ((length, width), F32), ((full, width), LOW),
                ((full, width), F32),
            ],
            attn(index, 7, 9, 10, 11) | feed(index) | ({} if last else attn(index + 1, 0, 1, 2)),
        )
        rout, rlse, mempre, second, wkv, wlow, seqpre, x, feedpre = results[-9:]
        kept.append(
            dict(
                z=z, q=q, kv=kv, core=core, chip=chip, both=both, att=att, pre=pre, first=first, rq=rq, rkv=rkv,
                wq=wq, rout=rout, rlse=rlse, mempre=mempre, second=second, wkv=wkv, wlow=wlow, seqpre=seqpre, x=x,
                feedpre=feedpre,
            )
        )
        z = results[0]
        if not last:
            q, kv = results[1:3]
    final = z
    grad = jnp.concatenate(
        [out_grad[0].astype(F32), jnp.pad(memory_cot[0].astype(F32), ((0, PAD - MEM), (0, 0)))]
    )
    square = ((width, width), LOW)
    square_f32 = [((full, width), F32)]
    made = [None] * layers
    for index in reversed(range(layers)):
        k = kept[index]
        gup, gdown, g11, g8, gbias, small_one, mem, seq, part = call(
            functools.partial(feed_back_kernel, share),
            f"feed_back_{index}",
            [grad, k["feedpre"], k["x"], k["seqpre"], k["wlow"], k["wq"], k["wkv"], k["first"], bias[index],
             gains[index]],
            [
                ((per, width, width), LOW), ((per, width, width), LOW), square, square, ((per, width), F32),
                ((5, width), F32), ((PAD, width), F32), ((length, width), F32), ((2 * PAD, width), F32),
            ],
            feed(index) | attn(index, 11, 8),
        )
        parts = everyone_of(part)
        g5, g6, g7, g9, g10, small_two, mem, seq, part = call(
            functools.partial(read_back_kernel, share),
            f"read_back_{index}",
            [parts, mem, seq, k["second"], k["mempre"], k["rout"], k["rlse"], k["rq"], k["rkv"], k["first"],
             k["pre"], gains[index]],
            [square] * 5
            + [((4, width), F32), ((PAD, width), F32), ((length, width), F32), ((PAD, width), F32)],
            attn(index, 9, 10, 7, 5, 6),
        )
        parts = everyone_of(part)
        g3, g4, small_three, joint, qgrad, kvgrad = call(
            functools.partial(attend_back_kernel, share),
            f"attend_back_{index}",
            [parts, mem, seq, k["first"], k["pre"], k["att"], k["q"], k["kv"], k["core"], k["chip"], k["both"],
             seg_keys, seg_queries, gains[index]],
            [square, square, ((2, width), F32), ((full, width), F32), ((full, width), LOW),
             ((every, 2 * width), LOW)],
            attn(index, 4, 3),
            [keys_scratch, bound_scratch, pltpu.VMEM((full, width), LOW)],
        )
        me = lax.axis_index("blk")
        chunks = kvgrad[: size * length].reshape(size // 2, 2, length, 2 * width)
        memory_part = kvgrad[size * length :]
        here = jnp.take(chunks, me % 2, axis=1)
        there = jnp.take(chunks, 1 - me % 2, axis=1)
        got, got_memory = flipped(there, 1), flipped(memory_part, 1)
        here = here.astype(F32) + got.astype(F32)
        memory_part = (memory_part.astype(F32) + got_memory.astype(F32)).astype(LOW)
        mine = jnp.take(here, me // 2, axis=0)
        theirs = jnp.take(here, 1 - me // 2, axis=0).astype(LOW)
        got, got_memory = flipped(theirs, 2), flipped(memory_part, 2)
        mine = (mine + got.astype(F32)).astype(LOW)
        memory_part = (memory_part.astype(F32) + got_memory.astype(F32)).astype(LOW)
        kvgrad = jnp.concatenate([mine, memory_part])
        g0, g1, g2, grad = call(
            functools.partial(input_back_kernel, share),
            f"input_back_{index}",
            [k["z"], joint, qgrad, kvgrad],
            [square, square, square] + square_f32,
            attn(index, 0, 1, 2),
        )
        made[index] = dict(
            attn=jnp.stack([g0, g1, g2, g3, g4, g5, g6, g7, g8, g9, g10, g11]),
            up=gup,
            down=gdown,
            bias=gbias.reshape(-1),
            gain=jnp.stack([small_two[2] + small_three[0], small_two[0], small_one[3], small_one[0]]),
            shift=jnp.stack([small_two[3] + small_three[1], small_two[1], small_one[4], small_one[1], small_one[2]]),
        )
    tiny = [jnp.stack([m[name] for m in made]) for name in ("bias", "gain", "shift")] + [grad[length : length + MEM] * share]
    tiny = [jnp.moveaxis(part.reshape(part.shape[:-1] + (everyone, -1)), -2, 0).reshape(everyone, -1) for part in tiny]
    tiny = jnp.concatenate(tiny, 1)
    tiny = jnp.pad(tiny, ((0, 0), (0, blocks * rows * width - tiny.shape[1]))).astype(LOW)
    outgoing = jnp.concatenate(
        [m["attn"] for m in made]
        + [m["up"] for m in made]
        + [
            m["down"].reshape(everyone, per, rows, width).transpose(1, 0, 2, 3).reshape(per, width, width)
            for m in made
        ]
        + [tiny.reshape(everyone, blocks, rows, width).transpose(1, 0, 2, 3).reshape(blocks, width, width)]
    )
    mine = lax.psum_scatter(outgoing, ALL, scatter_dimension=1, tiled=True).astype(F32)
    mine_small = mine[three:].reshape(-1)
    back = [mine_small[starts[k] : starts[k + 1]].reshape(small[k].shape) for k in range(4)]
    return (
        final[:length].astype(LOW)[None],
        final[length : length + MEM][None],
        grad[:length][None],
        back[3],
        mine[:one].reshape(layers, count, rows, width),
        mine[one:two].reshape(layers, per, rows, width).transpose(0, 2, 1, 3).reshape(layers, rows, hidden),
        mine[two:three].reshape(layers, per * rows, width),
        back[0],
        back[1],
        back[2],
    )


def solution(mesh):
    in_specs = (
        P("dp", "blk", None),
        P("dp", "blk"),
        P(None, ALL),
        P(None, None, ALL, None),
        P(None, ALL, None),
        P(None, ALL, None),
        P(None, ALL),
        P(None, None, ALL),
        P(None, None, ALL),
        P("dp", "blk", None),
        P("dp", None, None),
    )
    out_specs = (
        P("dp", "blk", None),
        P("dp", None, None),
        P("dp", "blk", None),
        P(None, ALL),
        P(None, None, ALL, None),
        P(None, ALL, None),
        P(None, ALL, None),
        P(None, ALL),
        P(None, None, ALL),
        P(None, None, ALL),
    )
    return jax.shard_map(local, mesh=mesh, in_specs=in_specs, out_specs=out_specs, check_vma=False)
```

```python
import functools

import jax
import jax.numpy as jnp
from jax import lax
from jax.experimental import pallas as pl
from jax.experimental.pallas import tpu as pltpu
from jax.sharding import PartitionSpec as P

HEADS = 8
HEAD = 64
MEM = 20
PAD = 32
NEG = -1000000000.0
BIG = 3.0e38
EPS = 1e-05
SCALE = HEAD**-0.5
ALL = ("dp", "blk")
LOW = jnp.bfloat16
F32 = jnp.float32
VMEM_LIMIT = 56 * 1024 * 1024
GATHER_AT = 4
PLAN = {
    1: [("early_1",), ("early_1",), ("early_1",), ("early_1",)],
    0: [
        ("early_1", "middle_1", "early_0"),
        ("middle_1", "early_0", "middle_0"),
        ("middle_1", "early_0", "attend_0"),
        ("middle_1", "early_0", "middle_0", "attend_0"),
        ("last", "middle_1", "middle_0", "attend_0"),
        ("last", "early_0", "middle_0", "attend_0"),
        ("last", "middle_0", "attend_0"),
        ("last",),
        ("last",),
    ],
}


def dot(a, b):
    return jnp.dot(a, b, preferred_element_type=F32)


def dot_nt(a, b):
    return lax.dot_general(a, b, (((1,), (1,)), ((), ())), preferred_element_type=F32)


def dot_tn(a, b):
    return lax.dot_general(a, b, (((0,), (0,)), ((), ())), preferred_element_type=F32)


def hat(x):
    center = x - jnp.mean(x, -1, keepdims=True)
    spread = jnp.mean(center * center, -1, keepdims=True)
    inv = lax.rsqrt(spread + EPS)
    return center * inv, inv


def norm(x, gain, shift):
    return hat(x)[0] * gain + shift


def norm_back(x, gain, grad):
    unit, inv = hat(x)
    scaled = grad * gain
    mean_one = jnp.mean(scaled, -1, keepdims=True)
    mean_two = jnp.mean(scaled * unit, -1, keepdims=True)
    return inv * (scaled - mean_one - unit * mean_two), grad * unit


def row(small_ref, rows_of, name, which):
    place = rows_of[name] + which
    return small_ref[place : place + 1, :]


def total(x):
    return jnp.sum(x, 0, keepdims=True)


def gelu_parts(u):
    k = 0.7978845608028654
    t = jnp.tanh(k * (u + 0.044715 * u * u * u))
    half = 0.5 * (1.0 + t)
    slope = half + 0.5 * u * (1.0 - t * t) * (k * (1.0 + 0.134145 * u * u))
    return u * half, slope


def head_mask(width):
    lanes = lax.broadcasted_iota(jnp.int32, (HEADS, 1, width), 2) // HEAD
    return lanes == lax.broadcasted_iota(jnp.int32, (HEADS, 1, width), 0)


def spread_heads(x):
    rows, width = x.shape
    full = jnp.where(head_mask(width), x.astype(F32)[None], 0.0)
    return full.reshape(HEADS * rows, width).astype(x.dtype)


def fold_heads(x):
    rows, width = x.shape
    full = x.reshape(HEADS, rows // HEADS, width)
    return jnp.sum(jnp.where(head_mask(width), full, 0.0), 0)


def two_heads(x):
    first = lax.broadcasted_iota(jnp.int32, x.shape, 1) < HEAD
    zero = jnp.zeros_like(x)
    return jnp.concatenate([jnp.where(first, x, zero), jnp.where(first, zero, x)], 0)


def pick_heads(x):
    width, rows = x.shape
    mine = (lax.broadcasted_iota(jnp.int32, x.shape, 0) < HEAD) == (
        lax.broadcasted_iota(jnp.int32, x.shape, 1) < rows // 2
    )
    both = jnp.where(mine, x, 0.0).T
    return both[: rows // 2] + both[rows // 2 :]


def bound_of(seg_keys, seg_queries):
    same = seg_keys == seg_queries
    allowed = (same | (seg_keys == -2.0) | (seg_queries == -1.0)) & (seg_keys != -3.0)
    return jnp.where(allowed, BIG, NEG)


def place_keys(keys_ref, own_ref, core_ref, chip_ref, both_ref, memory_ref):
    rows = core_ref.shape[0]
    me = lax.axis_index("blk")
    pieces = ((me, own_ref), (me ^ 1, core_ref), (me ^ 2, chip_ref), (me ^ 3, both_ref))
    for place, piece in pieces:
        keys_ref[pl.ds(pl.multiple_of(place * rows, rows), rows), :] = piece[0:rows, :]
    keys_ref[4 * rows :, :] = memory_ref[...]


def project(z, weight, q_ref, kv_ref, kvmem_ref):
    low = z.astype(LOW)
    rows, width = kv_ref.shape[0], low.shape[1]
    for part in (1, 2):
        lanes = pl.ds((part - 1) * width, width)
        value = dot(low, weight(part)).astype(LOW)
        kv_ref[:, lanes] = value[:rows]
        kvmem_ref[:, lanes] = value[rows:]
    q_ref[...] = dot(low, weight(0)).astype(LOW)


def first_kernel(weight, put, rows_of, tokens_ref, small_ref, z_ref, q_ref, kv_ref, kvmem_ref):
    rows = tokens_ref.shape[0]
    small = weight("small")[:, :128].astype(F32).T
    small_ref[...] = small
    z_ref[:rows, :] = tokens_ref[...].astype(F32)
    start = rows_of["memory"]
    z_ref[rows : rows + MEM, :] = small[start : start + MEM]
    z_ref[rows + MEM :, :] = jnp.zeros((PAD - MEM, small.shape[1]), F32)
    project(z_ref[...], weight, q_ref, kv_ref, kvmem_ref)


def attend_kernel(
    weight, put, rows_of, z_ref, q_ref, own_ref, core_ref, chip_ref, both_ref, kvmem_ref, segk_ref, segq_ref, small_ref,
    att_ref, pre_ref, one_ref, rq_ref, rkv_ref, wq_ref, part_ref,
    keys_ref, bound_ref,
):
    rows = core_ref.shape[0]
    width = z_ref.shape[1]
    place_keys(keys_ref, own_ref, core_ref, chip_ref, both_ref, kvmem_ref)
    bound_ref[...] = bound_of(segk_ref[...], segq_ref[...])

    def pair(step, carry):
        lanes = pl.ds(pl.multiple_of(step * 128, 128), 128)
        more = pl.ds(pl.multiple_of(width + step * 128, 128), 128)
        query = two_heads(q_ref[:, lanes]) * jnp.asarray(SCALE, LOW)
        keys = keys_ref[:, lanes]
        values = keys_ref[:, more]
        scores = jnp.minimum(dot_nt(keys, query), bound_ref[...])
        expo = jnp.exp(scores - jnp.max(scores, 0, keepdims=True))
        probs = expo * (1.0 / jnp.sum(expo, 0, keepdims=True))
        att_ref[:, lanes] = pick_heads(dot_tn(values, probs.astype(LOW))).astype(LOW)
        return carry

    lax.fori_loop(0, width // 128, pair, 0)
    pre = z_ref[...] + dot(att_ref[...], weight(3))
    pre_ref[...] = pre
    one = norm(pre, row(small_ref, rows_of, "gain", 0), row(small_ref, rows_of, "shift", 0))
    one_ref[...] = one
    low = one.astype(LOW)
    seq_low, mem_low = low[:rows], low[rows:]
    wq_ref[...] = dot(seq_low, weight(8)).astype(LOW)
    rq = dot(mem_low, weight(4)).astype(LOW)
    rk = dot(seq_low, weight(5)).astype(LOW)
    rv = dot(seq_low, weight(6)).astype(LOW)
    rq_ref[...] = rq
    rkv_ref[:, :width] = rk
    rkv_ref[:, width:] = rv
    scores = dot_nt(spread_heads(rq * jnp.asarray(SCALE, LOW)), rk)
    top = jnp.max(scores, -1, keepdims=True)
    expo = jnp.exp(scores - top)
    summed = jnp.sum(expo, -1, keepdims=True)
    part_ref[:, :width] = fold_heads(dot(expo.astype(LOW), rv))
    lanes = lax.broadcasted_iota(jnp.int32, (HEADS, PAD, 128), 2)
    heads = lax.broadcasted_iota(jnp.int32, (HEADS, PAD, 128), 0)
    top = jnp.where(lanes == heads, top.reshape(HEADS, PAD, 1), 0.0)
    summed = jnp.where(lanes == heads + HEADS, summed.reshape(HEADS, PAD, 1), 0.0)
    part_ref[:, width:] = jnp.sum(top + summed, 0)


def in_pairs(values):
    own, core, chip, both = values
    return (own + core) + (chip + both)


def widened(stats, start, width):
    lanes = lax.broadcasted_iota(jnp.int32, (128, width), 0)
    heads = lax.broadcasted_iota(jnp.int32, (128, width), 1) // HEAD + start
    return jnp.dot(
        stats, (lanes == heads).astype(F32), precision=lax.Precision.HIGHEST, preferred_element_type=F32
    )


def write_probs(wk, wq):
    scores = dot_nt(spread_heads(wk * jnp.asarray(SCALE, LOW)), wq)
    scores = scores.reshape(HEADS, PAD, scores.shape[1])
    real = lax.broadcasted_iota(jnp.int32, scores.shape, 1) < MEM
    scores = jnp.where(real, scores, NEG)
    expo = jnp.exp(scores - jnp.max(scores, 1, keepdims=True))
    return expo * (1.0 / jnp.sum(expo, 1, keepdims=True))


def finish_kernel(
    last, weight, put, rows_of, one_ref, own_ref, core_ref, chip_ref, both_ref, wq_ref, bias_ref, small_ref, *rest
):
    if last:
        (z_ref, rout_ref, rlse_ref, mempre_ref, two_ref, wkv_ref, wlow_ref, seqpre_ref, x_ref, feedpre_ref) = rest
    else:
        (z_ref, q_ref, kv_ref, kvmem_ref,
         rout_ref, rlse_ref, mempre_ref, two_ref, wkv_ref, wlow_ref, seqpre_ref, x_ref, feedpre_ref) = rest
    rows, width = wq_ref.shape
    parts = (own_ref, core_ref, chip_ref, both_ref)
    tops = [widened(part[:, width:], 0, width) for part in parts]
    sums = [widened(part[:, width:], HEADS, width) for part in parts]
    top = jnp.maximum(jnp.maximum(tops[0], tops[1]), jnp.maximum(tops[2], tops[3]))
    fades = [jnp.exp(value - top) for value in tops]
    accum = in_pairs([fade * part[:, :width] for fade, part in zip(fades, parts)])
    summed = in_pairs([fade * value for fade, value in zip(fades, sums)])
    rout = accum / summed
    rout_ref[...] = rout
    rlse_ref[...] = top + jnp.log(summed)
    mempre = one_ref[rows:, :] + dot(rout.astype(LOW), weight(7))
    mempre_ref[...] = mempre
    memtwo = norm(mempre, row(small_ref, rows_of, "gain", 1), row(small_ref, rows_of, "shift", 1))
    memlow = memtwo.astype(LOW)
    wk = dot(memlow, weight(9)).astype(LOW)
    wv = dot(memlow, weight(10)).astype(LOW)
    wkv_ref[:, :width] = wk
    wkv_ref[:, width:] = wv
    probs = write_probs(wk, wq_ref[...]).reshape(HEADS * PAD, rows)
    wlow = dot_tn(probs.astype(LOW), spread_heads(wv)).astype(LOW)
    wlow_ref[...] = wlow
    seqpre = one_ref[:rows, :] + dot(wlow, weight(11))
    seqpre_ref[...] = seqpre
    seqtwo = norm(seqpre, row(small_ref, rows_of, "gain", 2), row(small_ref, rows_of, "shift", 2))
    two_ref[:rows, :] = seqtwo
    two_ref[rows:, :] = memtwo
    two = two_ref[...]
    x = two.astype(LOW)
    x_ref[...] = x
    feed = two + row(small_ref, rows_of, "shift", 4)
    for part in range(bias_ref.shape[0]):
        u = dot(x, weight(("up", part))) + bias_ref[part : part + 1, :]
        feed = feed + dot(gelu_parts(u)[0].astype(LOW), weight("down", part))
    feedpre_ref[...] = feed
    z_ref[...] = norm(feed, row(small_ref, rows_of, "gain", 3), row(small_ref, rows_of, "shift", 3))
    if not last:
        project(z_ref[...], weight, q_ref, kv_ref, kvmem_ref)


def feed_back_kernel(
    share, weight, put, rows_of, grad_ref, feedpre_ref, x_ref, seqpre_ref, wlow_ref, wq_ref, wkv_ref, one_ref,
    bias_ref, small_ref,
    gbias_ref, gsmall_ref, mem_ref, seq_ref, part_ref,
):
    rows, width = wq_ref.shape
    full = grad_ref.shape[0]
    balance = jnp.where(lax.broadcasted_iota(jnp.int32, (full, 1), 0) < rows, 1.0, share)
    grad = grad_ref[...]
    feed, by_unit = norm_back(feedpre_ref[...], row(small_ref, rows_of, "gain", 3), grad)
    gsmall_ref[0:1, :] = total(by_unit * balance)
    gsmall_ref[1:2, :] = total(grad * balance)
    low = feed.astype(LOW)
    low_share = (low.astype(F32) * balance).astype(LOW)
    gsmall_ref[2:3, :] = total(low_share.astype(F32))
    x = x_ref[...]
    two = feed
    parts = bias_ref.shape[0]
    for part in range(parts):
        u = dot(x, weight(("up", part))) + bias_ref[part : part + 1, :]
        value, slope = gelu_parts(u)
        put(("down", part), dot_tn(value.astype(LOW), low_share))
        pre = (dot_nt(low, weight("down", part)) * slope).astype(LOW)
        pre_share = (pre.astype(F32) * balance).astype(LOW)
        gbias_ref[part : part + 1, :] = total(pre_share.astype(F32))
        put(("up", part), dot_tn(x, pre_share))
        two = two + dot_nt(pre, weight(("up", part)))
    mem_ref[...] = two[rows:]
    grad = two[:rows]
    seq, by_unit = norm_back(seqpre_ref[...], row(small_ref, rows_of, "gain", 2), grad)
    gsmall_ref[3:4, :] = total(by_unit)
    gsmall_ref[4:5, :] = total(grad)
    low = seq.astype(LOW)
    put(11, dot_tn(wlow_ref[...], low))
    out_low = dot_nt(low, weight(11)).astype(LOW)
    wk, wv = wkv_ref[:, :width], wkv_ref[:, width:]
    wq = wq_ref[...]
    probs = write_probs(wk, wq)
    prob_grad = dot_nt(spread_heads(wv), out_low).reshape(probs.shape)
    delta = jnp.sum(probs * prob_grad, 1, keepdims=True)
    score_grad = (probs * (prob_grad - delta)).reshape(HEADS * PAD, rows).astype(LOW)
    wq_low = (dot_tn(score_grad, spread_heads(wk)) * SCALE).astype(LOW)
    part_ref[:PAD, :] = (fold_heads(dot(score_grad, wq)) * SCALE).astype(LOW)
    part_ref[PAD:, :] = fold_heads(dot(probs.reshape(HEADS * PAD, rows).astype(LOW), out_low)).astype(LOW)
    put(8, dot_tn(one_ref[:rows, :].astype(LOW), wq_low))
    seq_ref[...] = seq + dot_nt(wq_low, weight(8))


def read_back_kernel(
    share, weight, put, rows_of, own_ref, core_ref, chip_ref, both_ref, mem_ref, seq_ref, two_ref, mempre_ref, rout_ref, rlse_ref, rq_ref, rkv_ref, one_ref,
    pre_ref, small_ref,
    gsmall_ref, memgrad_ref, seqjoint_ref, part_ref,
):
    rows, width = seq_ref.shape
    summed = in_pairs([part[...].astype(F32) for part in (own_ref, core_ref, chip_ref, both_ref)])
    k_low = summed[:PAD].astype(LOW)
    v_low = summed[PAD:].astype(LOW)
    mem_low = two_ref[rows:, :].astype(LOW)
    put(9, dot_tn(mem_low, k_low) * share)
    put(10, dot_tn(mem_low, v_low) * share)
    grad = mem_ref[...] + dot_nt(k_low, weight(9)) + dot_nt(v_low, weight(10))
    mem, by_unit = norm_back(mempre_ref[...], row(small_ref, rows_of, "gain", 1), grad)
    gsmall_ref[0:1, :] = total(by_unit) * share
    gsmall_ref[1:2, :] = total(grad) * share
    low = mem.astype(LOW)
    rout = rout_ref[...]
    put(7, dot_tn(rout.astype(LOW), low) * share)
    out_low = dot_nt(low, weight(7)).astype(LOW)
    memgrad_ref[...] = mem
    rk, rv = rkv_ref[:, :width], rkv_ref[:, width:]
    rq = spread_heads(rq_ref[...] * jnp.asarray(SCALE, LOW))
    out_wide = spread_heads(out_low)
    delta = jnp.sum(spread_heads(out_low.astype(F32) * rout), -1, keepdims=True)
    mask = head_mask(width)
    lse = jnp.max(jnp.where(mask, rlse_ref[...][None], -BIG).reshape(HEADS * PAD, width), -1, keepdims=True)
    probs = jnp.exp(dot_nt(rq, rk) - lse)
    score_grad = (probs * (dot_nt(out_wide, rv) - delta)).astype(LOW)
    part_ref[...] = (fold_heads(dot(score_grad, rk)) * SCALE).astype(LOW)
    key_low = dot_tn(score_grad, rq).astype(LOW)
    value_low = dot_tn(probs.astype(LOW), out_wide).astype(LOW)
    seq_low = one_ref[:rows, :].astype(LOW)
    put(5, dot_tn(seq_low, key_low))
    put(6, dot_tn(seq_low, value_low))
    grad = seq_ref[...] + dot_nt(key_low, weight(5)) + dot_nt(value_low, weight(6))
    joint, by_unit = norm_back(pre_ref[:rows, :], row(small_ref, rows_of, "gain", 0), grad)
    gsmall_ref[2:3, :] = total(by_unit)
    gsmall_ref[3:4, :] = total(grad)
    seqjoint_ref[...] = joint


def attend_back_kernel(
    share, weight, put, rows_of, z_ref, part_ref, corepart_ref, chippart_ref, bothpart_ref, memgrad_ref, seqjoint_ref, one_ref, pre_ref, att_ref,
    q_ref, own_ref, core_ref, chip_ref, both_ref, kvmem_ref, segk_ref, segq_ref, small_ref,
    gsmall_ref, joint_ref, qgrad_ref, keep_ref, send_ref,
    keys_ref, bound_ref, out_ref, kvgrad_ref,
):
    rows, width = seqjoint_ref.shape
    full = att_ref.shape[0]
    place_keys(keys_ref, own_ref, core_ref, chip_ref, both_ref, kvmem_ref)
    bound_ref[...] = bound_of(segk_ref[...], segq_ref[...])
    parts = (part_ref, corepart_ref, chippart_ref, bothpart_ref)
    q_low = in_pairs([part[...].astype(F32) for part in parts]).astype(LOW)
    put(4, dot_tn(one_ref[rows:, :].astype(LOW), q_low) * share)
    grad = memgrad_ref[...] + dot_nt(q_low, weight(4))
    mem, by_unit = norm_back(pre_ref[rows:, :], row(small_ref, rows_of, "gain", 0), grad)
    gsmall_ref[0:1, :] = total(by_unit) * share
    gsmall_ref[1:2, :] = total(grad) * share
    joint_ref[:rows, :] = seqjoint_ref[...]
    joint_ref[rows:, :] = mem
    low = joint_ref[...].astype(LOW)
    balance = jnp.where(lax.broadcasted_iota(jnp.int32, (full, 1), 0) < rows, 1.0, share)
    put(3, dot_tn(att_ref[...], (low.astype(F32) * balance).astype(LOW)))
    out_ref[...] = dot_nt(low, weight(3)).astype(LOW)

    def pair(step, carry):
        lanes = pl.ds(pl.multiple_of(step * 128, 128), 128)
        more = pl.ds(pl.multiple_of(width + step * 128, 128), 128)
        query = q_ref[:, lanes] * jnp.asarray(SCALE, LOW)
        out = out_ref[:, lanes]
        low_balance = jnp.concatenate([balance, balance], 0)
        query = two_heads(query)
        out = two_heads(out)
        keys = keys_ref[:, lanes]
        values = keys_ref[:, more]
        scores = jnp.minimum(dot_nt(keys, query), bound_ref[...])
        expo = jnp.exp(scores - jnp.max(scores, 0, keepdims=True))
        probs = expo * (1.0 / jnp.sum(expo, 0, keepdims=True))
        prob_grad = dot_nt(values, out)
        delta = jnp.sum(probs * prob_grad, 0, keepdims=True)
        score_grad = (probs * (prob_grad - delta)).astype(LOW)
        qgrad_ref[:, lanes] = (pick_heads(dot_tn(keys, score_grad)) * SCALE).astype(LOW)
        query_share = (query.astype(F32) * low_balance).astype(LOW)
        out_share = (out.astype(F32) * low_balance).astype(LOW)
        kvgrad_ref[:, lanes] = dot(score_grad, query_share).astype(LOW)
        kvgrad_ref[:, more] = dot(probs.astype(LOW), out_share).astype(LOW)
        return carry

    lax.fori_loop(0, width // 128, pair, 0)
    z_low = z_ref[...].astype(LOW)
    put(0, dot_tn(z_low, (qgrad_ref[...].astype(F32) * balance).astype(LOW)))
    me = lax.axis_index("blk")
    for place, (goal, other) in enumerate(((keep_ref, 0), (keep_ref, 2), (send_ref, 1), (send_ref, 3))):
        rest = pl.ds(pl.multiple_of((me ^ other) * rows, rows), rows)
        goal[place % 2 * rows : (place % 2 + 1) * rows, :] = kvgrad_ref[rest, :]
    for goal in (keep_ref, send_ref):
        goal[2 * rows :, :] = kvgrad_ref[4 * rows :, :]


def input_back_kernel(
    share, weight, put, rows_of, z_ref, joint_ref, qgrad_ref, mine_ref, sent_ref, got_ref, *rest
):
    *small_refs, zgrad_ref, kvgrad_ref = rest
    full, width = z_ref.shape
    rows = full - PAD
    balance = jnp.where(lax.broadcasted_iota(jnp.int32, (full, 1), 0) < rows, 1.0, share)
    low = z_ref[...].astype(LOW)
    kvgrad_ref[:rows, :] = (mine_ref[...] + got_ref[:rows, :].astype(F32)).astype(LOW)
    kvgrad_ref[rows:, :] = (sent_ref[rows:, :].astype(F32) + got_ref[rows:, :].astype(F32)).astype(LOW)
    grads = (qgrad_ref[...], kvgrad_ref[:, :width], kvgrad_ref[:, width:])
    grad = joint_ref[...]
    for part, value in enumerate(grads):
        if part > 0:
            put(part, dot_tn(low, (value.astype(F32) * balance).astype(LOW)))
        grad = grad + dot_nt(value, weight(part))
    zgrad_ref[...] = grad
    if small_refs:
        layers = [[ref[...] for ref in small_refs[k : k + 4]] for k in range(0, len(small_refs), 4)]
        lines = []
        for one, two, three, _ in layers:
            lines.extend([two[2:3] + three[0:1], two[0:1], one[3:4], one[0:1]])
        for one, two, three, _ in layers:
            lines.extend([two[3:4] + three[1:2], two[1:2], one[4:5], one[1:2], one[2:3]])
        lines.extend(bias for _, _, _, bias in layers)
        lines.append(grad[rows:] * share)
        small = jnp.concatenate(lines, 0)
        small = jnp.concatenate([small, jnp.zeros((width - small.shape[0], width), F32)], 0)
        put("small", small.T)


class Order:
    def __init__(self, stages):
        self.stages = stages

    def place(self, number):
        result = 0
        for stage in self.stages:
            result = 2 * result + ((number >> bit_place(stage)) & 1)
        return result

    def mine(self):
        result = 0
        for axis, bit in self.stages:
            result = 2 * result + ((lax.axis_index(axis) >> bit) & 1)
        return result


def call(kernel, name, cost, ins, outs, weights, scratch=(), grads=None, after=(), rows_of=None):
    sources, operands, begins = [], [], []
    for source, _, _ in weights.values():
        if not any(source is other for other in sources):
            sources.append(source)
            begins.append(len(operands))
            operands.extend(source[0])
    places, slots = {}, 0
    for key, (source, slot, count) in weights.items():
        which = [source is other for other in sources].index(True)
        places[key] = (which, slot, slots, count)
        slots = slots + count
    high, width = operands[0].shape[2:]
    shards = width // high
    grad_slots, number = {}, 0
    if grads is not None:
        for key in grads[0]:
            if key in ("down",):
                grad_slots[key] = number
                number += grads[2]
            else:
                grad_slots[key] = number
                number += 1
    halves = 0 if grads is None else (1 if grads[1] is None else 2)

    def body(*refs):
        in_refs, refs = refs[: len(ins)], refs[len(ins) :]
        operand_refs, refs = refs[: len(operands)], refs[len(operands) + len(after) :]
        grad_refs, refs = refs[:halves], refs[halves:]
        if halves:
            *refs, buffer, sems, made, made_sems = refs
        else:
            *refs, buffer, sems = refs
        core = lax.axis_index("blk") % 2
        copies = {}
        for turn, (key, (which, slot, place, count)) in enumerate(places.items()):
            copies[key] = []
            arrays = len(sources[which][0])
            piece = shards // arrays
            for part in range(arrays):
                copy = pltpu.make_async_copy(
                    operand_refs[begins[which] + part].at[:, pl.ds(slot, count)],
                    buffer.at[pl.ds(part * piece, piece), pl.ds(place, count)],
                    sems.at[turn, part],
                )
                copy.start()
                copies[key].append(copy)
        arrived = set()
        offsets = [None if order is None else order.mine() for _, order in sources]

        def weight(key, part=None):
            if key not in arrived:
                for copy in copies[key]:
                    copy.wait()
                arrived.add(key)
            which, _, place, count = places[key]
            order = sources[which][1]
            span = range(shards) if part is None else range(part * (shards // count), (part + 1) * (shards // count))
            pieces = []
            for shard in span:
                if order is None:
                    at = shard
                else:
                    at = ((shard % 2) ^ core) * (shards // 2) + (order.place(shard) ^ offsets[which])
                pieces.extend(buffer[at, place + slot] for slot in range(count))
            return jnp.concatenate(pieces, 0)

        out = []
        if halves:
            offset = None if grads[1] is None else grads[1].mine()

        def put(key, grad):
            low = grad.astype(LOW)
            if isinstance(key, tuple) and key[0] == "down":
                count, slot, first = grads[2], grad_slots["down"], key[1] * (shards // grads[2])
            else:
                count, slot, first = 1, grad_slots[key], 0
            for block in range(low.shape[0] // high):
                shard, inner = first + block // count, block % count
                value = low[block * high : (block + 1) * high]
                if halves == 1:
                    made[shard, slot + inner] = value
                else:
                    at = ((shard % 2) ^ core) * (shards // 2) + (grads[1].place(shard) ^ offset)
                    made[at, slot + inner] = value
            if count == 1 or key[1] == count - 1:
                piece = shards // halves
                for half in range(halves):
                    copy = pltpu.make_async_copy(
                        made.at[pl.ds(half * piece, piece), pl.ds(slot, count)],
                        grad_refs[half].at[:, pl.ds(slot, count)],
                        made_sems.at[slot, half],
                    )
                    copy.start()
                    out.append(copy)

        kernel(weight, put, rows_of, *in_refs, *refs)
        for copy in out:
            copy.wait()

    inside, anywhere = pl.BlockSpec(memory_space=pltpu.VMEM), pl.BlockSpec(memory_space=pl.ANY)
    shapes = [jax.ShapeDtypeStruct((shards // max(halves, 1), number, high, width), LOW)] * halves
    scratch = list(scratch) + [
        pltpu.VMEM((shards, slots, high, width), LOW),
        pltpu.SemaphoreType.DMA((len(weights), 2)),
    ]
    if halves:
        scratch += [pltpu.VMEM((shards, number, high, width), LOW), pltpu.SemaphoreType.DMA((number, 2))]
    results = pl.pallas_call(
        body,
        out_shape=shapes + [jax.ShapeDtypeStruct(shape, kind) for shape, kind in outs],
        in_specs=[inside] * len(ins) + [anywhere] * (len(operands) + len(after)),
        out_specs=[anywhere] * halves + [inside] * len(outs),
        scratch_shapes=scratch,
        compiler_params=pltpu.CompilerParams(vmem_limit_bytes=VMEM_LIMIT),
        cost_estimate=pl.CostEstimate(flops=int(cost * 1.1e8), bytes_accessed=0, transcendentals=0),
        name=name,
    )(*ins, *operands, *after)
    return ([results[:halves]] if halves else []) + list(results[halves:])


def flipped(value, bit):
    size = lax.axis_size("blk")
    return lax.ppermute(value, "blk", [(source, source ^ bit) for source in range(size)])


def quartet(value):
    return [value] + [flipped(value, bit) for bit in (1, 2, 3)]


def bits_of(axis):
    return lax.axis_size(axis).bit_length() - 1


def bit_place(stage):
    axis, bit = stage
    return bit if axis == "blk" else bits_of("blk") + bit


def swapped(value, stage):
    axis, bit = stage
    return lax.ppermute(value, axis, [(source, source ^ (1 << bit)) for source in range(lax.axis_size(axis))])


def fence(*arrays):
    return list(lax.optimization_barrier(tuple(arrays)))


class Gathering:
    def __init__(self, groups):
        self.groups = groups
        self.held = [shard[None] for shard, _, _ in groups]
        self.got, self.turn = {}, 0

    def begin(self):
        done = {}
        for number, (_, stages, first) in enumerate(self.groups):
            if first <= self.turn < first + len(stages):
                self.got[number] = swapped(self.held[number], stages[self.turn - first])
                if self.turn - first + 1 == len(stages):
                    done[number] = ((self.held[number], self.got.pop(number)), Order(stages[-2::-1]))
        return done

    def end(self, *others):
        for number, value in self.got.items():
            self.held[number] = jnp.concatenate([self.held[number], value])
        self.turn += 1
        waiting = [n for n, (_, stages, first) in enumerate(self.groups) if self.turn < first + len(stages)]
        bundle = fence(*[self.held[n] for n in waiting], *others)
        for number, value in zip(waiting, bundle):
            self.held[number] = value
        self.got = {}
        return bundle[len(waiting) :]


def joined(values):
    return values[0] if len(values) == 1 else jnp.concatenate(values, 1)


class Scattering:
    def __init__(self, arrays, stages):
        self.keeps = [keep for keep, _ in arrays]
        self.sends = [send for _, send in arrays]
        self.stages = list(stages)
        self.gots, self.result = None, None

    def begin(self):
        stage = self.stages.pop(0)
        self.gots = [swapped(send, stage) for send in self.sends]

    def end(self):
        sums = [keep.astype(F32) + got.astype(F32) for keep, got in zip(self.keeps, self.gots)]
        self.gots = None
        if not self.stages:
            self.result = joined(sums)[0]
            return
        half = sums[0].shape[0] // 2
        self.keeps = [joined([value[:half] for value in sums]).astype(LOW)]
        self.sends = [joined([value[half:] for value in sums]).astype(LOW)]


class Background:
    def __init__(self):
        self.sums, self.running = {}, []

    def add(self, name, arrays, stages):
        self.sums[name] = Scattering(arrays, stages)

    def begin(self, *names):
        for name in names:
            if name in self.sums:
                self.sums[name].begin()
                self.running.append(self.sums[name])

    def end(self, *others):
        if not self.running:
            return list(others)
        gots = [got for run in self.running for got in run.gots]
        gots = fence(*gots, *others)
        for run in self.running:
            run.gots, gots = gots[: len(run.gots)], gots[len(run.gots) :]
            run.end()
        self.running = []
        return gots


def local(
    tokens, segments, memory_init, attn_weights, ffn_in, ffn_out, ffn_bias, norm_gain, norm_shift, out_grad, memory_cot
):
    layers, count, rows, width = attn_weights.shape
    hidden = ffn_in.shape[2]
    per = hidden // width
    everyone = lax.axis_size("dp") * lax.axis_size("blk")
    direct = rows == 16
    core_bit, chip_bits = ("blk", 0), [("blk", bit) for bit in range(1, bits_of("blk"))]
    line_bits, near_bit = [("dp", bit) for bit in reversed(range(1, bits_of("dp")))], [("dp", 0)]

    small = [
        norm_gain.reshape(-1, rows), norm_shift.reshape(-1, rows), ffn_bias.reshape(-1, rows), memory_init
    ]
    starts = [sum(part.shape[0] for part in small[:k]) for k in range(5)]
    gain_rows, shift_rows = norm_gain.shape[1], norm_shift.shape[1]
    small = jnp.concatenate(small, 0).T.astype(LOW)
    small = jnp.pad(small, ((0, 0), (0, width - small.shape[1])))[None]

    def rows_of(index):
        return dict(gain=starts[0] + index * gain_rows, shift=starts[1] + index * shift_rows, memory=starts[3])

    attn_low, up_low, down_low = attn_weights.astype(LOW), ffn_in.astype(LOW), ffn_out.astype(LOW)
    up_low = up_low.reshape(layers, rows, per, width).transpose(0, 2, 1, 3)
    down_low = down_low.reshape(layers, per, rows, width)
    early, middle, late = (0, 1, 2), (3, 8, 4, 5, 6), (7, 9, 10, 11)
    table = {}

    def listed(source, index, keys):
        place = 0
        for key in keys:
            size = per if key == "down" else 1
            table[index, key] = (source, place, size)
            place += size

    ups = tuple(("up", part) for part in range(per))
    if direct:

        def picked(index, keys):
            return [attn_low[index, key][None] for key in keys]

        y_last = line_bits + chip_bits + near_bit + [core_bit]
        x_last = near_bit + line_bits + chip_bits + [core_bit]
        x_early = chip_bits + line_bits + near_bit + [core_bit]
        gathering = Gathering(
            [
                (jnp.concatenate(picked(0, early) + [small]), y_last, 0),
                (jnp.concatenate(picked(0, middle)), y_last, 1),
                (jnp.concatenate(picked(0, late) + [up_low[0]]), y_last, 2),
                (jnp.concatenate([down_low[0]] + picked(1, early)), x_last, 2),
                (jnp.concatenate(picked(1, middle)), x_early, 4),
            ]
        )
        rest = jnp.concatenate(picked(1, late) + [up_low[1], down_low[1]])
        for turn in range(4):
            if turn == GATHER_AT:
                whole = lax.all_gather(rest, ALL)
            gathering.begin()
            (rest,) = gathering.end(rest)
        if GATHER_AT == 4:
            whole = lax.all_gather(rest, ALL)
        listed(gathering.begin()[0], 0, early + ("small",))
        listed(((whole,), None), 1, late + ups + ("down",))
    else:
        packed = jnp.concatenate(
            [attn_low.reshape(-1, rows, width), up_low.reshape(-1, rows, width), small, down_low.reshape(-1, rows, width)]
        )
        whole = lax.all_gather(packed, ALL)
        split = layers * (count + per) + 1
        square = whole[:, :split].transpose(1, 0, 2, 3).reshape(split, -1, 16, width)
        downs = whole[:, split:].reshape(everyone, layers, per * rows, width).transpose(1, 0, 2, 3)
        downs = downs.reshape(layers, -1, per, 16, width).transpose(0, 2, 1, 3, 4).reshape(layers * per, -1, 16, width)
        source = ((jnp.concatenate([square, downs]).transpose(1, 0, 2, 3),), None)
        for index in range(layers):
            for key in range(count):
                table[index, key] = (source, index * count + key, 1)
            for part in range(per):
                table[index, ("up", part)] = (source, layers * count + index * per + part, 1)
            table[index, "down"] = (source, split + index * per, per)
        table[0, "small"] = (source, split - 1, 1)

    def attn(index, *keys):
        return {key: table[index, key] for key in keys}

    def feed(index):
        return attn(index, *ups, "down")

    length = tokens.shape[1]
    full = length + PAD
    size = lax.axis_size("blk")
    share = 1.0 / size
    me = lax.axis_index("blk")
    seg = segments[0].astype(F32)
    seg_parts = jnp.zeros((size, length), F32)
    for other, part in enumerate(quartet(segments)):
        seg_parts = lax.dynamic_update_slice(seg_parts, part.astype(F32), (me ^ other, 0))
    seg_keys = jnp.concatenate(
        [seg_parts.reshape(-1), jnp.full((MEM,), -2.0, F32), jnp.full((PAD - MEM,), -3.0, F32)]
    ).reshape(-1, 1)
    seg_row = jnp.concatenate([seg, jnp.full((PAD,), -1.0, F32)])
    seg_queries = jnp.concatenate([seg_row, seg_row]).reshape(1, -1)
    every = size * length + PAD
    keys_scratch = pltpu.VMEM((every, 2 * width), LOW)
    bound_scratch = pltpu.VMEM((every, 2 * full), F32)
    projected = [((full, width), LOW), ((length, 2 * width), LOW), ((PAD, 2 * width), LOW)]

    smalls, z, q, own, kvmem = call(
        first_kernel,
        "first",
        4,
        [tokens[0]],
        [((128, width), F32), ((full, width), F32)] + projected,
        attn(0, *early, "small"),
        rows_of=rows_of(0),
    )
    bias = smalls[starts[2] : starts[3]].reshape(layers, per, everyone, rows).transpose(0, 2, 1, 3)
    bias = bias.reshape(layers, per, width)
    kept = []
    for index in range(layers):
        core = flipped(own, 1)
        chip = flipped(own, 2)
        both = flipped(chip, 1)
        if direct:
            core, chip, both, seg_keys = gathering.end(core, chip, both, seg_keys)
            listed(gathering.begin()[1 if index == 0 else 4], index, middle)
        att, pre, first, rq, rkv, wq, part = call(
            attend_kernel,
            f"attend_{index}",
            13,
            [z, q, own, core, chip, both, kvmem, seg_keys, seg_queries, smalls],
            [
                ((full, width), LOW), ((full, width), F32), ((full, width), F32), ((PAD, width), LOW),
                ((length, 2 * width), LOW), ((length, width), LOW), ((PAD, width + 128), F32),
            ],
            attn(index, 3, 8, 4, 5, 6),
            [keys_scratch, bound_scratch],
            rows_of=rows_of(index),
        )
        parts = quartet(part)
        if direct and index == 0:
            parts = gathering.end(*parts)
            found = gathering.begin()
            listed(found[2], 0, late + ups)
            listed(found[3], 0, ("down",))
            for key in early:
                table[1, key] = (found[3], per + key, 1)
        last = index + 1 == layers
        results = call(
            functools.partial(finish_kernel, last),
            f"finish_{index}",
            10,
            [first, *parts, wq, bias[index], smalls],
            [((full, width), F32)]
            + ([] if last else projected)
            + [
                ((PAD, width), F32), ((PAD, width), F32), ((PAD, width), F32), ((full, width), F32),
                ((PAD, 2 * width), LOW), ((length, width), LOW), ((length, width), F32), ((full, width), LOW),
                ((full, width), F32),
            ],
            attn(index, 7, 9, 10, 11) | feed(index) | ({} if last else attn(index + 1, *early)),
            rows_of=rows_of(index),
        )
        rout, rlse, mempre, second, wkv, wlow, seqpre, x, feedpre = results[-9:]
        kept.append(
            dict(
                z=z, q=q, own=own, kvmem=kvmem, core=core, chip=chip, both=both, att=att, pre=pre, first=first,
                rq=rq, rkv=rkv, wq=wq, rout=rout, rlse=rlse, mempre=mempre, second=second, wkv=wkv, wlow=wlow,
                seqpre=seqpre, x=x, feedpre=feedpre,
            )
        )
        z = results[0]
        if not last:
            q, own, kvmem = results[1:4]
            if direct:
                q, own, kvmem = gathering.end(q, own, kvmem)
                gathering.begin()
    final = z
    grad = jnp.concatenate(
        [out_grad[0].astype(F32), jnp.pad(memory_cot[0].astype(F32), ((0, PAD - MEM), (0, 0)))]
    )
    background = Background()
    upward = line_bits[::-1]
    x_late = near_bit + upward + chip_bits
    y_first = near_bit + chip_bits + upward
    x_first = chip_bits + near_bit + upward
    z_first = upward[:1] + near_bit + chip_bits + upward[1:]
    orders = {"early": (z_first, x_late), "middle": (y_first, x_late), "attend": (x_first, x_late), "last": (y_first, x_late)}

    def given(keys, order):
        return (keys, Order(order) if direct else None, per)

    group_keys = [ups + ("down", 11, 8), (9, 10, 7, 5, 6), (4, 3, 0), (1, 2)]
    made = [None] * layers
    for index in reversed(range(layers)):
        k = kept[index]
        grads_one, gbias, small_one, mem, seq, part = call(
            functools.partial(feed_back_kernel, share),
            f"feed_back_{index}",
            14,
            [grad, k["feedpre"], k["x"], k["seqpre"], k["wlow"], k["wq"], k["wkv"], k["first"], bias[index], smalls],
            [
                ((per, width), F32),
                ((5, width), F32), ((PAD, width), F32), ((length, width), F32), ((2 * PAD, width), LOW),
            ],
            feed(index) | attn(index, 11, 8),
            grads=given(group_keys[0], orders["early"][min(index, 1)]),
            rows_of=rows_of(index),
        )
        part, mem, seq = background.end(part, mem, seq)
        if direct:
            background.add(f"early_{index}", [grads_one], [core_bit] + orders["early"][min(index, 1)])
        background.begin(*PLAN[index][0])
        grads_two, small_two, mem, seq, part = call(
            functools.partial(read_back_kernel, share),
            f"read_back_{index}",
            7,
            [*quartet(part), mem, seq, k["second"], k["mempre"], k["rout"], k["rlse"], k["rq"], k["rkv"],
             k["first"], k["pre"], smalls],
            [((4, width), F32), ((PAD, width), F32), ((length, width), F32), ((PAD, width), LOW)],
            attn(index, 9, 10, 7, 5, 6),
            grads=given(group_keys[1], orders["middle"][min(index, 1)]),
            rows_of=rows_of(index),
        )
        part, mem, seq = background.end(part, mem, seq)
        if direct and index == 0:
            background.add("middle_0", [grads_two], [core_bit] + orders["middle"][0])
        background.begin(*PLAN[index][1])
        grads_three, small_three, joint, qgrad, keep, send = call(
            functools.partial(attend_back_kernel, share),
            f"attend_back_{index}",
            18,
            [k["z"], *quartet(part), mem, seq, k["first"], k["pre"], k["att"], k["q"], k["own"], k["core"], k["chip"],
             k["both"], k["kvmem"], seg_keys, seg_queries, smalls],
            [((2, width), F32), ((full, width), F32), ((full, width), LOW),
             ((2 * length + PAD, 2 * width), LOW), ((2 * length + PAD, 2 * width), LOW)],
            attn(index, 4, 3),
            [keys_scratch, bound_scratch, pltpu.VMEM((full, width), LOW), keys_scratch],
            grads=given(group_keys[2], orders["attend"][min(index, 1)]),
            rows_of=rows_of(index),
        )
        keep, send = background.end(keep, send)
        if direct and index == 0:
            background.add("attend_0", [grads_three], [core_bit] + orders["attend"][0])
        background.begin(*PLAN[index][2])
        pair_sum = keep.astype(F32) + flipped(send, 1).astype(F32)
        mine_part, theirs = pair_sum[:length], pair_sum[length:].astype(LOW)
        got = flipped(theirs, 2)
        got, mine_part, theirs = background.end(got, mine_part, theirs)
        background.begin(*PLAN[index][3])
        made[index] = dict(
            small=[small_one, small_two, small_three],
            bias=gbias.reshape(everyone, per, rows).transpose(1, 0, 2).reshape(per, width),
        )
        tiny = sum([m["small"] + [m["bias"]] for m in made], []) if index == 0 else []
        grads_four, grad = call(
            functools.partial(input_back_kernel, share),
            f"input_back_{index}",
            5,
            [k["z"], joint, qgrad, mine_part, theirs, got] + tiny,
            [((full, width), F32)],
            attn(index, 0, 1, 2),
            [pltpu.VMEM((full, 2 * width), LOW)],
            grads=given(group_keys[3] + (("small",) if tiny else ()), orders["last"][min(index, 1)]),
        )
        if direct and index > 0:
            background.add(f"middle_{index}", [grads_two, grads_three, grads_four], [core_bit] + x_late)
        made[index]["grads"] = (grads_one, grads_two, grads_three, grads_four)

    mine = [{} for _ in range(layers)]
    if direct:
        (kept_four,) = background.end(grads_four[0])
        background.add("last", [(kept_four, grads_four[1])], [core_bit] + orders["last"][0])
        for names in PLAN[0][4:]:
            background.begin(*names)
            background.end()
        for index in range(layers):
            wanted = (f"early_{index}", f"middle_{index}") + (("attend_0", "last") if index == 0 else ())
            results = [background.sums[name].result for name in wanted]
            keys = list(group_keys)
            if index > 0:
                keys = [keys[0], keys[1] + keys[2] + keys[3]]
            else:
                keys[3] = keys[3] + ("small",)
            for result, held in zip(results, keys):
                place = 0
                for key in held:
                    number = per if key == "down" else 1
                    mine[index][key] = result[place : place + number].reshape(number * rows, width)
                    place += number
    else:
        outgoing, order = [], []
        for index, m in enumerate(made):
            held = sum(group_keys, ()) + (("small",) if index == 0 else ())
            stack = jnp.concatenate([part[0] for part in m["grads"]], 1).transpose(1, 0, 2, 3)
            place = 0
            for key in held:
                if key == "down":
                    downs = stack[place : place + per].transpose(1, 0, 2, 3).reshape(everyone, per, rows, width)
                    outgoing.append(downs.transpose(1, 0, 2, 3).reshape(per, width, width))
                    order.extend((index, ("down", part)) for part in range(per))
                    place += per
                else:
                    outgoing.append(stack[place].reshape(1, width, width))
                    order.append((index, key))
                    place += 1
        result = lax.psum_scatter(jnp.concatenate(outgoing), ALL, scatter_dimension=1, tiled=True).astype(F32)
        for place, (index, key) in enumerate(order):
            mine[index][key] = result[place]
        for m in mine:
            m["down"] = jnp.concatenate([m["down", part] for part in range(per)])
    back = mine[0]["small"].T
    return (
        final[:length].astype(LOW)[None],
        final[length : length + MEM][None],
        grad[:length][None],
        back[starts[3] : starts[4]],
        jnp.stack([jnp.stack([m[key] for key in range(count)]) for m in mine]),
        jnp.stack([jnp.concatenate([m["up", part] for part in range(per)], -1) for m in mine]),
        jnp.stack([m["down"] for m in mine]),
        back[starts[2] : starts[3]].reshape(ffn_bias.shape),
        back[starts[0] : starts[1]].reshape(norm_gain.shape),
        back[starts[1] : starts[2]].reshape(norm_shift.shape),
    )


def solution(mesh):
    in_specs = (
        P("dp", "blk", None),
        P("dp", "blk"),
        P(None, ALL),
        P(None, None, ALL, None),
        P(None, ALL, None),
        P(None, ALL, None),
        P(None, ALL),
        P(None, None, ALL),
        P(None, None, ALL),
        P("dp", "blk", None),
        P("dp", None, None),
    )
    out_specs = (
        P("dp", "blk", None),
        P("dp", None, None),
        P("dp", "blk", None),
        P(None, ALL),
        P(None, None, ALL, None),
        P(None, ALL, None),
        P(None, ALL, None),
        P(None, ALL),
        P(None, None, ALL),
        P(None, None, ALL),
    )
    return jax.shard_map(local, mesh=mesh, in_specs=in_specs, out_specs=out_specs, check_vma=False)
```

```python
import functools

import jax
import jax.numpy as jnp
from jax import lax
from jax.experimental import pallas as pl
from jax.experimental.pallas import tpu as pltpu
from jax.sharding import PartitionSpec as P

HEADS = 8
HEAD = 64
MEM = 20
PAD = 32
NEG = -1000000000.0
BIG = 3.0e38
EPS = 1e-05
SCALE = HEAD**-0.5
ALL = ("dp", "blk")
LOW = jnp.bfloat16
F32 = jnp.float32
VMEM_LIMIT = 24 * 1024 * 1024
PLAN = {
    1: [
        ("up_1", "down_1"),
        ("up_1", "down_1"),
        ("up_1", "down_1", "first_1"),
        ("up_1", "down_1", "first_1"),
        ("up_1", "down_1", "first_1"),
    ],
    0: [
        ("up_0", "down_0", "second_1", "first_1"),
        ("up_0", "down_0"),
        ("up_0", "down_0", "first_0", "second_1"),
        ("up_0", "down_0", "first_0", "second_1"),
        ("up_0", "first_1", "first_0", "second_1"),
        ("last", "second_0", "down_0"),
        ("last", "second_0", "first_0", "second_1"),
        ("last", "second_0", "first_0"),
        ("last", "second_0"),
        ("last", "second_0"),
    ],
}


def dot(a, b):
    return jnp.dot(a, b, preferred_element_type=F32)


def dot_nt(a, b):
    return lax.dot_general(a, b, (((1,), (1,)), ((), ())), preferred_element_type=F32)


def dot_tn(a, b):
    return lax.dot_general(a, b, (((0,), (0,)), ((), ())), preferred_element_type=F32)


def hat(x):
    center = x - jnp.mean(x, -1, keepdims=True)
    spread = jnp.mean(center * center, -1, keepdims=True)
    inv = lax.rsqrt(spread + EPS)
    return center * inv, inv


def norm(x, gain, shift):
    return hat(x)[0] * gain + shift


def norm_back(x, gain, grad):
    unit, inv = hat(x)
    scaled = grad * gain
    mean_one = jnp.mean(scaled, -1, keepdims=True)
    mean_two = jnp.mean(scaled * unit, -1, keepdims=True)
    return inv * (scaled - mean_one - unit * mean_two), grad * unit


def row(small_ref, rows_of, name, which):
    place = rows_of[name] + which
    return small_ref[place : place + 1, :]


def total(x):
    return jnp.sum(x, 0, keepdims=True)


def gelu_parts(u):
    k = 0.7978845608028654
    t = jnp.tanh(k * (u + 0.044715 * u * u * u))
    half = 0.5 * (1.0 + t)
    slope = half + 0.5 * u * (1.0 - t * t) * (k * (1.0 + 0.134145 * u * u))
    return u * half, slope


def head_mask(width):
    lanes = lax.broadcasted_iota(jnp.int32, (HEADS, 1, width), 2) // HEAD
    return lanes == lax.broadcasted_iota(jnp.int32, (HEADS, 1, width), 0)


def spread_heads(x):
    rows, width = x.shape
    full = jnp.where(head_mask(width), x.astype(F32)[None], 0.0)
    return full.reshape(HEADS * rows, width).astype(x.dtype)


def fold_heads(x):
    rows, width = x.shape
    full = x.reshape(HEADS, rows // HEADS, width)
    return jnp.sum(jnp.where(head_mask(width), full, 0.0), 0)


def two_heads(x):
    first = lax.broadcasted_iota(jnp.int32, x.shape, 1) < HEAD
    zero = jnp.zeros_like(x)
    return jnp.concatenate([jnp.where(first, x, zero), jnp.where(first, zero, x)], 0)


def pick_heads(x):
    width, rows = x.shape
    mine = (lax.broadcasted_iota(jnp.int32, x.shape, 0) < HEAD) == (
        lax.broadcasted_iota(jnp.int32, x.shape, 1) < rows // 2
    )
    both = jnp.where(mine, x, 0.0).T
    return both[: rows // 2] + both[rows // 2 :]


def place_bounds(bound_ref, seg_refs, seg_queries):
    rows = seg_refs[0].shape[1]
    me = lax.axis_index("blk")
    for other, seg_ref in enumerate(seg_refs):
        numbers = jnp.broadcast_to(seg_ref[...].astype(F32), (128, rows)).T[:, 0:1]
        allowed = (numbers == seg_queries) | (seg_queries == -1.0)
        place = pl.ds(pl.multiple_of((me ^ other) * rows, rows), rows)
        bound_ref[place, :] = jnp.where(allowed, BIG, NEG)
    memory = lax.broadcasted_iota(jnp.int32, (PAD, seg_queries.shape[1]), 0) < MEM
    bound_ref[4 * rows :, :] = jnp.where(memory, BIG, NEG)


def place_keys(keys_ref, own_ref, core_ref, chip_ref, both_ref, memory_ref):
    rows = core_ref.shape[0]
    me = lax.axis_index("blk")
    pieces = ((me, own_ref), (me ^ 1, core_ref), (me ^ 2, chip_ref), (me ^ 3, both_ref))
    for place, piece in pieces:
        keys_ref[pl.ds(pl.multiple_of(place * rows, rows), rows), :] = piece[0:rows, :]
    keys_ref[4 * rows :, :] = memory_ref[...]


def project(z, weight, q_ref, kv_ref, kvmem_ref):
    low = z.astype(LOW)
    rows, width = kv_ref.shape[0], low.shape[1]
    for part in (1, 2):
        lanes = pl.ds((part - 1) * width, width)
        value = dot(low, weight(part)).astype(LOW)
        kv_ref[:, lanes] = value[:rows]
        kvmem_ref[:, lanes] = value[rows:]
    q_ref[...] = dot(low, weight(0)).astype(LOW)


def bias_order(width, high, per):
    lanes = lax.broadcasted_iota(jnp.int32, (width, width), 0)
    shard, inner = lanes // (per * high), lanes % (per * high)
    goal = inner // high * (width // per) + shard * high + inner % high
    return (goal == lax.broadcasted_iota(jnp.int32, (width, width), 1)).astype(LOW)


def first_kernel(weight, put, rows_of, tokens_ref, small_ref, z_ref, q_ref, kv_ref, kvmem_ref):
    rows = tokens_ref.shape[0]
    columns = weight("small")[:, :128]
    small = columns.astype(F32).T
    width = small.shape[1]
    small_ref[...] = small
    high, per, start = rows_of["sizes"]
    order = bias_order(width, high, per)
    for layer in range((rows_of["memory"] - start) // per):
        lines = small[start + layer * per : start + (layer + 1) * per].astype(LOW)
        piece = width // per
        for part in range(per):
            line = jnp.concatenate([lines[j : j + 1, part * piece : (part + 1) * piece] for j in range(per)], 1)
            place = 64 + layer * per + part
            small_ref[place : place + 1, :] = dot_nt(line, order)
    z_ref[:rows, :] = tokens_ref[...].astype(F32)
    start = rows_of["memory"]
    z_ref[rows : rows + MEM, :] = small[start : start + MEM]
    z_ref[rows + MEM :, :] = jnp.zeros((PAD - MEM, small.shape[1]), F32)
    project(z_ref[...], weight, q_ref, kv_ref, kvmem_ref)


def attend_kernel(
    weight, put, rows_of, z_ref, q_ref, own_ref, core_ref, chip_ref, both_ref, kvmem_ref, sega_ref, segb_ref, segc_ref, segd_ref, segq_ref, small_ref,
    att_ref, lse_ref, pre_ref, one_ref, rq_ref, rkv_ref, wq_ref, part_ref,
    keys_ref, bound_ref,
):
    rows = core_ref.shape[0]
    width = z_ref.shape[1]
    place_keys(keys_ref, own_ref, core_ref, chip_ref, both_ref, kvmem_ref)
    place_bounds(bound_ref, (sega_ref, segb_ref, segc_ref, segd_ref), segq_ref[...])

    def pair(step, carry):
        lanes = pl.ds(pl.multiple_of(step * 128, 128), 128)
        more = pl.ds(pl.multiple_of(width + step * 128, 128), 128)
        query = two_heads(q_ref[:, lanes]) * jnp.asarray(SCALE, LOW)
        keys = keys_ref[:, lanes]
        values = keys_ref[:, more]
        scores = jnp.minimum(dot_nt(keys, query), bound_ref[...])
        top = jnp.max(scores, 0, keepdims=True)
        expo = jnp.exp(scores - top)
        summed = jnp.sum(expo, 0, keepdims=True)
        att_ref[:, lanes] = pick_heads(dot_tn(values, expo.astype(LOW)) * (1.0 / summed)).astype(LOW)
        lse_ref[pl.ds(step, 1), :] = top + jnp.log(summed)
        return carry

    lax.fori_loop(0, width // 128, pair, 0)
    pre = z_ref[...] + dot(att_ref[...], weight(3))
    pre_ref[...] = pre
    one = norm(pre, row(small_ref, rows_of, "gain", 0), row(small_ref, rows_of, "shift", 0))
    one_ref[...] = one
    low = one.astype(LOW)
    seq_low, mem_low = low[:rows], low[rows:]
    wq_ref[...] = dot(seq_low, weight(8)).astype(LOW)
    rq = dot(mem_low, weight(4)).astype(LOW)
    rk = dot(seq_low, weight(5)).astype(LOW)
    rv = dot(seq_low, weight(6)).astype(LOW)
    rq_ref[...] = rq
    rkv_ref[:, :width] = rk
    rkv_ref[:, width:] = rv
    scores = dot_nt(spread_heads(rq * jnp.asarray(SCALE, LOW)), rk)
    top = jnp.max(scores, -1, keepdims=True)
    expo = jnp.exp(scores - top)
    summed = jnp.sum(expo, -1, keepdims=True)
    part_ref[:, :width] = fold_heads(dot(expo.astype(LOW), rv))
    lanes = lax.broadcasted_iota(jnp.int32, (HEADS, PAD, 128), 2)
    heads = lax.broadcasted_iota(jnp.int32, (HEADS, PAD, 128), 0)
    top = jnp.where(lanes == heads, top.reshape(HEADS, PAD, 1), 0.0)
    summed = jnp.where(lanes == heads + HEADS, summed.reshape(HEADS, PAD, 1), 0.0)
    part_ref[:, width:] = jnp.sum(top + summed, 0)


def in_pairs(values):
    own, core, chip, both = values
    return (own + core) + (chip + both)


def widened(stats, start, width):
    lanes = lax.broadcasted_iota(jnp.int32, (128, width), 0)
    heads = lax.broadcasted_iota(jnp.int32, (128, width), 1) // HEAD + start
    return jnp.dot(
        stats, (lanes == heads).astype(F32), precision=lax.Precision.HIGHEST, preferred_element_type=F32
    )


def write_probs(wk, wq):
    scores = dot_nt(spread_heads(wk * jnp.asarray(SCALE, LOW)), wq)
    scores = scores.reshape(HEADS, PAD, scores.shape[1])
    real = lax.broadcasted_iota(jnp.int32, scores.shape, 1) < MEM
    scores = jnp.where(real, scores, NEG)
    expo = jnp.exp(scores - jnp.max(scores, 1, keepdims=True))
    return expo * (1.0 / jnp.sum(expo, 1, keepdims=True))


def finish_kernel(
    last, weight, put, rows_of, one_ref, own_ref, core_ref, chip_ref, both_ref, wq_ref, small_ref, *rest
):
    if last:
        (z_ref, rout_ref, rlse_ref, mempre_ref, two_ref, wkv_ref, wlow_ref, seqpre_ref, x_ref, feedpre_ref) = rest
    else:
        (z_ref, q_ref, kv_ref, kvmem_ref,
         rout_ref, rlse_ref, mempre_ref, two_ref, wkv_ref, wlow_ref, seqpre_ref, x_ref, feedpre_ref) = rest
    rows, width = wq_ref.shape
    parts = (own_ref, core_ref, chip_ref, both_ref)
    tops = [widened(part[:, width:], 0, width) for part in parts]
    sums = [widened(part[:, width:], HEADS, width) for part in parts]
    top = jnp.maximum(jnp.maximum(tops[0], tops[1]), jnp.maximum(tops[2], tops[3]))
    fades = [jnp.exp(value - top) for value in tops]
    accum = in_pairs([fade * part[:, :width] for fade, part in zip(fades, parts)])
    summed = in_pairs([fade * value for fade, value in zip(fades, sums)])
    rout = accum / summed
    rout_ref[...] = rout
    rlse_ref[...] = top + jnp.log(summed)
    mempre = one_ref[rows:, :] + dot(rout.astype(LOW), weight(7))
    mempre_ref[...] = mempre
    memtwo = norm(mempre, row(small_ref, rows_of, "gain", 1), row(small_ref, rows_of, "shift", 1))
    memlow = memtwo.astype(LOW)
    wk = dot(memlow, weight(9)).astype(LOW)
    wv = dot(memlow, weight(10)).astype(LOW)
    wkv_ref[:, :width] = wk
    wkv_ref[:, width:] = wv
    probs = write_probs(wk, wq_ref[...]).reshape(HEADS * PAD, rows)
    wlow = dot_tn(probs.astype(LOW), spread_heads(wv)).astype(LOW)
    wlow_ref[...] = wlow
    seqpre = one_ref[:rows, :] + dot(wlow, weight(11))
    seqpre_ref[...] = seqpre
    seqtwo = norm(seqpre, row(small_ref, rows_of, "gain", 2), row(small_ref, rows_of, "shift", 2))
    two_ref[:rows, :] = seqtwo
    two_ref[rows:, :] = memtwo
    two = two_ref[...]
    x = two.astype(LOW)
    x_ref[...] = x
    feed = two + row(small_ref, rows_of, "shift", 4)
    for part in range(rows_of["sizes"][1]):
        u = dot(x, weight(("up", part))) + row(small_ref, rows_of, "bias", part)
        feed = feed + dot(gelu_parts(u)[0].astype(LOW), weight("down", part))
    feedpre_ref[...] = feed
    z_ref[...] = norm(feed, row(small_ref, rows_of, "gain", 3), row(small_ref, rows_of, "shift", 3))
    if not last:
        project(z_ref[...], weight, q_ref, kv_ref, kvmem_ref)


def feed_back_kernel(
    share, weight, put, rows_of, grad_ref, feedpre_ref, x_ref, seqpre_ref, wlow_ref, wq_ref, wkv_ref, one_ref,
    small_ref,
    gbias_ref, gsmall_ref, mem_ref, seq_ref, part_ref,
):
    rows, width = wq_ref.shape
    full = grad_ref.shape[0]
    balance = jnp.where(lax.broadcasted_iota(jnp.int32, (full, 1), 0) < rows, 1.0, share)
    grad = grad_ref[...]
    feed, by_unit = norm_back(feedpre_ref[...], row(small_ref, rows_of, "gain", 3), grad)
    gsmall_ref[0:1, :] = total(by_unit * balance)
    gsmall_ref[1:2, :] = total(grad * balance)
    low = feed.astype(LOW)
    low_share = (low.astype(F32) * balance).astype(LOW)
    gsmall_ref[2:3, :] = total(low_share.astype(F32))
    x = x_ref[...]
    two = feed
    high, parts, _ = rows_of["sizes"]
    order = bias_order(width, high, parts)
    piece = width // parts
    for part in range(parts):
        u = dot(x, weight(("up", part))) + row(small_ref, rows_of, "bias", part)
        value, slope = gelu_parts(u)
        put(("down", part), dot_tn(value.astype(LOW), low_share))
        pre = (dot_nt(low, weight("down", part)) * slope).astype(LOW)
        pre_share = (pre.astype(F32) * balance).astype(LOW)
        line = dot(total(pre_share.astype(F32)).astype(LOW), order)
        for j in range(parts):
            gbias_ref[j : j + 1, part * piece : (part + 1) * piece] = line[:, j * piece : (j + 1) * piece]
        put(("up", part), dot_tn(x, pre_share))
        two = two + dot_nt(pre, weight(("up", part)))
    mem_ref[...] = two[rows:]
    grad = two[:rows]
    seq, by_unit = norm_back(seqpre_ref[...], row(small_ref, rows_of, "gain", 2), grad)
    gsmall_ref[3:4, :] = total(by_unit)
    gsmall_ref[4:5, :] = total(grad)
    low = seq.astype(LOW)
    put(11, dot_tn(wlow_ref[...], low))
    out_low = dot_nt(low, weight(11)).astype(LOW)
    wk, wv = wkv_ref[:, :width], wkv_ref[:, width:]
    wq = wq_ref[...]
    probs = write_probs(wk, wq)
    prob_grad = dot_nt(spread_heads(wv), out_low).reshape(probs.shape)
    delta = jnp.sum(probs * prob_grad, 1, keepdims=True)
    score_grad = (probs * (prob_grad - delta)).reshape(HEADS * PAD, rows).astype(LOW)
    wq_low = (dot_tn(score_grad, spread_heads(wk)) * SCALE).astype(LOW)
    part_ref[:PAD, :] = (fold_heads(dot(score_grad, wq)) * SCALE).astype(LOW)
    part_ref[PAD:, :] = fold_heads(dot(probs.reshape(HEADS * PAD, rows).astype(LOW), out_low)).astype(LOW)
    put(8, dot_tn(one_ref[:rows, :].astype(LOW), wq_low))
    seq_ref[...] = seq + dot_nt(wq_low, weight(8))


def read_back_kernel(
    share, weight, put, rows_of, own_ref, core_ref, chip_ref, both_ref, mem_ref, seq_ref, two_ref, mempre_ref, rout_ref, rlse_ref, rq_ref, rkv_ref, one_ref,
    pre_ref, small_ref,
    gsmall_ref, memgrad_ref, seqjoint_ref, part_ref,
):
    rows, width = seq_ref.shape
    summed = in_pairs([part[...].astype(F32) for part in (own_ref, core_ref, chip_ref, both_ref)])
    k_low = summed[:PAD].astype(LOW)
    v_low = summed[PAD:].astype(LOW)
    mem_low = two_ref[rows:, :].astype(LOW)
    put(9, dot_tn(mem_low, k_low) * share)
    put(10, dot_tn(mem_low, v_low) * share)
    grad = mem_ref[...] + dot_nt(k_low, weight(9)) + dot_nt(v_low, weight(10))
    mem, by_unit = norm_back(mempre_ref[...], row(small_ref, rows_of, "gain", 1), grad)
    gsmall_ref[0:1, :] = total(by_unit) * share
    gsmall_ref[1:2, :] = total(grad) * share
    low = mem.astype(LOW)
    rout = rout_ref[...]
    put(7, dot_tn(rout.astype(LOW), low) * share)
    out_low = dot_nt(low, weight(7)).astype(LOW)
    memgrad_ref[...] = mem
    rk, rv = rkv_ref[:, :width], rkv_ref[:, width:]
    rq = spread_heads(rq_ref[...] * jnp.asarray(SCALE, LOW))
    out_wide = spread_heads(out_low)
    delta = jnp.sum(spread_heads(out_low.astype(F32) * rout), -1, keepdims=True)
    mask = head_mask(width)
    lse = jnp.max(jnp.where(mask, rlse_ref[...][None], -BIG).reshape(HEADS * PAD, width), -1, keepdims=True)
    probs = jnp.exp(dot_nt(rq, rk) - lse)
    score_grad = (probs * (dot_nt(out_wide, rv) - delta)).astype(LOW)
    part_ref[...] = (fold_heads(dot(score_grad, rk)) * SCALE).astype(LOW)
    key_low = dot_tn(score_grad, rq).astype(LOW)
    value_low = dot_tn(probs.astype(LOW), out_wide).astype(LOW)
    seq_low = one_ref[:rows, :].astype(LOW)
    put(5, dot_tn(seq_low, key_low))
    put(6, dot_tn(seq_low, value_low))
    grad = seq_ref[...] + dot_nt(key_low, weight(5)) + dot_nt(value_low, weight(6))
    joint, by_unit = norm_back(pre_ref[:rows, :], row(small_ref, rows_of, "gain", 0), grad)
    gsmall_ref[2:3, :] = total(by_unit)
    gsmall_ref[3:4, :] = total(grad)
    seqjoint_ref[...] = joint


def attend_back_kernel(
    share, weight, put, rows_of, z_ref, part_ref, corepart_ref, chippart_ref, bothpart_ref, memgrad_ref, seqjoint_ref, one_ref, pre_ref, att_ref, lse_ref,
    q_ref, own_ref, core_ref, chip_ref, both_ref, kvmem_ref, sega_ref, segb_ref, segc_ref, segd_ref, segq_ref, small_ref,
    gsmall_ref, joint_ref, qgrad_ref, keep_ref, pass_ref, send_ref,
    keys_ref, bound_ref, out_ref, kvgrad_ref,
):
    rows, width = seqjoint_ref.shape
    full = att_ref.shape[0]
    place_keys(keys_ref, own_ref, core_ref, chip_ref, both_ref, kvmem_ref)
    place_bounds(bound_ref, (sega_ref, segb_ref, segc_ref, segd_ref), segq_ref[...])
    parts = (part_ref, corepart_ref, chippart_ref, bothpart_ref)
    q_low = in_pairs([part[...].astype(F32) for part in parts]).astype(LOW)
    put(4, dot_tn(one_ref[rows:, :].astype(LOW), q_low) * share)
    grad = memgrad_ref[...] + dot_nt(q_low, weight(4))
    mem, by_unit = norm_back(pre_ref[rows:, :], row(small_ref, rows_of, "gain", 0), grad)
    gsmall_ref[0:1, :] = total(by_unit) * share
    gsmall_ref[1:2, :] = total(grad) * share
    joint_ref[:rows, :] = seqjoint_ref[...]
    joint_ref[rows:, :] = mem
    low = joint_ref[...].astype(LOW)
    balance = jnp.where(lax.broadcasted_iota(jnp.int32, (full, 1), 0) < rows, 1.0, share)
    put(3, dot_tn(att_ref[...], (low.astype(F32) * balance).astype(LOW)))
    out_ref[...] = dot_nt(low, weight(3)).astype(LOW)

    def pair(step, carry):
        lanes = pl.ds(pl.multiple_of(step * 128, 128), 128)
        more = pl.ds(pl.multiple_of(width + step * 128, 128), 128)
        query = q_ref[:, lanes] * jnp.asarray(SCALE, LOW)
        out = out_ref[:, lanes]
        low_balance = jnp.concatenate([balance, balance], 0)
        product = (out.astype(F32) * att_ref[:, lanes].astype(F32)).T
        delta = jnp.concatenate([total(product[:HEAD]), total(product[HEAD:])], 1)
        query = two_heads(query)
        out = two_heads(out)
        keys = keys_ref[:, lanes]
        values = keys_ref[:, more]
        scores = jnp.minimum(dot_nt(keys, query), bound_ref[...])
        probs = jnp.exp(scores - lse_ref[pl.ds(step, 1), :])
        prob_grad = dot_nt(values, out)
        score_grad = (probs * (prob_grad - delta)).astype(LOW)
        qgrad_ref[:, lanes] = (pick_heads(dot_tn(keys, score_grad)) * SCALE).astype(LOW)
        query_share = (query.astype(F32) * low_balance).astype(LOW)
        out_share = (out.astype(F32) * low_balance).astype(LOW)
        kvgrad_ref[:, lanes] = dot(score_grad, query_share).astype(LOW)
        kvgrad_ref[:, more] = dot(probs.astype(LOW), out_share).astype(LOW)
        return carry

    lax.fori_loop(0, width // 128, pair, 0)
    z_low = z_ref[...].astype(LOW)
    put(0, dot_tn(z_low, (qgrad_ref[...].astype(F32) * balance).astype(LOW)))
    me = lax.axis_index("blk")
    for goal, place, other in ((keep_ref, 0, 0), (pass_ref, 0, 2), (send_ref, 0, 1), (send_ref, rows, 3)):
        rest = pl.ds(pl.multiple_of((me ^ other) * rows, rows), rows)
        goal[place : place + rows, :] = kvgrad_ref[rest, :]
    pass_ref[rows:, :] = kvgrad_ref[4 * rows :, :]
    send_ref[2 * rows :, :] = kvgrad_ref[4 * rows :, :]


def input_back_kernel(
    share, weight, put, rows_of, z_ref, joint_ref, qgrad_ref, keep_ref, near_ref, sent_ref, got_ref, *rest
):
    *small_refs, zgrad_ref, kvgrad_ref = rest
    full, width = z_ref.shape
    rows = full - PAD
    balance = jnp.where(lax.broadcasted_iota(jnp.int32, (full, 1), 0) < rows, 1.0, share)
    low = z_ref[...].astype(LOW)
    mine = keep_ref[...].astype(F32) + near_ref[:rows, :].astype(F32)
    kvgrad_ref[:rows, :] = (mine + got_ref[:rows, :].astype(F32)).astype(LOW)
    kvgrad_ref[rows:, :] = (sent_ref[rows:, :].astype(F32) + got_ref[rows:, :].astype(F32)).astype(LOW)
    grads = (qgrad_ref[...], kvgrad_ref[:, :width], kvgrad_ref[:, width:])
    grad = joint_ref[...]
    for part, value in enumerate(grads):
        if part > 0:
            put(part, dot_tn(low, (value.astype(F32) * balance).astype(LOW)))
        grad = grad + dot_nt(value, weight(part))
    zgrad_ref[...] = grad
    if small_refs:
        layers = [[ref[...] for ref in small_refs[k : k + 4]] for k in range(0, len(small_refs), 4)]
        lines = []
        for one, two, three, _ in layers:
            lines.extend([two[2:3] + three[0:1], two[0:1], one[3:4], one[0:1]])
        for one, two, three, _ in layers:
            lines.extend([two[3:4] + three[1:2], two[1:2], one[4:5], one[1:2], one[2:3]])
        lines.extend(bias for _, _, _, bias in layers)
        lines.append(grad[rows:] * share)
        small = jnp.concatenate(lines, 0)
        small = jnp.concatenate([small, jnp.zeros((width - small.shape[0], width), F32)], 0)
        put("small", small.T)


class Order:
    def __init__(self, stages):
        self.stages = stages

    def place(self, number):
        result = 0
        for stage in self.stages:
            result = 2 * result + ((number >> bit_place(stage)) & 1)
        return result

    def mine(self):
        result = 0
        for axis, bit in self.stages:
            result = 2 * result + ((lax.axis_index(axis) >> bit) & 1)
        return result


def call(kernel, name, cost, ins, outs, weights, scratch=(), grads=(), rows_of=None):
    sources, operands, begins = [], [], []
    for source, _, _ in weights.values():
        if not any(source is other for other in sources):
            sources.append(source)
            begins.append(len(operands))
            operands.extend(source[0])
    places, slots = {}, 0
    for key, (source, slot, count) in weights.items():
        which = [source is other for other in sources].index(True)
        places[key] = (which, slot, slots, count)
        slots = slots + count
    high, width = operands[0].shape[2:]
    shards = width // high
    groups, goals, aliases, shapes, made_shapes, grad_places = [], [], {}, [], [], {}
    for number, (keys, order, count, total_slots, into) in enumerate(grads):
        place = 0
        for key in keys:
            grad_places[key] = (number, place, count if key == "down" else 1)
            place += grad_places[key][2]
        halves = 1 if order is None else 2
        arrays, start = into or ((), 0)
        for half, array in enumerate(arrays):
            aliases[len(ins) + len(operands) + len(goals)] = len(shapes) + half
            goals.append(array)
        groups.append((order, halves, len(shapes), start))
        shapes += [jax.ShapeDtypeStruct((shards // halves, total_slots or place, high, width), LOW)] * halves
        made_shapes += [pltpu.VMEM((shards, place, high, width), LOW), pltpu.SemaphoreType.DMA((place, 2))]

    def body(*refs):
        in_refs, refs = refs[: len(ins)], refs[len(ins) :]
        operand_refs, refs = refs[: len(operands)], refs[len(operands) + len(goals) :]
        grad_refs, refs = refs[: len(shapes)], refs[len(shapes) :]
        refs, made_refs = refs[: len(refs) - len(made_shapes)], refs[len(refs) - len(made_shapes) :]
        *refs, buffer, sems = refs
        core = lax.axis_index("blk") % 2
        copies = {}
        for turn, (key, (which, slot, place, count)) in enumerate(places.items()):
            copies[key] = []
            arrays = len(sources[which][0])
            piece = shards // arrays
            for part in range(arrays):
                copy = pltpu.make_async_copy(
                    operand_refs[begins[which] + part].at[:, pl.ds(slot, count)],
                    buffer.at[pl.ds(part * piece, piece), pl.ds(place, count)],
                    sems.at[turn, part],
                )
                copy.start()
                copies[key].append(copy)
        arrived = set()
        offsets = [None if order is None else order.mine() for _, order in sources]
        goal_offsets = [None if order is None else order.mine() for order, _, _, _ in groups]

        def weight(key, part=None):
            if key not in arrived:
                for copy in copies[key]:
                    copy.wait()
                arrived.add(key)
            which, _, place, count = places[key]
            order = sources[which][1]
            span = range(shards) if part is None else range(part * (shards // count), (part + 1) * (shards // count))
            pieces = []
            for shard in span:
                if order is None:
                    at = shard
                else:
                    at = ((shard % 2) ^ core) * (shards // 2) + (order.place(shard) ^ offsets[which])
                pieces.extend(buffer[at, place + slot] for slot in range(count))
            return jnp.concatenate(pieces, 0)

        out = []

        def put(key, grad):
            low = grad.astype(LOW)
            down = isinstance(key, tuple) and key[0] == "down"
            number, slot, count = grad_places["down" if down else key]
            order, halves, begin, start = groups[number]
            made, made_sems = made_refs[2 * number], made_refs[2 * number + 1]
            first = key[1] * (shards // count) if down else 0
            for block in range(low.shape[0] // high):
                shard, inner = first + block // count, block % count
                at = shard
                if order is not None:
                    at = ((shard % 2) ^ core) * (shards // 2) + (order.place(shard) ^ goal_offsets[number])
                made[at, slot + inner] = low[block * high : (block + 1) * high]
            if not down or key[1] == count - 1:
                piece = shards // halves
                for half in range(halves):
                    copy = pltpu.make_async_copy(
                        made.at[pl.ds(half * piece, piece), pl.ds(slot, count)],
                        grad_refs[begin + half].at[:, pl.ds(start + slot, count)],
                        made_sems.at[slot, half],
                    )
                    copy.start()
                    out.append(copy)

        kernel(weight, put, rows_of, *in_refs, *refs)
        for copy in out:
            copy.wait()

    inside, anywhere = pl.BlockSpec(memory_space=pltpu.VMEM), pl.BlockSpec(memory_space=pl.ANY)
    results = pl.pallas_call(
        body,
        out_shape=shapes + [jax.ShapeDtypeStruct(shape, kind) for shape, kind in outs],
        in_specs=[inside] * len(ins) + [anywhere] * (len(operands) + len(goals)),
        out_specs=[anywhere] * len(shapes) + [inside] * len(outs),
        scratch_shapes=list(scratch)
        + [pltpu.VMEM((shards, slots, high, width), LOW), pltpu.SemaphoreType.DMA((len(weights), 2))]
        + made_shapes,
        input_output_aliases=aliases,
        compiler_params=pltpu.CompilerParams(vmem_limit_bytes=VMEM_LIMIT),
        cost_estimate=pl.CostEstimate(flops=int(cost * 3.3e8), bytes_accessed=0, transcendentals=0),
        name=name,
    )(*ins, *operands, *goals)
    made = [results[begin : begin + halves] for _, halves, begin, _ in groups]
    return made + list(results[len(shapes) :])


def flipped(value, bit):
    size = lax.axis_size("blk")
    return lax.ppermute(value, "blk", [(source, source ^ bit) for source in range(size)])


def quartet(value):
    chip = flipped(value, 2)
    return [value, flipped(value, 1), chip, flipped(chip, 1)]


def bits_of(axis):
    return lax.axis_size(axis).bit_length() - 1


def bit_place(stage):
    axis, bit = stage
    return bit if axis == "blk" else bits_of("blk") + bit


def swapped(value, stage):
    axis, bit = stage
    return lax.ppermute(value, axis, [(source, source ^ (1 << bit)) for source in range(lax.axis_size(axis))])


def fence(*arrays):
    return list(lax.optimization_barrier(tuple(arrays)))


class Gathering:
    def __init__(self, groups):
        self.groups = groups
        self.held = [shard[None] for shard, _, _ in groups]
        self.got, self.turn = {}, 0

    def begin(self):
        done = {}
        for number, (_, stages, first) in enumerate(self.groups):
            if first <= self.turn < first + len(stages) and stages[self.turn - first] is not None:
                self.got[number] = swapped(self.held[number], stages[self.turn - first])
                if self.turn - first + 1 == len(stages) and stages[-1] == ("blk", 0):
                    done[number] = ((self.held[number], self.got.pop(number)), Order([s for s in stages[-2::-1] if s]))
        return done

    def split(self, number, slots, stages):
        held, (shard, done, _) = self.held[number], self.groups[number]
        parts = (held[:, :slots], held[:, slots:])
        for place, part, more in zip((number, len(self.groups)), parts, stages):
            self.groups[place : place + 1] = [(shard, done + more, self.turn - len(done))]
            self.held[place : place + 1] = [part]

    def end(self, *others):
        numbers = list(self.got)
        bundle = fence(*self.got.values(), *others)
        for number, value in zip(numbers, bundle):
            self.held[number] = jnp.concatenate([self.held[number], value])
        self.got = {}
        self.turn += 1
        return bundle[len(numbers) :]


def joined(values):
    return values[0] if len(values) == 1 else jnp.concatenate(values, 1)


class Scattering:
    def __init__(self, arrays, stages):
        self.keeps = [keep for keep, _ in arrays]
        self.sends = [send for _, send in arrays]
        self.stages = list(stages)
        self.gots, self.result = None, None

    def begin(self):
        stage = self.stages.pop(0)
        self.gots = [swapped(send, stage) for send in self.sends]

    def end(self):
        sums = [keep.astype(F32) + got.astype(F32) for keep, got in zip(self.keeps, self.gots)]
        self.gots = None
        if not self.stages:
            self.result = joined(sums)[0]
            return
        half = sums[0].shape[0] // 2
        self.keeps = [joined([value[:half] for value in sums]).astype(LOW)]
        self.sends = [joined([value[half:] for value in sums]).astype(LOW)]


class Background:
    def __init__(self):
        self.sums, self.running, self.staying = {}, [], set()

    def add(self, name, arrays, stages):
        self.sums[name] = Scattering(arrays, stages)

    def begin(self, *names):
        self.staying = {name[1:] for name in names if name[0] == "~"}
        for name in names:
            short = name.rstrip("+")
            if short in self.sums:
                self.sums[short].begin()
                self.running.append(short)
                if short != name:
                    self.staying.add(short)

    def end(self, *others):
        ending = [self.sums[name] for name in self.running if name not in self.staying]
        self.running = [name for name in self.running if name in self.staying]
        self.staying = set()
        gots = fence(*[got for run in ending for got in run.gots], *others)
        for run in ending:
            run.gots, gots = gots[: len(run.gots)], gots[len(run.gots) :]
            run.end()
        return gots


def local(
    tokens, segments, memory_init, attn_weights, ffn_in, ffn_out, ffn_bias, norm_gain, norm_shift, out_grad, memory_cot
):
    layers, count, rows, width = attn_weights.shape
    hidden = ffn_in.shape[2]
    per = hidden // width
    everyone = lax.axis_size("dp") * lax.axis_size("blk")
    direct = rows == 16
    core_bit, chip_bits = ("blk", 0), [("blk", bit) for bit in range(1, bits_of("blk"))]
    line_bits, near_bit = [("dp", bit) for bit in reversed(range(1, bits_of("dp")))], [("dp", 0)]

    small = [
        norm_gain.reshape(-1, rows), norm_shift.reshape(-1, rows), ffn_bias.reshape(-1, rows), memory_init
    ]
    starts = [sum(part.shape[0] for part in small[:k]) for k in range(5)]
    gain_rows, shift_rows = norm_gain.shape[1], norm_shift.shape[1]
    small = jnp.concatenate(small, 0).T.astype(LOW)
    small = jnp.pad(small, ((0, 0), (0, width - small.shape[1])))[None]

    def rows_of(index):
        return dict(
            gain=starts[0] + index * gain_rows,
            shift=starts[1] + index * shift_rows,
            bias=64 + index * per,
            memory=starts[3],
            sizes=(rows, per, starts[2]),
        )

    seg_low = segments.astype(LOW)

    def lowered(attn, up, down):
        up = up.astype(LOW).reshape(layers, rows, per, width).transpose(0, 2, 1, 3)
        return attn, up, down.astype(LOW).reshape(layers, per, rows, width)

    attn_low, up_low, down_low = lowered(attn_weights, ffn_in, ffn_out)
    early, middle, late = (0, 1, 2), (3, 8, 4, 5, 6), (7, 9, 10, 11)
    table = {}

    def listed(source, index, keys):
        place = 0
        for key in keys:
            size = per if key == "down" else 1
            table[index, key] = (source, place, size)
            place += size

    ups = tuple(("up", part) for part in range(per))
    if direct:

        def picked(index, keys):
            return [attn_low[index, key][None].astype(LOW) for key in keys]

        far, line = line_bits[:1], line_bits[1:]
        last = [core_bit]
        pause = [None]
        gathering = Gathering(
            [
                (jnp.concatenate(picked(0, early) + [small]), far + line + chip_bits + near_bit + last, 0),
                (jnp.concatenate(picked(0, middle)), far + line + near_bit + chip_bits + last, 0),
            ]
        )
        gathering.begin()
        attn_weights, ffn_in, ffn_out, seg_low = gathering.end(attn_weights, ffn_in, ffn_out, seg_low)
        attn_low, up_low, down_low = lowered(attn_weights, ffn_in, ffn_out)
        gathering.groups += [
            (
                jnp.concatenate(picked(0, late) + [up_low[0, :1]]),
                far + line + near_bit + chip_bits + last,
                2,
            ),
            (
                jnp.concatenate([down_low[0], up_low[0, 1:2]]),
                chip_bits + far + line + pause + near_bit + last,
                1,
            ),
            (
                jnp.concatenate([up_low[0, 2:]] + picked(1, early)),
                near_bit + chip_bits + pause + far + line + last,
                1,
            ),
            (jnp.concatenate(picked(1, middle)), far + line + chip_bits + near_bit + last, 4),
            (jnp.concatenate(picked(1, late) + [up_low[1], down_low[1]]), far + line, 6),
        ]
        gathering.held += [shard[None] for shard, _, _ in gathering.groups[2:]]
        gathering.begin()
        seg_all = gathering.end(*quartet(seg_low))
        for turn in range(2, 4):
            gathering.begin()
            gathering.end()
        found = gathering.begin()
        listed(found[0], 0, early + ("small",))
        listed(found[1], 0, middle)
    else:
        packed = jnp.concatenate(
            [attn_low.astype(LOW).reshape(-1, rows, width), up_low.reshape(-1, rows, width), small, down_low.reshape(-1, rows, width)]
        )
        whole = lax.all_gather(packed, ALL)
        split = layers * (count + per) + 1
        square = whole[:, :split].transpose(1, 0, 2, 3).reshape(split, -1, 16, width)
        downs = whole[:, split:].reshape(everyone, layers, per * rows, width).transpose(1, 0, 2, 3)
        downs = downs.reshape(layers, -1, per, 16, width).transpose(0, 2, 1, 3, 4).reshape(layers * per, -1, 16, width)
        source = ((jnp.concatenate([square, downs]).transpose(1, 0, 2, 3),), None)
        for index in range(layers):
            for key in range(count):
                table[index, key] = (source, index * count + key, 1)
            for part in range(per):
                table[index, ("up", part)] = (source, layers * count + index * per + part, 1)
            table[index, "down"] = (source, split + index * per, per)
        table[0, "small"] = (source, split - 1, 1)

    def attn(index, *keys):
        return {key: table[index, key] for key in keys}

    def feed(index):
        return attn(index, *ups, "down")

    length = tokens.shape[1]
    full = length + PAD
    size = lax.axis_size("blk")
    share = 1.0 / size
    me = lax.axis_index("blk")
    seg = segments[0].astype(F32)
    seg_all = seg_all if direct else quartet(seg_low)
    seg_row = jnp.concatenate([seg, jnp.full((PAD,), -1.0, F32)])
    seg_queries = jnp.concatenate([seg_row, seg_row]).reshape(1, -1)
    every = size * length + PAD
    keys_scratch = pltpu.VMEM((every, 2 * width), LOW)
    bound_scratch = pltpu.VMEM((every, 2 * full), F32)
    projected = [((full, width), LOW), ((length, 2 * width), LOW), ((PAD, 2 * width), LOW)]

    smalls, z, q, own, kvmem = call(
        first_kernel,
        "first",
        4,
        [tokens[0]],
        [((128, width), F32), ((full, width), F32)] + projected,
        attn(0, *early, "small"),
        rows_of=rows_of(0),
    )
    kept = []
    for index in range(layers):
        core = flipped(own, 1)
        chip = flipped(own, 2)
        both = flipped(chip, 1)
        if direct:
            core, chip, both = gathering.end(core, chip, both)
            if index > 0:
                gathering.split(6, len(late) + 2, [chip_bits + near_bit + [core_bit], near_bit + chip_bits + [core_bit]])
            found = gathering.begin()
            if index > 0:
                listed(found[5], index, middle)
        att, lse, pre, first, rq, rkv, wq, part = call(
            attend_kernel,
            f"attend_{index}",
            13,
            [z, q, own, core, chip, both, kvmem, *seg_all, seg_queries, smalls],
            [
                ((full, width), LOW), ((width // 128, 2 * full), F32), ((full, width), F32), ((full, width), F32),
                ((PAD, width), LOW),
                ((length, 2 * width), LOW), ((length, width), LOW), ((PAD, width + 128), F32),
            ],
            attn(index, 3, 8, 4, 5, 6),
            [keys_scratch, bound_scratch],
            rows_of=rows_of(index),
        )
        if direct and index > 0:
            (part,) = gathering.end(part)
            gathering.begin()
        parts = quartet(part)
        if direct and index > 0:
            parts = gathering.end(*parts)
            found = gathering.begin()
            listed(found[6], 1, late + ups[:2])
            listed(found[7], 1, ups[2:] + ("down",))
        if direct and index == 0:
            parts = gathering.end(*parts)
            found = gathering.begin()
            listed(found[2], 0, late + ups[:1])
            listed(found[3], 0, ("down",) + ups[1:2])
            listed(found[4], 0, ups[2:])
            for key in early:
                table[1, key] = (found[4], per - 2 + key, 1)
        last = index + 1 == layers
        results = call(
            functools.partial(finish_kernel, last),
            f"finish_{index}",
            10,
            [first, *parts, wq, smalls],
            [((full, width), F32)]
            + ([] if last else projected)
            + [
                ((PAD, width), F32), ((PAD, width), F32), ((PAD, width), F32), ((full, width), F32),
                ((PAD, 2 * width), LOW), ((length, width), LOW), ((length, width), F32), ((full, width), LOW),
                ((full, width), F32),
            ],
            attn(index, 7, 9, 10, 11) | feed(index) | ({} if last else attn(index + 1, *early)),
            rows_of=rows_of(index),
        )
        rout, rlse, mempre, second, wkv, wlow, seqpre, x, feedpre = results[-9:]
        kept.append(
            dict(
                z=z, q=q, own=own, kvmem=kvmem, core=core, chip=chip, both=both, att=att, lse=lse, pre=pre, first=first,
                rq=rq, rkv=rkv, wq=wq, rout=rout, rlse=rlse, mempre=mempre, second=second, wkv=wkv, wlow=wlow,
                seqpre=seqpre, x=x, feedpre=feedpre,
            )
        )
        z = results[0]
        if not last:
            q, own, kvmem = results[1:4]
            if direct:
                q, own, kvmem = gathering.end(q, own, kvmem)
                gathering.begin()
    final = z
    grad = jnp.concatenate(
        [out_grad[0].astype(F32), jnp.pad(memory_cot[0].astype(F32), ((0, PAD - MEM), (0, 0)))]
    )
    background = Background()
    y, x, upward = near_bit, chip_bits, line_bits[::-1]
    orders = {
        "up_1": y + upward + x,
        "up_0": y + upward + x,
        "down_1": upward[:1] + y + upward[1:] + x,
        "down_0": upward[:1] + y + upward[1:] + x,
        "first_1": y + upward + x,
        "second_1": x + upward[:1] + y + upward[1:],
        "second_0": upward[:1] + y + x + upward[1:],
    }

    def order_of(name):
        return orders.get(name, y + x + upward)

    def group(name, keys, slots=None, into=None):
        if not direct:
            return (keys, None, per, None, None)
        return (keys, Order(order_of(name)), per, slots, into)

    group_keys = [ups, ("down",), (11, 8), (9, 10, 7, 5, 6), (4, 3, 0), (1, 2)]
    made = [None] * layers
    for index in reversed(range(layers)):
        k = kept[index]
        names = {name: f"{name}_{index}" for name in ("up", "down", "first", "second")}
        end_name = names["second"] if index > 0 else "last"
        plan = iter(PLAN[index])

        def start(name, arrays):
            if direct:
                background.add(name, [arrays], [core_bit] + order_of(name))

        grads_up, grads_down, grads_first, gbias, small_one, mem, seq, part = call(
            functools.partial(feed_back_kernel, share),
            f"feed_back_{index}",
            11,
            [grad, k["feedpre"], k["x"], k["seqpre"], k["wlow"], k["wq"], k["wkv"], k["first"], smalls],
            [
                ((per, width), F32),
                ((5, width), F32), ((PAD, width), F32), ((length, width), F32), ((2 * PAD, width), LOW),
            ],
            feed(index) | attn(index, 11, 8),
            grads=[
                group(names["up"], group_keys[0]),
                group(names["down"], group_keys[1]),
                group(names["first"], group_keys[2], 7),
            ],
            rows_of=rows_of(index),
        )
        halves = len(grads_up)
        part, mem, seq, *both = background.end(part, mem, seq, *grads_up, *grads_down)
        grads_up, grads_down = both[:halves], both[halves:]
        start(names["up"], grads_up)
        start(names["down"], grads_down)
        if index + 1 < layers:
            start(*waiting)
        background.begin(*next(plan))
        parts = background.end(*quartet(part))
        background.begin(*next(plan))
        grads_read, small_two, mem, seq, part = call(
            functools.partial(read_back_kernel, share),
            f"read_back_{index}",
            4,
            [*parts, mem, seq, k["second"], k["mempre"], k["rout"], k["rlse"], k["rq"], k["rkv"],
             k["first"], k["pre"], smalls],
            [((4, width), F32), ((PAD, width), F32), ((length, width), F32), ((PAD, width), LOW)],
            attn(index, 9, 10, 7, 5, 6),
            grads=[group(names["first"], group_keys[3], 7, (grads_first, 2))],
            rows_of=rows_of(index),
        )
        count_read = len(grads_read)
        mem, seq, *rest = background.end(mem, seq, *grads_read, *quartet(part))
        grads_read, parts = rest[:count_read], rest[count_read:]
        start(names["first"], grads_read)
        background.begin(*next(plan))
        grads_attend, small_three, joint, qgrad, keep, pass_on, send = call(
            functools.partial(attend_back_kernel, share),
            f"attend_back_{index}",
            14,
            [k["z"], *parts, mem, seq, k["first"], k["pre"], k["att"], k["lse"], k["q"], k["own"], k["core"], k["chip"],
             k["both"], k["kvmem"], *seg_all, seg_queries, smalls],
            [((2, width), F32), ((full, width), F32), ((full, width), LOW),
             ((length, 2 * width), LOW), ((length + PAD, 2 * width), LOW), ((2 * length + PAD, 2 * width), LOW)],
            attn(index, 4, 3),
            [keys_scratch, bound_scratch, pltpu.VMEM((full, width), LOW), keys_scratch],
            grads=[group(names["second"], group_keys[4], 5 if index > 0 else 3)],
            rows_of=rows_of(index),
        )
        pass_on, send, *grads_attend = background.end(pass_on, send, *grads_attend)
        background.begin(*next(plan))
        near = flipped(send, 1)
        theirs = (pass_on.astype(F32) + near[length:].astype(F32)).astype(LOW)
        got = flipped(theirs, 2)
        got, theirs = background.end(got, theirs)
        background.begin(*next(plan))
        made[index] = dict(small=[small_one, small_two, small_three], bias=gbias)
        tiny = sum([m["small"] + [m["bias"]] for m in made], []) if index == 0 else []
        grads_last, grad = call(
            functools.partial(input_back_kernel, share),
            f"input_back_{index}",
            3,
            [k["z"], joint, qgrad, keep, near, theirs, got] + tiny,
            [((full, width), F32)],
            attn(index, 0, 1, 2),
            [pltpu.VMEM((full, 2 * width), LOW)],
            grads=[
                group(
                    end_name,
                    group_keys[5] + (("small",) if tiny else ()),
                    *((5, (grads_attend, 3)) if index > 0 else ()),
                )
            ],
            rows_of=rows_of(index),
        )
        waiting = (end_name, grads_last)
        made[index]["grads"] = (grads_up, grads_down, grads_first, grads_read, grads_attend, grads_last)

    mine = [{} for _ in range(layers)]
    if direct:
        start("last", grads_last)
        start("second_0", grads_attend)
        background.begin(*next(plan))
        background.end()
        for moves in plan:
            background.begin(*moves)
            background.end()
        for index in range(layers):
            wanted = [f"{name}_{index}" for name in ("up", "down", "first", "second")] + (["last"] if index == 0 else [])
            results = [background.sums[name].result for name in wanted]
            keys = [group_keys[0], group_keys[1], group_keys[2] + group_keys[3], group_keys[4]]
            if index > 0:
                keys[3] = keys[3] + group_keys[5]
            else:
                keys.append(group_keys[5] + ("small",))
            for result, held in zip(results, keys):
                place = 0
                for key in held:
                    number = per if key == "down" else 1
                    mine[index][key] = result[place : place + number].reshape(number * rows, width)
                    place += number
    else:
        outgoing, order = [], []
        for index, m in enumerate(made):
            held = sum(group_keys, ()) + (("small",) if index == 0 else ())
            stack = jnp.concatenate([part[0] for part in m["grads"]], 1).transpose(1, 0, 2, 3)
            place = 0
            for key in held:
                if key == "down":
                    downs = stack[place : place + per].transpose(1, 0, 2, 3).reshape(everyone, per, rows, width)
                    outgoing.append(downs.transpose(1, 0, 2, 3).reshape(per, width, width))
                    order.extend((index, ("down", part)) for part in range(per))
                    place += per
                else:
                    outgoing.append(stack[place].reshape(1, width, width))
                    order.append((index, key))
                    place += 1
        result = lax.psum_scatter(jnp.concatenate(outgoing), ALL, scatter_dimension=1, tiled=True).astype(F32)
        for place, (index, key) in enumerate(order):
            mine[index][key] = result[place]
        for m in mine:
            m["down"] = jnp.concatenate([m["down", part] for part in range(per)])
    back = mine[0]["small"].T
    return (
        final[:length].astype(LOW)[None],
        final[length : length + MEM][None],
        grad[:length][None],
        back[starts[3] : starts[4]],
        jnp.stack([jnp.stack([m[key] for key in range(count)]) for m in mine]),
        jnp.stack([jnp.concatenate([m["up", part] for part in range(per)], -1) for m in mine]),
        jnp.stack([m["down"] for m in mine]),
        back[starts[2] : starts[3]].reshape(ffn_bias.shape),
        back[starts[0] : starts[1]].reshape(norm_gain.shape),
        back[starts[1] : starts[2]].reshape(norm_shift.shape),
    )


def solution(mesh):
    in_specs = (
        P("dp", "blk", None),
        P("dp", "blk"),
        P(None, ALL),
        P(None, None, ALL, None),
        P(None, ALL, None),
        P(None, ALL, None),
        P(None, ALL),
        P(None, None, ALL),
        P(None, None, ALL),
        P("dp", "blk", None),
        P("dp", None, None),
    )
    out_specs = (
        P("dp", "blk", None),
        P("dp", None, None),
        P("dp", "blk", None),
        P(None, ALL),
        P(None, None, ALL, None),
        P(None, ALL, None),
        P(None, ALL, None),
        P(None, ALL),
        P(None, None, ALL),
        P(None, None, ALL),
    )
    return jax.shard_map(local, mesh=mesh, in_specs=in_specs, out_specs=out_specs, check_vma=False)
```

```python
import functools

import jax
import jax.numpy as jnp
from jax import lax
from jax.experimental import pallas as pl
from jax.experimental.pallas import tpu as pltpu
from jax.sharding import PartitionSpec as P

HEADS = 8
HEAD = 64
MEM = 20
PAD = 32
NEG = -1000000000.0
BIG = 3.0e38
EPS = 1e-05
SCALE = HEAD**-0.5
ALL = ("dp", "blk")
LOW = jnp.bfloat16
F32 = jnp.float32
VMEM_LIMIT = 20 * 1024 * 1024
PLAN = {
    1: [
        ("up_1", "down_1"),
        ("up_1", "down_1"),
        ("up_1", "down_1", "first_1"),
        ("up_1", "down_1", "first_1"),
        ("up_1", "down_1", "first_1"),
    ],
    0: [
        ("up_0", "down_0", "second_1"),
        ("up_0", "down_0"),
        ("up_0", "down_0", "first_0", "second_1"),
        ("up_0", "down_0", "first_0", "second_1", "second_0"),
        ("first_0", "second_0", "up_0", "first_1", "second_1"),
        ("last", "down_0"),
        ("last", "second_0", "first_0", "second_1", "first_1"),
        ("last", "first_0"),
    ],
}


def dot(a, b):
    return jnp.dot(a, b, preferred_element_type=F32)


def dot_nt(a, b):
    return lax.dot_general(a, b, (((1,), (1,)), ((), ())), preferred_element_type=F32)


def dot_tn(a, b):
    return lax.dot_general(a, b, (((0,), (0,)), ((), ())), preferred_element_type=F32)


def hat(x):
    center = x - jnp.mean(x, -1, keepdims=True)
    spread = jnp.mean(center * center, -1, keepdims=True)
    inv = lax.rsqrt(spread + EPS)
    return center * inv, inv


def norm(x, gain, shift):
    return hat(x)[0] * gain + shift


def norm_back(x, gain, grad):
    unit, inv = hat(x)
    scaled = grad * gain
    mean_one = jnp.mean(scaled, -1, keepdims=True)
    mean_two = jnp.mean(scaled * unit, -1, keepdims=True)
    return inv * (scaled - mean_one - unit * mean_two), grad * unit


def row(small_ref, rows_of, name, which):
    place = rows_of[name] + which
    return small_ref[place : place + 1, :]


def total(x):
    return jnp.sum(x, 0, keepdims=True)


def gelu_parts(u):
    k = 0.7978845608028654
    t = jnp.tanh(k * (u + 0.044715 * u * u * u))
    half = 0.5 * (1.0 + t)
    slope = half + 0.5 * u * (1.0 - t * t) * (k * (1.0 + 0.134145 * u * u))
    return u * half, slope


def head_mask(width):
    lanes = lax.broadcasted_iota(jnp.int32, (HEADS, 1, width), 2) // HEAD
    return lanes == lax.broadcasted_iota(jnp.int32, (HEADS, 1, width), 0)


def spread_heads(x):
    rows, width = x.shape
    full = jnp.where(head_mask(width), x.astype(F32)[None], 0.0)
    return full.reshape(HEADS * rows, width).astype(x.dtype)


def fold_heads(x):
    rows, width = x.shape
    full = x.reshape(HEADS, rows // HEADS, width)
    return jnp.sum(jnp.where(head_mask(width), full, 0.0), 0)


def two_heads(x):
    first = lax.broadcasted_iota(jnp.int32, x.shape, 1) < HEAD
    zero = jnp.zeros_like(x)
    return jnp.concatenate([jnp.where(first, x, zero), jnp.where(first, zero, x)], 0)


def pick_heads(x):
    width, rows = x.shape
    mine = (lax.broadcasted_iota(jnp.int32, x.shape, 0) < HEAD) == (
        lax.broadcasted_iota(jnp.int32, x.shape, 1) < rows // 2
    )
    both = jnp.where(mine, x, 0.0).T
    return both[: rows // 2] + both[rows // 2 :]


def place_bounds(bound_ref, seg_ref, seg_queries):
    parts, rows = seg_ref.shape
    me = lax.axis_index("blk")
    for other in range(parts):
        numbers = jnp.broadcast_to(seg_ref[other : other + 1, :], (128, rows)).T[:, 0:1]
        allowed = (numbers == seg_queries) | (seg_queries == -1.0)
        place = pl.ds(pl.multiple_of((me ^ other) * rows, rows), rows)
        bound_ref[place, :] = jnp.where(allowed, BIG, NEG)
    memory = lax.broadcasted_iota(jnp.int32, (PAD, seg_queries.shape[1]), 0) < MEM
    bound_ref[4 * rows :, :] = jnp.where(memory, BIG, NEG)


def place_keys(keys_ref, own_ref, core_ref, chip_ref, both_ref, memory_ref):
    rows = core_ref.shape[0]
    me = lax.axis_index("blk")
    pieces = ((me, own_ref), (me ^ 1, core_ref), (me ^ 2, chip_ref), (me ^ 3, both_ref))
    for place, piece in pieces:
        keys_ref[pl.ds(pl.multiple_of(place * rows, rows), rows), :] = piece[0:rows, :]
    keys_ref[4 * rows :, :] = memory_ref[...]


def project(z, weight, q_ref, kv_ref, kvmem_ref):
    low = z.astype(LOW)
    rows, width = kv_ref.shape[0], low.shape[1]
    for part in (1, 2):
        lanes = pl.ds((part - 1) * width, width)
        value = dot(low, weight(part)).astype(LOW)
        kv_ref[:, lanes] = value[:rows]
        kvmem_ref[:, lanes] = value[rows:]
    q_ref[...] = dot(low, weight(0)).astype(LOW)


def bias_order(width, high, per):
    lanes = lax.broadcasted_iota(jnp.int32, (width, width), 0)
    shard, inner = lanes // (per * high), lanes % (per * high)
    goal = inner // high * (width // per) + shard * high + inner % high
    return (goal == lax.broadcasted_iota(jnp.int32, (width, width), 1)).astype(LOW)


def first_kernel(weight, put, rows_of, tokens_ref, small_ref, z_ref, q_ref, kv_ref, kvmem_ref, *seg_refs):
    rows = tokens_ref.shape[0]
    columns = weight("small")
    if seg_refs:
        seg_ref, number_ref = seg_refs
        number_ref[...] = columns[:, 128:256].astype(F32)
        high, size = rows_of["sizes"][0], lax.axis_size("blk")
        for other in range(size):
            shard = lax.axis_index("dp") * size + (lax.axis_index("blk") ^ other)
            numbers = number_ref[pl.ds(pl.multiple_of(shard * high, high), high), :]
            for line in range(rows // 128):
                seg_ref[other : other + 1, line * 128 : (line + 1) * 128] = numbers[line : line + 1]
    columns = columns[:, :128]
    small = columns.astype(F32).T
    width = small.shape[1]
    small_ref[...] = small
    high, per, start = rows_of["sizes"]
    order = bias_order(width, high, per)
    for layer in range((rows_of["memory"] - start) // per):
        lines = small[start + layer * per : start + (layer + 1) * per].astype(LOW)
        piece = width // per
        for part in range(per):
            line = jnp.concatenate([lines[j : j + 1, part * piece : (part + 1) * piece] for j in range(per)], 1)
            place = 64 + layer * per + part
            small_ref[place : place + 1, :] = dot_nt(line, order)
    z_ref[:rows, :] = tokens_ref[...].astype(F32)
    start = rows_of["memory"]
    z_ref[rows : rows + MEM, :] = small[start : start + MEM]
    z_ref[rows + MEM :, :] = jnp.zeros((PAD - MEM, small.shape[1]), F32)
    project(z_ref[...], weight, q_ref, kv_ref, kvmem_ref)


def attend_kernel(
    weight, put, rows_of, z_ref, q_ref, own_ref, core_ref, chip_ref, both_ref, kvmem_ref, segs_ref, segq_ref, small_ref,
    att_ref, lse_ref, pre_ref, one_ref, rq_ref, rkv_ref, wq_ref, part_ref,
    keys_ref, bound_ref,
):
    rows = core_ref.shape[0]
    width = z_ref.shape[1]
    place_keys(keys_ref, own_ref, core_ref, chip_ref, both_ref, kvmem_ref)
    place_bounds(bound_ref, segs_ref, segq_ref[...])

    def pair(step, carry):
        lanes = pl.ds(pl.multiple_of(step * 128, 128), 128)
        more = pl.ds(pl.multiple_of(width + step * 128, 128), 128)
        query = two_heads(q_ref[:, lanes]) * jnp.asarray(SCALE, LOW)
        keys = keys_ref[:, lanes]
        values = keys_ref[:, more]
        scores = jnp.minimum(dot_nt(keys, query), bound_ref[...])
        top = jnp.max(scores, 0, keepdims=True)
        expo = jnp.exp(scores - top)
        summed = jnp.sum(expo, 0, keepdims=True)
        att_ref[:, lanes] = pick_heads(dot_tn(values, expo.astype(LOW)) * (1.0 / summed)).astype(LOW)
        lse_ref[pl.ds(step, 1), :] = top + jnp.log(summed)
        return carry

    lax.fori_loop(0, width // 128, pair, 0)
    pre = z_ref[...] + dot(att_ref[...], weight(3))
    pre_ref[...] = pre
    one = norm(pre, row(small_ref, rows_of, "gain", 0), row(small_ref, rows_of, "shift", 0))
    one_ref[...] = one
    low = one.astype(LOW)
    seq_low, mem_low = low[:rows], low[rows:]
    wq_ref[...] = dot(seq_low, weight(8)).astype(LOW)
    rq = dot(mem_low, weight(4)).astype(LOW)
    rk = dot(seq_low, weight(5)).astype(LOW)
    rv = dot(seq_low, weight(6)).astype(LOW)
    rq_ref[...] = rq
    rkv_ref[:, :width] = rk
    rkv_ref[:, width:] = rv
    scores = dot_nt(spread_heads(rq * jnp.asarray(SCALE, LOW)), rk)
    top = jnp.max(scores, -1, keepdims=True)
    expo = jnp.exp(scores - top)
    summed = jnp.sum(expo, -1, keepdims=True)
    part_ref[:, :width] = fold_heads(dot(expo.astype(LOW), rv))
    lanes = lax.broadcasted_iota(jnp.int32, (HEADS, PAD, 128), 2)
    heads = lax.broadcasted_iota(jnp.int32, (HEADS, PAD, 128), 0)
    top = jnp.where(lanes == heads, top.reshape(HEADS, PAD, 1), 0.0)
    summed = jnp.where(lanes == heads + HEADS, summed.reshape(HEADS, PAD, 1), 0.0)
    part_ref[:, width:] = jnp.sum(top + summed, 0)


def in_pairs(values):
    own, core, chip, both = values
    return (own + core) + (chip + both)


def widened(stats, start, width):
    lanes = lax.broadcasted_iota(jnp.int32, (128, width), 0)
    heads = lax.broadcasted_iota(jnp.int32, (128, width), 1) // HEAD + start
    return jnp.dot(
        stats, (lanes == heads).astype(F32), precision=lax.Precision.HIGHEST, preferred_element_type=F32
    )


def write_probs(wk, wq):
    scores = dot_nt(spread_heads(wk * jnp.asarray(SCALE, LOW)), wq)
    scores = scores.reshape(HEADS, PAD, scores.shape[1])
    real = lax.broadcasted_iota(jnp.int32, scores.shape, 1) < MEM
    scores = jnp.where(real, scores, NEG)
    expo = jnp.exp(scores - jnp.max(scores, 1, keepdims=True))
    return expo * (1.0 / jnp.sum(expo, 1, keepdims=True))


def finish_kernel(
    last, weight, put, rows_of, one_ref, own_ref, core_ref, chip_ref, both_ref, wq_ref, small_ref, *rest
):
    if last:
        (z_ref, rout_ref, rlse_ref, mempre_ref, two_ref, wkv_ref, wlow_ref, seqpre_ref, x_ref, feedpre_ref) = rest
    else:
        (z_ref, q_ref, kv_ref, kvmem_ref,
         rout_ref, rlse_ref, mempre_ref, two_ref, wkv_ref, wlow_ref, seqpre_ref, x_ref, feedpre_ref) = rest
    rows, width = wq_ref.shape
    parts = (own_ref, core_ref, chip_ref, both_ref)
    tops = [widened(part[:, width:], 0, width) for part in parts]
    sums = [widened(part[:, width:], HEADS, width) for part in parts]
    top = jnp.maximum(jnp.maximum(tops[0], tops[1]), jnp.maximum(tops[2], tops[3]))
    fades = [jnp.exp(value - top) for value in tops]
    accum = in_pairs([fade * part[:, :width] for fade, part in zip(fades, parts)])
    summed = in_pairs([fade * value for fade, value in zip(fades, sums)])
    rout = accum / summed
    rout_ref[...] = rout
    rlse_ref[...] = top + jnp.log(summed)
    mempre = one_ref[rows:, :] + dot(rout.astype(LOW), weight(7))
    mempre_ref[...] = mempre
    memtwo = norm(mempre, row(small_ref, rows_of, "gain", 1), row(small_ref, rows_of, "shift", 1))
    memlow = memtwo.astype(LOW)
    wk = dot(memlow, weight(9)).astype(LOW)
    wv = dot(memlow, weight(10)).astype(LOW)
    wkv_ref[:, :width] = wk
    wkv_ref[:, width:] = wv
    probs = write_probs(wk, wq_ref[...]).reshape(HEADS * PAD, rows)
    wlow = dot_tn(probs.astype(LOW), spread_heads(wv)).astype(LOW)
    wlow_ref[...] = wlow
    seqpre = one_ref[:rows, :] + dot(wlow, weight(11))
    seqpre_ref[...] = seqpre
    seqtwo = norm(seqpre, row(small_ref, rows_of, "gain", 2), row(small_ref, rows_of, "shift", 2))
    two_ref[:rows, :] = seqtwo
    two_ref[rows:, :] = memtwo
    two = two_ref[...]
    x = two.astype(LOW)
    x_ref[...] = x
    feed = two + row(small_ref, rows_of, "shift", 4)
    for part in range(rows_of["sizes"][1]):
        u = dot(x, weight(("up", part))) + row(small_ref, rows_of, "bias", part)
        feed = feed + dot(gelu_parts(u)[0].astype(LOW), weight("down", part))
    feedpre_ref[...] = feed
    z_ref[...] = norm(feed, row(small_ref, rows_of, "gain", 3), row(small_ref, rows_of, "shift", 3))
    if not last:
        project(z_ref[...], weight, q_ref, kv_ref, kvmem_ref)


def feed_back_kernel(
    share, weight, put, rows_of, grad_ref, feedpre_ref, x_ref, seqpre_ref, wlow_ref, wq_ref, wkv_ref, one_ref,
    small_ref,
    gbias_ref, gsmall_ref, mem_ref, seq_ref, part_ref,
):
    rows, width = wq_ref.shape
    full = grad_ref.shape[0]
    balance = jnp.where(lax.broadcasted_iota(jnp.int32, (full, 1), 0) < rows, 1.0, share)
    grad = grad_ref[...]
    feed, by_unit = norm_back(feedpre_ref[...], row(small_ref, rows_of, "gain", 3), grad)
    gsmall_ref[0:1, :] = total(by_unit * balance)
    gsmall_ref[1:2, :] = total(grad * balance)
    low = feed.astype(LOW)
    low_share = (low.astype(F32) * balance).astype(LOW)
    gsmall_ref[2:3, :] = total(low_share.astype(F32))
    x = x_ref[...]
    two = feed
    high, parts, _ = rows_of["sizes"]
    order = bias_order(width, high, parts)
    piece = width // parts
    for part in range(parts):
        u = dot(x, weight(("up", part))) + row(small_ref, rows_of, "bias", part)
        value, slope = gelu_parts(u)
        put(("down", part), dot_tn(value.astype(LOW), low_share))
        pre = (dot_nt(low, weight("down", part)) * slope).astype(LOW)
        pre_share = (pre.astype(F32) * balance).astype(LOW)
        line = dot(total(pre_share.astype(F32)).astype(LOW), order)
        for j in range(parts):
            gbias_ref[j : j + 1, part * piece : (part + 1) * piece] = line[:, j * piece : (j + 1) * piece]
        put(("up", part), dot_tn(x, pre_share))
        two = two + dot_nt(pre, weight(("up", part)))
    mem_ref[...] = two[rows:]
    grad = two[:rows]
    seq, by_unit = norm_back(seqpre_ref[...], row(small_ref, rows_of, "gain", 2), grad)
    gsmall_ref[3:4, :] = total(by_unit)
    gsmall_ref[4:5, :] = total(grad)
    low = seq.astype(LOW)
    put(11, dot_tn(wlow_ref[...], low))
    out_low = dot_nt(low, weight(11)).astype(LOW)
    wk, wv = wkv_ref[:, :width], wkv_ref[:, width:]
    wq = wq_ref[...]
    probs = write_probs(wk, wq)
    prob_grad = dot_nt(spread_heads(wv), out_low).reshape(probs.shape)
    delta = jnp.sum(probs * prob_grad, 1, keepdims=True)
    score_grad = (probs * (prob_grad - delta)).reshape(HEADS * PAD, rows).astype(LOW)
    wq_low = (dot_tn(score_grad, spread_heads(wk)) * SCALE).astype(LOW)
    part_ref[:PAD, :] = (fold_heads(dot(score_grad, wq)) * SCALE).astype(LOW)
    part_ref[PAD:, :] = fold_heads(dot(probs.reshape(HEADS * PAD, rows).astype(LOW), out_low)).astype(LOW)
    put(8, dot_tn(one_ref[:rows, :].astype(LOW), wq_low))
    seq_ref[...] = seq + dot_nt(wq_low, weight(8))


def read_back_kernel(
    share, weight, put, rows_of, own_ref, core_ref, chip_ref, both_ref, mem_ref, seq_ref, two_ref, mempre_ref, rout_ref, rlse_ref, rq_ref, rkv_ref, one_ref,
    pre_ref, small_ref,
    gsmall_ref, memgrad_ref, seqjoint_ref, part_ref,
):
    rows, width = seq_ref.shape
    summed = in_pairs([part[...].astype(F32) for part in (own_ref, core_ref, chip_ref, both_ref)])
    k_low = summed[:PAD].astype(LOW)
    v_low = summed[PAD:].astype(LOW)
    mem_low = two_ref[rows:, :].astype(LOW)
    put(9, dot_tn(mem_low, k_low) * share)
    put(10, dot_tn(mem_low, v_low) * share)
    grad = mem_ref[...] + dot_nt(k_low, weight(9)) + dot_nt(v_low, weight(10))
    mem, by_unit = norm_back(mempre_ref[...], row(small_ref, rows_of, "gain", 1), grad)
    gsmall_ref[0:1, :] = total(by_unit) * share
    gsmall_ref[1:2, :] = total(grad) * share
    low = mem.astype(LOW)
    rout = rout_ref[...]
    put(7, dot_tn(rout.astype(LOW), low) * share)
    out_low = dot_nt(low, weight(7)).astype(LOW)
    memgrad_ref[...] = mem
    rk, rv = rkv_ref[:, :width], rkv_ref[:, width:]
    rq = spread_heads(rq_ref[...] * jnp.asarray(SCALE, LOW))
    out_wide = spread_heads(out_low)
    delta = jnp.sum(spread_heads(out_low.astype(F32) * rout), -1, keepdims=True)
    mask = head_mask(width)
    lse = jnp.max(jnp.where(mask, rlse_ref[...][None], -BIG).reshape(HEADS * PAD, width), -1, keepdims=True)
    probs = jnp.exp(dot_nt(rq, rk) - lse)
    score_grad = (probs * (dot_nt(out_wide, rv) - delta)).astype(LOW)
    part_ref[...] = (fold_heads(dot(score_grad, rk)) * SCALE).astype(LOW)
    key_low = dot_tn(score_grad, rq).astype(LOW)
    value_low = dot_tn(probs.astype(LOW), out_wide).astype(LOW)
    seq_low = one_ref[:rows, :].astype(LOW)
    put(5, dot_tn(seq_low, key_low))
    put(6, dot_tn(seq_low, value_low))
    grad = seq_ref[...] + dot_nt(key_low, weight(5)) + dot_nt(value_low, weight(6))
    joint, by_unit = norm_back(pre_ref[:rows, :], row(small_ref, rows_of, "gain", 0), grad)
    gsmall_ref[2:3, :] = total(by_unit)
    gsmall_ref[3:4, :] = total(grad)
    seqjoint_ref[...] = joint


def attend_back_kernel(
    share, weight, put, rows_of, z_ref, part_ref, corepart_ref, chippart_ref, bothpart_ref, memgrad_ref, seqjoint_ref, one_ref, pre_ref, att_ref, lse_ref,
    q_ref, own_ref, core_ref, chip_ref, both_ref, kvmem_ref, segs_ref, segq_ref, small_ref,
    gsmall_ref, joint_ref, qgrad_ref, keep_ref, pass_ref, send_ref,
    keys_ref, bound_ref, out_ref, kvgrad_ref,
):
    rows, width = seqjoint_ref.shape
    full = att_ref.shape[0]
    place_keys(keys_ref, own_ref, core_ref, chip_ref, both_ref, kvmem_ref)
    place_bounds(bound_ref, segs_ref, segq_ref[...])
    parts = (part_ref, corepart_ref, chippart_ref, bothpart_ref)
    q_low = in_pairs([part[...].astype(F32) for part in parts]).astype(LOW)
    put(4, dot_tn(one_ref[rows:, :].astype(LOW), q_low) * share)
    grad = memgrad_ref[...] + dot_nt(q_low, weight(4))
    mem, by_unit = norm_back(pre_ref[rows:, :], row(small_ref, rows_of, "gain", 0), grad)
    gsmall_ref[0:1, :] = total(by_unit) * share
    gsmall_ref[1:2, :] = total(grad) * share
    joint_ref[:rows, :] = seqjoint_ref[...]
    joint_ref[rows:, :] = mem
    low = joint_ref[...].astype(LOW)
    balance = jnp.where(lax.broadcasted_iota(jnp.int32, (full, 1), 0) < rows, 1.0, share)
    put(3, dot_tn(att_ref[...], (low.astype(F32) * balance).astype(LOW)))
    out_ref[...] = dot_nt(low, weight(3)).astype(LOW)

    def pair(step, carry):
        lanes = pl.ds(pl.multiple_of(step * 128, 128), 128)
        more = pl.ds(pl.multiple_of(width + step * 128, 128), 128)
        query = q_ref[:, lanes] * jnp.asarray(SCALE, LOW)
        out = out_ref[:, lanes]
        low_balance = jnp.concatenate([balance, balance], 0)
        product = (out.astype(F32) * att_ref[:, lanes].astype(F32)).T
        delta = jnp.concatenate([total(product[:HEAD]), total(product[HEAD:])], 1)
        query = two_heads(query)
        out = two_heads(out)
        keys = keys_ref[:, lanes]
        values = keys_ref[:, more]
        scores = jnp.minimum(dot_nt(keys, query), bound_ref[...])
        probs = jnp.exp(scores - lse_ref[pl.ds(step, 1), :])
        prob_grad = dot_nt(values, out)
        score_grad = (probs * (prob_grad - delta)).astype(LOW)
        qgrad_ref[:, lanes] = (pick_heads(dot_tn(keys, score_grad)) * SCALE).astype(LOW)
        query_share = (query.astype(F32) * low_balance).astype(LOW)
        out_share = (out.astype(F32) * low_balance).astype(LOW)
        kvgrad_ref[:, lanes] = dot(score_grad, query_share).astype(LOW)
        kvgrad_ref[:, more] = dot(probs.astype(LOW), out_share).astype(LOW)
        return carry

    lax.fori_loop(0, width // 128, pair, 0)
    z_low = z_ref[...].astype(LOW)
    put(0, dot_tn(z_low, (qgrad_ref[...].astype(F32) * balance).astype(LOW)))
    me = lax.axis_index("blk")
    for goal, place, other in ((keep_ref, 0, 0), (pass_ref, 0, 2), (send_ref, 0, 1), (send_ref, rows, 3)):
        rest = pl.ds(pl.multiple_of((me ^ other) * rows, rows), rows)
        goal[place : place + rows, :] = kvgrad_ref[rest, :]
    pass_ref[rows:, :] = kvgrad_ref[4 * rows :, :]
    send_ref[2 * rows :, :] = kvgrad_ref[4 * rows :, :]


def input_back_kernel(
    share, weight, put, rows_of, z_ref, joint_ref, qgrad_ref, keep_ref, near_ref, sent_ref, got_ref, *rest
):
    *small_refs, zgrad_ref, kvgrad_ref = rest
    full, width = z_ref.shape
    rows = full - PAD
    balance = jnp.where(lax.broadcasted_iota(jnp.int32, (full, 1), 0) < rows, 1.0, share)
    low = z_ref[...].astype(LOW)
    mine = keep_ref[...].astype(F32) + near_ref[:rows, :].astype(F32)
    kvgrad_ref[:rows, :] = (mine + got_ref[:rows, :].astype(F32)).astype(LOW)
    kvgrad_ref[rows:, :] = (sent_ref[rows:, :].astype(F32) + got_ref[rows:, :].astype(F32)).astype(LOW)
    grads = (qgrad_ref[...], kvgrad_ref[:, :width], kvgrad_ref[:, width:])
    grad = joint_ref[...]
    for part, value in enumerate(grads):
        if part > 0:
            put(part, dot_tn(low, (value.astype(F32) * balance).astype(LOW)))
        grad = grad + dot_nt(value, weight(part))
    zgrad_ref[...] = grad
    if small_refs:
        layers = [[ref[...] for ref in small_refs[k : k + 4]] for k in range(0, len(small_refs), 4)]
        lines = []
        for one, two, three, _ in layers:
            lines.extend([two[2:3] + three[0:1], two[0:1], one[3:4], one[0:1]])
        for one, two, three, _ in layers:
            lines.extend([two[3:4] + three[1:2], two[1:2], one[4:5], one[1:2], one[2:3]])
        lines.extend(bias for _, _, _, bias in layers)
        lines.append(grad[rows:] * share)
        small = jnp.concatenate(lines, 0)
        small = jnp.concatenate([small, jnp.zeros((width - small.shape[0], width), F32)], 0)
        put("small", small.T)


class Order:
    def __init__(self, stages):
        self.stages = stages

    def place(self, number):
        result = 0
        for stage in self.stages:
            result = 2 * result + ((number >> bit_place(stage)) & 1)
        return result

    def mine(self):
        result = 0
        for axis, bit in self.stages:
            result = 2 * result + ((lax.axis_index(axis) >> bit) & 1)
        return result


def call(kernel, name, cost, ins, outs, weights, scratch=(), grads=(), rows_of=None):
    sources, operands, begins = [], [], []
    for source, _, _ in weights.values():
        if not any(source is other for other in sources):
            sources.append(source)
            begins.append(len(operands))
            operands.extend(source[0])
    places, slots = {}, 0
    for key, (source, slot, count) in weights.items():
        which = [source is other for other in sources].index(True)
        places[key] = (which, slot, slots, count)
        slots = slots + count
    high, width = operands[0].shape[2:]
    shards = width // high
    groups, goals, aliases, shapes, made_shapes, grad_places = [], [], {}, [], [], {}
    for number, (keys, order, count, total_slots, into) in enumerate(grads):
        place = 0
        for key in keys:
            grad_places[key] = (number, place, count if key == "down" else 1)
            place += grad_places[key][2]
        halves = 1 if order is None else 2
        arrays, start = into or ((), 0)
        for half, array in enumerate(arrays):
            aliases[len(ins) + len(operands) + len(goals)] = len(shapes) + half
            goals.append(array)
        groups.append((order, halves, len(shapes), start))
        shapes += [jax.ShapeDtypeStruct((shards // halves, total_slots or place, high, width), LOW)] * halves
        made_shapes += [pltpu.VMEM((shards, place, high, width), LOW), pltpu.SemaphoreType.DMA((place, 2))]

    def body(*refs):
        in_refs, refs = refs[: len(ins)], refs[len(ins) :]
        operand_refs, refs = refs[: len(operands)], refs[len(operands) + len(goals) :]
        grad_refs, refs = refs[: len(shapes)], refs[len(shapes) :]
        refs, made_refs = refs[: len(refs) - len(made_shapes)], refs[len(refs) - len(made_shapes) :]
        *refs, buffer, sems = refs
        core = lax.axis_index("blk") % 2
        copies = {}
        for turn, (key, (which, slot, place, count)) in enumerate(places.items()):
            copies[key] = []
            arrays = len(sources[which][0])
            piece = shards // arrays
            for part in range(arrays):
                copy = pltpu.make_async_copy(
                    operand_refs[begins[which] + part].at[:, pl.ds(slot, count)],
                    buffer.at[pl.ds(part * piece, piece), pl.ds(place, count)],
                    sems.at[turn, part],
                )
                copy.start()
                copies[key].append(copy)
        arrived = set()
        offsets = [None if order is None else order.mine() for _, order in sources]
        goal_offsets = [None if order is None else order.mine() for order, _, _, _ in groups]

        def weight(key, part=None):
            if key not in arrived:
                for copy in copies[key]:
                    copy.wait()
                arrived.add(key)
            which, _, place, count = places[key]
            order = sources[which][1]
            span = range(shards) if part is None else range(part * (shards // count), (part + 1) * (shards // count))
            pieces = []
            for shard in span:
                if order is None:
                    at = shard
                else:
                    at = ((shard % 2) ^ core) * (shards // 2) + (order.place(shard) ^ offsets[which])
                pieces.extend(buffer[at, place + slot] for slot in range(count))
            return jnp.concatenate(pieces, 0)

        out = []

        def put(key, grad):
            low = grad.astype(LOW)
            down = isinstance(key, tuple) and key[0] == "down"
            number, slot, count = grad_places["down" if down else key]
            order, halves, begin, start = groups[number]
            made, made_sems = made_refs[2 * number], made_refs[2 * number + 1]
            first = key[1] * (shards // count) if down else 0
            for block in range(low.shape[0] // high):
                shard, inner = first + block // count, block % count
                at = shard
                if order is not None:
                    at = ((shard % 2) ^ core) * (shards // 2) + (order.place(shard) ^ goal_offsets[number])
                made[at, slot + inner] = low[block * high : (block + 1) * high]
            if not down or key[1] == count - 1:
                piece = shards // halves
                for half in range(halves):
                    copy = pltpu.make_async_copy(
                        made.at[pl.ds(half * piece, piece), pl.ds(slot, count)],
                        grad_refs[begin + half].at[:, pl.ds(start + slot, count)],
                        made_sems.at[slot, half],
                    )
                    copy.start()
                    out.append(copy)

        kernel(weight, put, rows_of, *in_refs, *refs)
        for copy in out:
            copy.wait()

    inside, anywhere = pl.BlockSpec(memory_space=pltpu.VMEM), pl.BlockSpec(memory_space=pl.ANY)
    results = pl.pallas_call(
        body,
        out_shape=shapes + [jax.ShapeDtypeStruct(shape, kind) for shape, kind in outs],
        in_specs=[inside] * len(ins) + [anywhere] * (len(operands) + len(goals)),
        out_specs=[anywhere] * len(shapes) + [inside] * len(outs),
        scratch_shapes=list(scratch)
        + [pltpu.VMEM((shards, slots, high, width), LOW), pltpu.SemaphoreType.DMA((len(weights), 2))]
        + made_shapes,
        input_output_aliases=aliases,
        compiler_params=pltpu.CompilerParams(vmem_limit_bytes=VMEM_LIMIT),
        cost_estimate=pl.CostEstimate(flops=int(cost * 3.3e8), bytes_accessed=0, transcendentals=0),
        name=name,
    )(*ins, *operands, *goals)
    made = [results[begin : begin + halves] for _, halves, begin, _ in groups]
    return made + list(results[len(shapes) :])


def flipped(value, bit):
    size = lax.axis_size("blk")
    return lax.ppermute(value, "blk", [(source, source ^ bit) for source in range(size)])


def fence(*arrays):
    return list(lax.optimization_barrier(tuple(arrays)))


def quartet(value):
    return both_chips(value, flipped(value, 2))


def both_chips(own, chip):
    return [own, flipped(own, 1), chip, flipped(chip, 1)]


def bits_of(axis):
    return lax.axis_size(axis).bit_length() - 1


def bit_place(stage):
    axis, bit = stage
    return bit if axis == "blk" else bits_of("blk") + bit


def pack_kernel(attn_ref, *refs):
    inputs, out_ref, (lines_ref, wide_ref, *held, sems) = refs[:5], refs[5], refs[6:]
    count, high, width = out_ref.shape
    origins = (attn_ref.at[0, pl.ds(0, count - 1)],) + inputs
    copies = [
        pltpu.make_async_copy(origin, goal, sems.at[place])
        for place, (origin, goal) in enumerate(zip(origins, [wide_ref] + held))
    ]
    for copy in copies:
        copy.start()
    lines_ref[...] = jnp.zeros(lines_ref.shape, F32)
    for copy in copies:
        copy.wait()
    gain_ref, shift_ref, bias_ref, memory_ref, seg_ref = held
    layers, rows, _ = gain_ref.shape
    place = layers * rows
    for layer in range(layers):
        lines_ref[layer * rows : (layer + 1) * rows, 0:high] = gain_ref[layer]
    rows = shift_ref.shape[0]
    for line in range(rows):
        for layer in range(layers):
            goal = place + layer * rows + line
            lines_ref[goal : goal + 1, 0:high] = shift_ref[line, layer : layer + 1]
    place += layers * rows
    layers, hidden = bias_ref.shape
    for layer in range(layers):
        for part in range(hidden // high):
            lines_ref[place : place + 1, 0:high] = bias_ref[layer : layer + 1, part * high : (part + 1) * high]
            place += 1
    columns = lines_ref[...].T
    lines_ref[...] = columns
    lines_ref[0:high, place : place + MEM] = memory_ref[...]
    out_ref[count - 1] = jnp.zeros((high, width), LOW)
    out_ref[count - 1, :, 0:128] = lines_ref[0:high, :].astype(LOW)
    lines_ref[...] = jnp.zeros(lines_ref.shape, F32)
    for line in range(seg_ref.shape[1] // 128):
        lines_ref[line : line + 1, :] = seg_ref[:, line * 128 : (line + 1) * 128].astype(F32)
    out_ref[count - 1, :, 128:256] = lines_ref[0:high, :].astype(LOW)
    out_ref[0 : count - 1] = wide_ref[...].astype(LOW)


def unpack_kernel(slot, sums_ref, gain_ref, shift_ref, bias_ref, memory_ref, lines_ref):
    high = sums_ref.shape[1]
    lines_ref[...] = jnp.zeros(lines_ref.shape, F32)
    lines_ref[0:high, :] = sums_ref[slot, :, 0:128]
    lines = lines_ref[...].T
    place = 0
    for ref in (gain_ref, shift_ref):
        layers, rows, _ = ref.shape
        for layer in range(layers):
            ref[layer] = lines[place : place + rows, 0:high]
            place += rows
    layers, hidden = bias_ref.shape
    for layer in range(layers):
        for part in range(hidden // high):
            bias_ref[layer : layer + 1, part * high : (part + 1) * high] = lines[place : place + 1, 0:high]
            place += 1
    memory_ref[...] = lines[place : place + MEM, 0:high]


def flat(stages):
    return [bit for stage in stages for bit in (stage if isinstance(stage[0], tuple) else (stage,))]


def swapped(value, stage):
    if isinstance(stage[0], tuple):
        mask = sum(1 << bit_place(bit) for bit in stage)
        everyone = lax.axis_size("dp") * lax.axis_size("blk")
        return lax.ppermute(value, ALL, [(source, source ^ mask) for source in range(everyone)])
    axis, bit = stage
    return lax.ppermute(value, axis, [(source, source ^ (1 << bit)) for source in range(lax.axis_size(axis))])


class Gathering:
    def __init__(self, groups):
        self.groups = groups
        self.held = [shard[None] for shard, _, _ in groups]
        self.got, self.turn = {}, 0

    def begin(self):
        done = {}
        for number, (_, stages, first) in enumerate(self.groups):
            if first <= self.turn < first + len(stages) and stages[self.turn - first] is not None:
                self.got[number] = swapped(self.held[number], stages[self.turn - first])
                if self.turn - first + 1 == len(stages) and stages[-1] == ("blk", 0):
                    done[number] = ((self.held[number], self.got.pop(number)), Order([s for s in stages[-2::-1] if s]))
        return done

    def split(self, number, slots, stages):
        held, (shard, done, _) = self.held[number], self.groups[number]
        parts = (held[:, :slots], held[:, slots:])
        for place, part, more in zip((number, len(self.groups)), parts, stages):
            self.groups[place : place + 1] = [(shard, done + more, self.turn - len(done))]
            self.held[place : place + 1] = [part]

    def end(self, *others):
        numbers = list(self.got)
        bundle = fence(*self.got.values(), *others)
        for number, value in zip(numbers, bundle):
            self.held[number] = jnp.concatenate([self.held[number], value])
        self.got = {}
        self.turn += 1
        return bundle[len(numbers) :]


def joined(values):
    return values[0] if len(values) == 1 else jnp.concatenate(values, 1)


class Scattering:
    def __init__(self, arrays, stages):
        self.keeps = [keep for keep, _ in arrays]
        self.sends = [[send for _, send in arrays]]
        self.stages = list(stages)
        self.gots, self.result = None, None

    def begin(self):
        bits = flat([self.stages.pop(0)])
        self.gots = []
        for piece, sends in enumerate(self.sends):
            some = tuple(bit for place, bit in enumerate(bits) if (piece + 1) >> (len(bits) - 1 - place) & 1)
            self.gots.extend(swapped(send, some if len(some) > 1 else some[0]) for send in sends)

    def end(self):
        sums = []
        for place, keep in enumerate(self.keeps):
            value = keep.astype(F32)
            for got in self.gots[place :: len(self.keeps)]:
                value = value + got.astype(F32)
            sums.append(value)
        self.gots = None
        if not self.stages:
            self.result = joined(sums)[0]
            return
        pieces = 2 ** len(flat(self.stages[:1]))
        size = sums[0].shape[0] // pieces
        parts = [joined([value[k * size : (k + 1) * size] for value in sums]).astype(LOW) for k in range(pieces)]
        self.keeps, self.sends = parts[:1], [[part] for part in parts[1:]]


class Background:
    def __init__(self):
        self.sums, self.running, self.staying = {}, [], set()

    def add(self, name, arrays, stages):
        self.sums[name] = Scattering(arrays, stages)

    def begin(self, *names):
        self.staying = {name[1:] for name in names if name[0] == "~"}
        for name in names:
            short = name.rstrip("+")
            if short in self.sums:
                self.sums[short].begin()
                self.running.append(short)
                if short != name:
                    self.staying.add(short)

    def merge(self, name, other):
        one, two = self.sums[name], self.sums[other]
        if one.stages and one.stages == two.stages:
            one.keeps = [joined(one.keeps + two.keeps)]
            one.sends = [[joined(first + second)] for first, second in zip(one.sends, two.sends)]
            two.stages = []

    def end(self, *others):
        ending = [self.sums[name] for name in self.running if name not in self.staying]
        self.running = [name for name in self.running if name in self.staying]
        self.staying = set()
        gots = fence(*[got for run in ending for got in run.gots], *others)
        for run in ending:
            run.gots, gots = gots[: len(run.gots)], gots[len(run.gots) :]
            run.end()
        return gots


def local(
    tokens, segments, memory_init, attn_weights, ffn_in, ffn_out, ffn_bias, norm_gain, norm_shift, out_grad, memory_cot
):
    layers, count, rows, width = attn_weights.shape
    hidden = ffn_in.shape[2]
    per = hidden // width
    everyone = lax.axis_size("dp") * lax.axis_size("blk")
    direct = rows == 16
    core_bit, chip_bits = ("blk", 0), [("blk", bit) for bit in range(1, bits_of("blk"))]
    line_bits, near_bit = [("dp", bit) for bit in reversed(range(1, bits_of("dp")))], [("dp", 0)]

    small = [
        norm_gain.reshape(-1, rows), norm_shift.reshape(-1, rows), ffn_bias.reshape(-1, rows), memory_init
    ]
    starts = [sum(part.shape[0] for part in small[:k]) for k in range(5)]
    gain_rows, shift_rows = norm_gain.shape[1], norm_shift.shape[1]
    small = jnp.concatenate(small, 0).T.astype(LOW)
    numbers = jnp.pad(segments.reshape(-1, 128).astype(LOW), ((0, rows - segments.size // 128), (0, 0)))
    small = jnp.concatenate([jnp.pad(small, ((0, 0), (0, 128 - small.shape[1]))), numbers], 1)
    small = jnp.pad(small, ((0, 0), (0, width - small.shape[1])))[None]

    def rows_of(index):
        return dict(
            gain=starts[0] + index * gain_rows,
            shift=starts[1] + index * shift_rows,
            bias=64 + index * per,
            memory=starts[3],
            sizes=(rows, per, starts[2]),
        )

    def lowered(attn, up, down):
        up = up.astype(LOW).reshape(layers, rows, per, width).transpose(0, 2, 1, 3)
        return attn, up, down.astype(LOW).reshape(layers, per, rows, width)

    attn_low, up_low, down_low = lowered(attn_weights, ffn_in, ffn_out)
    early, middle, late = (0, 1, 2), (3, 8, 4, 5, 6), (7, 9, 10, 11)
    table = {}

    def listed(source, index, keys):
        place = 0
        for key in keys:
            size = per if key == "down" else 1
            table[index, key] = (source, place, size)
            place += size

    ups = tuple(("up", part) for part in range(per))
    if direct:

        def picked(index, keys):
            return [attn_low[index, key][None].astype(LOW) for key in keys]

        far, line = line_bits[:1], line_bits[1:]
        last = [core_bit]
        pause = [None]
        inside, anywhere = pl.BlockSpec(memory_space=pltpu.VMEM), pl.BlockSpec(memory_space=pl.ANY)
        packed_small = (norm_gain, norm_shift.transpose(1, 0, 2), ffn_bias, memory_init.T, segments)
        first_shard = pl.pallas_call(
            pack_kernel,
            out_shape=jax.ShapeDtypeStruct((len(early) + 1, rows, width), LOW),
            in_specs=[pl.BlockSpec(memory_space=pltpu.HBM)] * 6,
            out_specs=inside,
            scratch_shapes=[pltpu.VMEM((128, 128), F32), pltpu.VMEM((len(early), rows, width), F32)]
            + [
                pltpu.VMEM(part.shape, part.dtype)
                for part in packed_small
            ]
            + [pltpu.SemaphoreType.DMA((6,))],
            compiler_params=pltpu.CompilerParams(vmem_limit_bytes=3 * VMEM_LIMIT),
            name="pack",
        )(attn_weights, *packed_small)
        gathering = Gathering(
            [
                (first_shard, far + line + chip_bits + near_bit + last, 0),
                (jnp.concatenate(picked(0, middle)), far + line + near_bit + chip_bits + last, 0),
            ]
        )
        gathering.begin()
        attn_weights, ffn_in, ffn_out = gathering.end(attn_weights, ffn_in, ffn_out)
        attn_low, up_low, down_low = lowered(attn_weights, ffn_in, ffn_out)
        gathering.groups += [
            (
                jnp.concatenate(picked(0, late) + [up_low[0, :1]]),
                far + line + near_bit + chip_bits + last,
                2,
            ),
            (
                jnp.concatenate([down_low[0], up_low[0, 1:2]]),
                chip_bits + far + line + pause + near_bit + last,
                1,
            ),
            (
                jnp.concatenate([up_low[0, 2:]] + picked(1, early)),
                far + chip_bits + pause + near_bit + line + last,
                1,
            ),
            (jnp.concatenate(picked(1, middle)), far + line + chip_bits + near_bit + last, 4),
            (jnp.concatenate(picked(1, late) + [up_low[1]]), far + line, 6),
            (down_low[1], near_bit + far + chip_bits + line + last, 6),
        ]
        gathering.held += [shard[None] for shard, _, _ in gathering.groups[2:]]
        gathering.begin()
        gathering.end()
        for turn in range(2, 4):
            gathering.begin()
            gathering.end()
        found = gathering.begin()
        arrived = fence(*[source[0][1] for source in (found[0], found[1])])
        for number, got in enumerate(arrived):
            found[number] = ((found[number][0][0], got), found[number][1])
        listed(found[0], 0, early + ("small",))
        listed(found[1], 0, middle)
    else:
        packed = jnp.concatenate(
            [attn_low.astype(LOW).reshape(-1, rows, width), up_low.reshape(-1, rows, width), small, down_low.reshape(-1, rows, width)]
        )
        whole = lax.all_gather(packed, ALL)
        split = layers * (count + per) + 1
        square = whole[:, :split].transpose(1, 0, 2, 3).reshape(split, -1, 16, width)
        downs = whole[:, split:].reshape(everyone, layers, per * rows, width).transpose(1, 0, 2, 3)
        downs = downs.reshape(layers, -1, per, 16, width).transpose(0, 2, 1, 3, 4).reshape(layers * per, -1, 16, width)
        source = ((jnp.concatenate([square, downs]).transpose(1, 0, 2, 3),), None)
        for index in range(layers):
            for key in range(count):
                table[index, key] = (source, index * count + key, 1)
            for part in range(per):
                table[index, ("up", part)] = (source, layers * count + index * per + part, 1)
            table[index, "down"] = (source, split + index * per, per)
        table[0, "small"] = (source, split - 1, 1)

    def attn(index, *keys):
        return {key: table[index, key] for key in keys}

    def feed(index):
        return attn(index, *ups, "down")

    length = tokens.shape[1]
    full = length + PAD
    size = lax.axis_size("blk")
    share = 1.0 / size
    me = lax.axis_index("blk")
    seg = segments[0].astype(F32)
    seg_row = jnp.concatenate([seg, jnp.full((PAD,), -1.0, F32)])
    seg_queries = jnp.concatenate([seg_row, seg_row]).reshape(1, -1)
    every = size * length + PAD
    keys_scratch = pltpu.VMEM((every, 2 * width), LOW)
    bound_scratch = pltpu.VMEM((every, 2 * full), F32)
    projected = [((full, width), LOW), ((length, 2 * width), LOW), ((PAD, 2 * width), LOW)]

    smalls, z, q, own, kvmem, *numbers = call(
        first_kernel,
        "first",
        4,
        [tokens[0]],
        [((128, width), F32), ((full, width), F32)] + projected + ([((size, length), F32)] if direct else []),
        attn(0, *early, "small"),
        [pltpu.VMEM((width, 128), F32)] if direct else [],
        rows_of=rows_of(0),
    )
    seg_all = numbers[0] if direct else jnp.concatenate(quartet(segments.astype(LOW))).astype(F32)
    kept = []
    for index in range(layers):
        chip = flipped(own, 2)
        if direct:
            own, chip = gathering.end(own, chip)
            if index > 0:
                gathering.split(6, len(late), [chip_bits + near_bit + [core_bit], near_bit + chip_bits + [core_bit]])
            found = gathering.begin()
            if index > 0:
                listed(found[5], index, middle)
        _, core, _, both = both_chips(own, chip)
        att, lse, pre, first, rq, rkv, wq, part = call(
            attend_kernel,
            f"attend_{index}",
            13,
            [z, q, own, core, chip, both, kvmem, seg_all, seg_queries, smalls],
            [
                ((full, width), LOW), ((width // 128, 2 * full), F32), ((full, width), F32), ((full, width), F32),
                ((PAD, width), LOW),
                ((length, 2 * width), LOW), ((length, width), LOW), ((PAD, width + 128), F32),
            ],
            attn(index, 3, 8, 4, 5, 6),
            [keys_scratch, bound_scratch],
            rows_of=rows_of(index),
        )
        if direct and index > 0:
            (part,) = gathering.end(part)
            gathering.begin()
        part_chip = flipped(part, 2)
        if direct:
            part, part_chip = gathering.end(part, part_chip)
            found = gathering.begin()
            if index == 0:
                listed(found[2], 0, late + ups[:1])
                listed(found[3], 0, ("down",) + ups[1:2])
                listed(found[4], 0, ups[2:])
                for key in early:
                    table[1, key] = (found[4], per - 2 + key, 1)
            else:
                listed(found[6], 1, late)
                listed(found[7], 1, ("down",))
                listed(found[8], 1, ups)
        parts = both_chips(part, part_chip)
        last = index + 1 == layers
        results = call(
            functools.partial(finish_kernel, last),
            f"finish_{index}",
            10,
            [first, *parts, wq, smalls],
            [((full, width), F32)]
            + ([] if last else projected)
            + [
                ((PAD, width), F32), ((PAD, width), F32), ((PAD, width), F32), ((full, width), F32),
                ((PAD, 2 * width), LOW), ((length, width), LOW), ((length, width), F32), ((full, width), LOW),
                ((full, width), F32),
            ],
            attn(index, 7, 9, 10, 11) | feed(index) | ({} if last else attn(index + 1, *early)),
            rows_of=rows_of(index),
        )
        rout, rlse, mempre, second, wkv, wlow, seqpre, x, feedpre = results[-9:]
        kept.append(
            dict(
                z=z, q=q, own=own, kvmem=kvmem, core=core, chip=chip, both=both, att=att, lse=lse, pre=pre, first=first,
                rq=rq, rkv=rkv, wq=wq, rout=rout, rlse=rlse, mempre=mempre, second=second, wkv=wkv, wlow=wlow,
                seqpre=seqpre, x=x, feedpre=feedpre,
            )
        )
        z = results[0]
        if not last:
            q, own, kvmem = results[1:4]
            if direct:
                q, own, kvmem = gathering.end(q, own, kvmem)
                gathering.begin()
    final = z
    grad = jnp.concatenate(
        [out_grad[0].astype(F32), jnp.pad(memory_cot[0].astype(F32), ((0, PAD - MEM), (0, 0)))]
    )
    background = Background()
    y, x, upward = near_bit, chip_bits, line_bits[::-1]
    orders = {
        "up_1": y + upward + x,
        "up_0": y + upward + x,
        "down_1": upward[:1] + y + upward[1:] + x,
        "down_0": upward[:1] + y + upward[1:] + x,
        "first_1": y + upward + x,
        "second_1": x + upward[:1] + y + upward[1:],
        "second_0": y + x + [tuple(upward)],
        "last": [tuple(y + x), tuple(upward)],
    }

    def order_of(name):
        return orders.get(name, y + x + upward)

    def group(name, keys, slots=None, into=None):
        if not direct:
            return (keys, None, per, None, None)
        return (keys, Order(flat(order_of(name))), per, slots, into)

    group_keys = [ups + (11,), ("down", 8), (9, 10, 7, 5, 6), (4, 3, 0), (1, 2)]
    made = [None] * layers
    for index in reversed(range(layers)):
        k = kept[index]
        names = {name: f"{name}_{index}" for name in ("up", "down", "first", "second")}
        end_name = names["second"] if index > 0 else "last"
        plan = iter(PLAN[index])

        def start(name, arrays):
            if direct:
                background.add(name, [arrays], [core_bit] + order_of(name))

        grads_up, grads_down, gbias, small_one, mem, seq, part = call(
            functools.partial(feed_back_kernel, share),
            f"feed_back_{index}",
            11,
            [grad, k["feedpre"], k["x"], k["seqpre"], k["wlow"], k["wq"], k["wkv"], k["first"], smalls],
            [
                ((per, width), F32),
                ((5, width), F32), ((PAD, width), F32), ((length, width), F32), ((2 * PAD, width), LOW),
            ],
            feed(index) | attn(index, 11, 8),
            grads=[
                group(names["up"], group_keys[0]),
                group(names["down"], group_keys[1]),
            ],
            rows_of=rows_of(index),
        )
        halves = len(grads_up)
        part, mem, seq, *both = background.end(part, mem, seq, *grads_up, *grads_down)
        grads_up, grads_down = both[:halves], both[halves:]
        start(names["up"], grads_up)
        start(names["down"], grads_down)
        if index + 1 < layers:
            start(*waiting)
        background.begin(*next(plan))
        part, chip = background.end(part, flipped(part, 2))
        background.begin(*next(plan))
        parts = both_chips(part, chip)
        grads_read, small_two, mem, seq, part = call(
            functools.partial(read_back_kernel, share),
            f"read_back_{index}",
            4,
            [*parts, mem, seq, k["second"], k["mempre"], k["rout"], k["rlse"], k["rq"], k["rkv"],
             k["first"], k["pre"], smalls],
            [((4, width), F32), ((PAD, width), F32), ((length, width), F32), ((PAD, width), LOW)],
            attn(index, 9, 10, 7, 5, 6),
            grads=[group(names["first"], group_keys[2])],
            rows_of=rows_of(index),
        )
        mem, seq, part, chip, *grads_read = background.end(mem, seq, part, flipped(part, 2), *grads_read)
        start(names["first"], grads_read)
        background.begin(*next(plan))
        parts = both_chips(part, chip)
        grads_attend, small_three, joint, qgrad, keep, pass_on, send = call(
            functools.partial(attend_back_kernel, share),
            f"attend_back_{index}",
            14,
            [k["z"], *parts, mem, seq, k["first"], k["pre"], k["att"], k["lse"], k["q"], k["own"], k["core"], k["chip"],
             k["both"], k["kvmem"], seg_all, seg_queries, smalls],
            [((2, width), F32), ((full, width), F32), ((full, width), LOW),
             ((length, 2 * width), LOW), ((length + PAD, 2 * width), LOW), ((2 * length + PAD, 2 * width), LOW)],
            attn(index, 4, 3),
            [keys_scratch, bound_scratch, pltpu.VMEM((full, width), LOW), keys_scratch],
            grads=[group(names["second"], group_keys[3], 5 if index > 0 else 3)],
            rows_of=rows_of(index),
        )
        pass_on, send, *grads_attend = background.end(pass_on, send, *grads_attend)
        if index == 0:
            start(names["second"], grads_attend)
        background.begin(*next(plan))
        near = flipped(send, 1)
        theirs = (pass_on.astype(F32) + near[length:].astype(F32)).astype(LOW)
        got = flipped(theirs, 2)
        got, theirs = background.end(got, theirs)
        background.begin(*next(plan))
        made[index] = dict(small=[small_one, small_two, small_three], bias=gbias)
        tiny = sum([m["small"] + [m["bias"]] for m in made], []) if index == 0 else []
        grads_last, grad = call(
            functools.partial(input_back_kernel, share),
            f"input_back_{index}",
            3,
            [k["z"], joint, qgrad, keep, near, theirs, got] + tiny,
            [((full, width), F32)],
            attn(index, 0, 1, 2),
            [pltpu.VMEM((full, 2 * width), LOW)],
            grads=[
                group(
                    end_name,
                    group_keys[4] + (("small",) if tiny else ()),
                    *((5, (grads_attend, 3)) if index > 0 else ()),
                )
            ],
            rows_of=rows_of(index),
        )
        waiting = (end_name, grads_last)
        made[index]["grads"] = (grads_up, grads_down, grads_read, grads_attend, grads_last)

    mine = [{} for _ in range(layers)]
    if direct:
        start("last", grads_last)
        background.begin(*next(plan))
        background.end()
        for moves in plan:
            background.begin(*moves)
            background.end()
            background.merge("last", "second_0")
        for index in range(layers):
            wanted = [f"{name}_{index}" for name in ("up", "down", "first", "second")] + (["last"] if index == 0 else [])
            if index == 0:
                both = last_sums = background.sums["last"].result
                background.sums["last"].result, background.sums["second_0"].result = both[:3], both[3:]
            results = [background.sums[name].result for name in wanted]
            keys = list(group_keys[:4])
            if index > 0:
                keys[3] = keys[3] + group_keys[4]
            else:
                keys.append(group_keys[4] + ("small",))
            for result, held in zip(results, keys):
                place = 0
                for key in held:
                    number = per if key == "down" else 1
                    mine[index][key] = result[place : place + number].reshape(number * rows, width)
                    place += number
    else:
        outgoing, order = [], []
        for index, m in enumerate(made):
            held = sum(group_keys, ()) + (("small",) if index == 0 else ())
            stack = jnp.concatenate([part[0] for part in m["grads"]], 1).transpose(1, 0, 2, 3)
            place = 0
            for key in held:
                if key == "down":
                    downs = stack[place : place + per].transpose(1, 0, 2, 3).reshape(everyone, per, rows, width)
                    outgoing.append(downs.transpose(1, 0, 2, 3).reshape(per, width, width))
                    order.extend((index, ("down", part)) for part in range(per))
                    place += per
                else:
                    outgoing.append(stack[place].reshape(1, width, width))
                    order.append((index, key))
                    place += 1
        result = lax.psum_scatter(jnp.concatenate(outgoing), ALL, scatter_dimension=1, tiled=True).astype(F32)
        for place, (index, key) in enumerate(order):
            mine[index][key] = result[place]
        for m in mine:
            m["down"] = jnp.concatenate([m["down", part] for part in range(per)])
    if direct:
        small_grads = pl.pallas_call(
            functools.partial(unpack_kernel, 2),
            out_shape=[
                jax.ShapeDtypeStruct(part.shape, F32) for part in (norm_gain, norm_shift, ffn_bias, memory_init)
            ],
            in_specs=[inside],
            out_specs=[inside] * 4,
            scratch_shapes=[pltpu.VMEM((128, 128), F32)],
            compiler_params=pltpu.CompilerParams(vmem_limit_bytes=VMEM_LIMIT),
            name="unpack",
        )(last_sums)
    else:
        back = mine[0]["small"].T
        small_grads = [back[starts[k] : starts[k + 1]].reshape(part.shape) for k, part in enumerate(
            (norm_gain, norm_shift, ffn_bias, memory_init)
        )]
    return (
        final[:length].astype(LOW)[None],
        final[length : length + MEM][None],
        grad[:length][None],
        small_grads[3],
        jnp.stack([jnp.stack([m[key] for key in range(count)]) for m in mine]),
        jnp.stack([jnp.concatenate([m["up", part] for part in range(per)], -1) for m in mine]),
        jnp.stack([m["down"] for m in mine]),
        small_grads[2],
        small_grads[0],
        small_grads[1],
    )


def solution(mesh):
    in_specs = (
        P("dp", "blk", None),
        P("dp", "blk"),
        P(None, ALL),
        P(None, None, ALL, None),
        P(None, ALL, None),
        P(None, ALL, None),
        P(None, ALL),
        P(None, None, ALL),
        P(None, None, ALL),
        P("dp", "blk", None),
        P("dp", None, None),
    )
    out_specs = (
        P("dp", "blk", None),
        P("dp", None, None),
        P("dp", "blk", None),
        P(None, ALL),
        P(None, None, ALL, None),
        P(None, ALL, None),
        P(None, ALL, None),
        P(None, ALL),
        P(None, None, ALL),
        P(None, None, ALL),
    )
    return jax.shard_map(local, mesh=mesh, in_specs=in_specs, out_specs=out_specs, check_vma=False)
```

```python
import functools

import jax
import jax.numpy as jnp
from jax import lax
from jax.experimental import pallas as pl
from jax.experimental.pallas import tpu as pltpu
from jax.sharding import PartitionSpec as P

HEADS = 8
HEAD = 64
MEM = 20
PAD = 32
NEG = -1000000000.0
BIG = 3.0e38
EPS = 1e-05
SCALE = HEAD**-0.5
ALL = ("dp", "blk")
LOW = jnp.bfloat16
F32 = jnp.float32
VMEM_LIMIT = 20 * 1024 * 1024
PLAN = {
    1: [
        ("up_1", "down_1"),
        ("up_1", "down_1"),
        ("up_1", "down_1", "first_1"),
        ("up_1", "down_1", "first_1"),
        ("up_1", "down_1", "first_1"),
    ],
    0: [
        ("up_0", "down_0", "second_1"),
        ("up_0", "down_0"),
        ("up_0", "down_0", "first_0", "second_1", "first_1"),
        ("up_0", "down_0", "first_0", "second_1", "second_0"),
        ("first_0", "second_0", "up_0", "first_1", "second_1"),
        ("last", "down_0"),
        ("last", "second_0", "first_0", "second_1"),
        ("last", "first_0"),
    ],
}


def dot(a, b):
    return jnp.dot(a, b, preferred_element_type=F32)


def dot_nt(a, b):
    return lax.dot_general(a, b, (((1,), (1,)), ((), ())), preferred_element_type=F32)


def dot_tn(a, b):
    return lax.dot_general(a, b, (((0,), (0,)), ((), ())), preferred_element_type=F32)


def hat(x):
    center = x - jnp.mean(x, -1, keepdims=True)
    spread = jnp.mean(center * center, -1, keepdims=True)
    inv = lax.rsqrt(spread + EPS)
    return center * inv, inv


def norm(x, gain, shift):
    return hat(x)[0] * gain + shift


def norm_back(x, gain, grad):
    unit, inv = hat(x)
    scaled = grad * gain
    mean_one = jnp.mean(scaled, -1, keepdims=True)
    mean_two = jnp.mean(scaled * unit, -1, keepdims=True)
    return inv * (scaled - mean_one - unit * mean_two), grad * unit


def row(small_ref, rows_of, name, which):
    place = rows_of[name] + which
    return small_ref[place : place + 1, :]


def total(x):
    return jnp.sum(x, 0, keepdims=True)


def gelu_parts(u):
    k = 0.7978845608028654
    t = jnp.tanh(k * (u + 0.044715 * u * u * u))
    half = 0.5 * (1.0 + t)
    slope = half + 0.5 * u * (1.0 - t * t) * (k * (1.0 + 0.134145 * u * u))
    return u * half, slope


def head_mask(width):
    lanes = lax.broadcasted_iota(jnp.int32, (HEADS, 1, width), 2) // HEAD
    return lanes == lax.broadcasted_iota(jnp.int32, (HEADS, 1, width), 0)


def spread_heads(x):
    rows, width = x.shape
    full = jnp.where(head_mask(width), x.astype(F32)[None], 0.0)
    return full.reshape(HEADS * rows, width).astype(x.dtype)


def fold_heads(x):
    rows, width = x.shape
    full = x.reshape(HEADS, rows // HEADS, width)
    return jnp.sum(jnp.where(head_mask(width), full, 0.0), 0)


def two_heads(x):
    first = lax.broadcasted_iota(jnp.int32, x.shape, 1) < HEAD
    zero = jnp.zeros_like(x)
    return jnp.concatenate([jnp.where(first, x, zero), jnp.where(first, zero, x)], 0)


def pick_heads(x):
    width, rows = x.shape
    mine = (lax.broadcasted_iota(jnp.int32, x.shape, 0) < HEAD) == (
        lax.broadcasted_iota(jnp.int32, x.shape, 1) < rows // 2
    )
    both = jnp.where(mine, x, 0.0).T
    return both[: rows // 2] + both[rows // 2 :]


def place_bounds(bound_ref, seg_ref, seg_queries):
    parts, rows = seg_ref.shape
    me = lax.axis_index("blk")
    for other in range(parts):
        numbers = jnp.broadcast_to(seg_ref[other : other + 1, :], (128, rows)).T[:, 0:1]
        allowed = (numbers == seg_queries) | (seg_queries == -1.0)
        place = pl.ds(pl.multiple_of((me ^ other) * rows, rows), rows)
        bound_ref[place, :] = jnp.where(allowed, BIG, NEG)
    memory = lax.broadcasted_iota(jnp.int32, (PAD, seg_queries.shape[1]), 0) < MEM
    bound_ref[4 * rows :, :] = jnp.where(memory, BIG, NEG)


def place_keys(keys_ref, own_ref, core_ref, chip_ref, both_ref, memory_ref):
    rows = core_ref.shape[0]
    me = lax.axis_index("blk")
    pieces = ((me, own_ref), (me ^ 1, core_ref), (me ^ 2, chip_ref), (me ^ 3, both_ref))
    for place, piece in pieces:
        keys_ref[pl.ds(pl.multiple_of(place * rows, rows), rows), :] = piece[0:rows, :]
    keys_ref[4 * rows :, :] = memory_ref[...]


def project(z, weight, q_ref, kv_ref, kvmem_ref):
    low = z.astype(LOW)
    rows, width = kv_ref.shape[0], low.shape[1]
    for part in (1, 2):
        lanes = pl.ds((part - 1) * width, width)
        value = dot(low, weight(part)).astype(LOW)
        kv_ref[:, lanes] = value[:rows]
        kvmem_ref[:, lanes] = value[rows:]
    q_ref[...] = dot(low, weight(0)).astype(LOW)


def bias_order(width, high, per):
    lanes = lax.broadcasted_iota(jnp.int32, (width, width), 0)
    shard, inner = lanes // (per * high), lanes % (per * high)
    goal = inner // high * (width // per) + shard * high + inner % high
    return (goal == lax.broadcasted_iota(jnp.int32, (width, width), 1)).astype(LOW)


def first_kernel(weight, put, rows_of, tokens_ref, small_ref, z_ref, q_ref, kv_ref, kvmem_ref, *seg_refs):
    rows = tokens_ref.shape[0]
    columns = weight("small")
    if seg_refs:
        seg_ref, number_ref = seg_refs
        number_ref[...] = columns[:, 128:256].astype(F32)
        high, size = rows_of["sizes"][0], lax.axis_size("blk")
        for other in range(size):
            shard = lax.axis_index("dp") * size + (lax.axis_index("blk") ^ other)
            numbers = number_ref[pl.ds(pl.multiple_of(shard * high, high), high), :]
            for line in range(rows // 128):
                seg_ref[other : other + 1, line * 128 : (line + 1) * 128] = numbers[line : line + 1]
    columns = columns[:, :128]
    small = columns.astype(F32).T
    width = small.shape[1]
    small_ref[...] = small
    high, per, start = rows_of["sizes"]
    order = bias_order(width, high, per)
    for layer in range((rows_of["memory"] - start) // per):
        lines = small[start + layer * per : start + (layer + 1) * per].astype(LOW)
        piece = width // per
        for part in range(per):
            line = jnp.concatenate([lines[j : j + 1, part * piece : (part + 1) * piece] for j in range(per)], 1)
            place = 64 + layer * per + part
            small_ref[place : place + 1, :] = dot_nt(line, order)
    z_ref[:rows, :] = tokens_ref[...].astype(F32)
    start = rows_of["memory"]
    z_ref[rows : rows + MEM, :] = small[start : start + MEM]
    z_ref[rows + MEM :, :] = jnp.zeros((PAD - MEM, small.shape[1]), F32)
    project(z_ref[...], weight, q_ref, kv_ref, kvmem_ref)


def attend_kernel(
    weight, put, rows_of, z_ref, q_ref, own_ref, core_ref, chip_ref, both_ref, kvmem_ref, segs_ref, segq_ref, small_ref,
    att_ref, lse_ref, pre_ref, one_ref, rq_ref, rkv_ref, wq_ref, part_ref,
    keys_ref, bound_ref,
):
    rows = core_ref.shape[0]
    width = z_ref.shape[1]
    place_keys(keys_ref, own_ref, core_ref, chip_ref, both_ref, kvmem_ref)
    place_bounds(bound_ref, segs_ref, segq_ref[...])

    def pair(step, carry):
        lanes = pl.ds(pl.multiple_of(step * 128, 128), 128)
        more = pl.ds(pl.multiple_of(width + step * 128, 128), 128)
        query = two_heads(q_ref[:, lanes]) * jnp.asarray(SCALE, LOW)
        keys = keys_ref[:, lanes]
        values = keys_ref[:, more]
        scores = jnp.minimum(dot_nt(keys, query), bound_ref[...])
        top = jnp.max(scores, 0, keepdims=True)
        expo = jnp.exp(scores - top)
        summed = jnp.sum(expo, 0, keepdims=True)
        att_ref[:, lanes] = pick_heads(dot_tn(values, expo.astype(LOW)) * (1.0 / summed)).astype(LOW)
        lse_ref[pl.ds(step, 1), :] = top + jnp.log(summed)
        return carry

    lax.fori_loop(0, width // 128, pair, 0)
    pre = z_ref[...] + dot(att_ref[...], weight(3))
    pre_ref[...] = pre
    one = norm(pre, row(small_ref, rows_of, "gain", 0), row(small_ref, rows_of, "shift", 0))
    one_ref[...] = one
    low = one.astype(LOW)
    seq_low, mem_low = low[:rows], low[rows:]
    wq_ref[...] = dot(seq_low, weight(8)).astype(LOW)
    rq = dot(mem_low, weight(4)).astype(LOW)
    rk = dot(seq_low, weight(5)).astype(LOW)
    rv = dot(seq_low, weight(6)).astype(LOW)
    rq_ref[...] = rq
    rkv_ref[:, :width] = rk
    rkv_ref[:, width:] = rv
    scores = dot_nt(spread_heads(rq * jnp.asarray(SCALE, LOW)), rk)
    top = jnp.max(scores, -1, keepdims=True)
    expo = jnp.exp(scores - top)
    summed = jnp.sum(expo, -1, keepdims=True)
    part_ref[:, :width] = fold_heads(dot(expo.astype(LOW), rv))
    lanes = lax.broadcasted_iota(jnp.int32, (HEADS, PAD, 128), 2)
    heads = lax.broadcasted_iota(jnp.int32, (HEADS, PAD, 128), 0)
    top = jnp.where(lanes == heads, top.reshape(HEADS, PAD, 1), 0.0)
    summed = jnp.where(lanes == heads + HEADS, summed.reshape(HEADS, PAD, 1), 0.0)
    part_ref[:, width:] = jnp.sum(top + summed, 0)


def in_pairs(values):
    own, core, chip, both = values
    return (own + core) + (chip + both)


def widened(stats, start, width):
    lanes = lax.broadcasted_iota(jnp.int32, (128, width), 0)
    heads = lax.broadcasted_iota(jnp.int32, (128, width), 1) // HEAD + start
    return jnp.dot(
        stats, (lanes == heads).astype(F32), precision=lax.Precision.HIGHEST, preferred_element_type=F32
    )


def write_probs(wk, wq):
    scores = dot_nt(spread_heads(wk * jnp.asarray(SCALE, LOW)), wq)
    scores = scores.reshape(HEADS, PAD, scores.shape[1])
    real = lax.broadcasted_iota(jnp.int32, scores.shape, 1) < MEM
    scores = jnp.where(real, scores, NEG)
    expo = jnp.exp(scores - jnp.max(scores, 1, keepdims=True))
    return expo * (1.0 / jnp.sum(expo, 1, keepdims=True))


def finish_kernel(
    last, weight, put, rows_of, one_ref, own_ref, core_ref, chip_ref, both_ref, wq_ref, small_ref, *rest
):
    if last:
        (z_ref, rout_ref, rlse_ref, mempre_ref, two_ref, wkv_ref, wlow_ref, seqpre_ref, x_ref, feedpre_ref) = rest
    else:
        (z_ref, q_ref, kv_ref, kvmem_ref,
         rout_ref, rlse_ref, mempre_ref, two_ref, wkv_ref, wlow_ref, seqpre_ref, x_ref, feedpre_ref) = rest
    rows, width = wq_ref.shape
    parts = (own_ref, core_ref, chip_ref, both_ref)
    tops = [widened(part[:, width:], 0, width) for part in parts]
    sums = [widened(part[:, width:], HEADS, width) for part in parts]
    top = jnp.maximum(jnp.maximum(tops[0], tops[1]), jnp.maximum(tops[2], tops[3]))
    fades = [jnp.exp(value - top) for value in tops]
    accum = in_pairs([fade * part[:, :width] for fade, part in zip(fades, parts)])
    summed = in_pairs([fade * value for fade, value in zip(fades, sums)])
    rout = accum / summed
    rout_ref[...] = rout
    rlse_ref[...] = top + jnp.log(summed)
    mempre = one_ref[rows:, :] + dot(rout.astype(LOW), weight(7))
    mempre_ref[...] = mempre
    memtwo = norm(mempre, row(small_ref, rows_of, "gain", 1), row(small_ref, rows_of, "shift", 1))
    memlow = memtwo.astype(LOW)
    wk = dot(memlow, weight(9)).astype(LOW)
    wv = dot(memlow, weight(10)).astype(LOW)
    wkv_ref[:, :width] = wk
    wkv_ref[:, width:] = wv
    probs = write_probs(wk, wq_ref[...]).reshape(HEADS * PAD, rows)
    wlow = dot_tn(probs.astype(LOW), spread_heads(wv)).astype(LOW)
    wlow_ref[...] = wlow
    seqpre = one_ref[:rows, :] + dot(wlow, weight(11))
    seqpre_ref[...] = seqpre
    seqtwo = norm(seqpre, row(small_ref, rows_of, "gain", 2), row(small_ref, rows_of, "shift", 2))
    two_ref[:rows, :] = seqtwo
    two_ref[rows:, :] = memtwo
    two = two_ref[...]
    x = two.astype(LOW)
    x_ref[...] = x
    feed = two + row(small_ref, rows_of, "shift", 4)
    for part in range(rows_of["sizes"][1]):
        u = dot(x, weight(("up", part))) + row(small_ref, rows_of, "bias", part)
        feed = feed + dot(gelu_parts(u)[0].astype(LOW), weight("down", part))
    feedpre_ref[...] = feed
    z_ref[...] = norm(feed, row(small_ref, rows_of, "gain", 3), row(small_ref, rows_of, "shift", 3))
    if not last:
        project(z_ref[...], weight, q_ref, kv_ref, kvmem_ref)


def feed_back_kernel(
    share, weight, put, rows_of, grad_ref, feedpre_ref, x_ref, seqpre_ref, wlow_ref, wq_ref, wkv_ref, one_ref,
    small_ref,
    gbias_ref, gsmall_ref, mem_ref, seq_ref, part_ref,
):
    rows, width = wq_ref.shape
    full = grad_ref.shape[0]
    balance = jnp.where(lax.broadcasted_iota(jnp.int32, (full, 1), 0) < rows, 1.0, share)
    grad = grad_ref[...]
    feed, by_unit = norm_back(feedpre_ref[...], row(small_ref, rows_of, "gain", 3), grad)
    gsmall_ref[0:1, :] = total(by_unit * balance)
    gsmall_ref[1:2, :] = total(grad * balance)
    low = feed.astype(LOW)
    low_share = (low.astype(F32) * balance).astype(LOW)
    gsmall_ref[2:3, :] = total(low_share.astype(F32))
    x = x_ref[...]
    two = feed
    high, parts, _ = rows_of["sizes"]
    order = bias_order(width, high, parts)
    piece = width // parts
    for part in range(parts):
        u = dot(x, weight(("up", part))) + row(small_ref, rows_of, "bias", part)
        value, slope = gelu_parts(u)
        put(("down", part), dot_tn(value.astype(LOW), low_share))
        pre = (dot_nt(low, weight("down", part)) * slope).astype(LOW)
        pre_share = (pre.astype(F32) * balance).astype(LOW)
        line = dot(total(pre_share.astype(F32)).astype(LOW), order)
        for j in range(parts):
            gbias_ref[j : j + 1, part * piece : (part + 1) * piece] = line[:, j * piece : (j + 1) * piece]
        put(("up", part), dot_tn(x, pre_share))
        two = two + dot_nt(pre, weight(("up", part)))
    mem_ref[...] = two[rows:]
    grad = two[:rows]
    seq, by_unit = norm_back(seqpre_ref[...], row(small_ref, rows_of, "gain", 2), grad)
    gsmall_ref[3:4, :] = total(by_unit)
    gsmall_ref[4:5, :] = total(grad)
    low = seq.astype(LOW)
    put(11, dot_tn(wlow_ref[...], low))
    out_low = dot_nt(low, weight(11)).astype(LOW)
    wk, wv = wkv_ref[:, :width], wkv_ref[:, width:]
    wq = wq_ref[...]
    probs = write_probs(wk, wq)
    prob_grad = dot_nt(spread_heads(wv), out_low).reshape(probs.shape)
    delta = jnp.sum(probs * prob_grad, 1, keepdims=True)
    score_grad = (probs * (prob_grad - delta)).reshape(HEADS * PAD, rows).astype(LOW)
    wq_low = (dot_tn(score_grad, spread_heads(wk)) * SCALE).astype(LOW)
    part_ref[:PAD, :] = (fold_heads(dot(score_grad, wq)) * SCALE).astype(LOW)
    part_ref[PAD:, :] = fold_heads(dot(probs.reshape(HEADS * PAD, rows).astype(LOW), out_low)).astype(LOW)
    put(8, dot_tn(one_ref[:rows, :].astype(LOW), wq_low))
    seq_ref[...] = seq + dot_nt(wq_low, weight(8))


def read_back_kernel(
    share, weight, put, rows_of, own_ref, core_ref, chip_ref, both_ref, mem_ref, seq_ref, two_ref, mempre_ref, rout_ref, rlse_ref, rq_ref, rkv_ref, one_ref,
    pre_ref, small_ref,
    gsmall_ref, memgrad_ref, seqjoint_ref, part_ref,
):
    rows, width = seq_ref.shape
    summed = in_pairs([part[...].astype(F32) for part in (own_ref, core_ref, chip_ref, both_ref)])
    k_low = summed[:PAD].astype(LOW)
    v_low = summed[PAD:].astype(LOW)
    mem_low = two_ref[rows:, :].astype(LOW)
    put(9, dot_tn(mem_low, k_low) * share)
    put(10, dot_tn(mem_low, v_low) * share)
    grad = mem_ref[...] + dot_nt(k_low, weight(9)) + dot_nt(v_low, weight(10))
    mem, by_unit = norm_back(mempre_ref[...], row(small_ref, rows_of, "gain", 1), grad)
    gsmall_ref[0:1, :] = total(by_unit) * share
    gsmall_ref[1:2, :] = total(grad) * share
    low = mem.astype(LOW)
    rout = rout_ref[...]
    put(7, dot_tn(rout.astype(LOW), low) * share)
    out_low = dot_nt(low, weight(7)).astype(LOW)
    memgrad_ref[...] = mem
    rk, rv = rkv_ref[:, :width], rkv_ref[:, width:]
    rq = spread_heads(rq_ref[...] * jnp.asarray(SCALE, LOW))
    out_wide = spread_heads(out_low)
    delta = jnp.sum(spread_heads(out_low.astype(F32) * rout), -1, keepdims=True)
    mask = head_mask(width)
    lse = jnp.max(jnp.where(mask, rlse_ref[...][None], -BIG).reshape(HEADS * PAD, width), -1, keepdims=True)
    probs = jnp.exp(dot_nt(rq, rk) - lse)
    score_grad = (probs * (dot_nt(out_wide, rv) - delta)).astype(LOW)
    part_ref[...] = (fold_heads(dot(score_grad, rk)) * SCALE).astype(LOW)
    key_low = dot_tn(score_grad, rq).astype(LOW)
    value_low = dot_tn(probs.astype(LOW), out_wide).astype(LOW)
    seq_low = one_ref[:rows, :].astype(LOW)
    put(5, dot_tn(seq_low, key_low))
    put(6, dot_tn(seq_low, value_low))
    grad = seq_ref[...] + dot_nt(key_low, weight(5)) + dot_nt(value_low, weight(6))
    joint, by_unit = norm_back(pre_ref[:rows, :], row(small_ref, rows_of, "gain", 0), grad)
    gsmall_ref[2:3, :] = total(by_unit)
    gsmall_ref[3:4, :] = total(grad)
    seqjoint_ref[...] = joint


def attend_back_kernel(
    share, weight, put, rows_of, z_ref, part_ref, corepart_ref, chippart_ref, bothpart_ref, memgrad_ref, seqjoint_ref, one_ref, pre_ref, att_ref, lse_ref,
    q_ref, own_ref, core_ref, chip_ref, both_ref, kvmem_ref, segs_ref, segq_ref, small_ref,
    gsmall_ref, joint_ref, qgrad_ref, keep_ref, pass_ref, send_ref,
    keys_ref, bound_ref, out_ref, kvgrad_ref,
):
    rows, width = seqjoint_ref.shape
    full = att_ref.shape[0]
    place_keys(keys_ref, own_ref, core_ref, chip_ref, both_ref, kvmem_ref)
    place_bounds(bound_ref, segs_ref, segq_ref[...])
    parts = (part_ref, corepart_ref, chippart_ref, bothpart_ref)
    q_low = in_pairs([part[...].astype(F32) for part in parts]).astype(LOW)
    put(4, dot_tn(one_ref[rows:, :].astype(LOW), q_low) * share)
    grad = memgrad_ref[...] + dot_nt(q_low, weight(4))
    mem, by_unit = norm_back(pre_ref[rows:, :], row(small_ref, rows_of, "gain", 0), grad)
    gsmall_ref[0:1, :] = total(by_unit) * share
    gsmall_ref[1:2, :] = total(grad) * share
    joint_ref[:rows, :] = seqjoint_ref[...]
    joint_ref[rows:, :] = mem
    low = joint_ref[...].astype(LOW)
    balance = jnp.where(lax.broadcasted_iota(jnp.int32, (full, 1), 0) < rows, 1.0, share)
    put(3, dot_tn(att_ref[...], (low.astype(F32) * balance).astype(LOW)))
    out_ref[...] = dot_nt(low, weight(3)).astype(LOW)

    def pair(step, carry):
        lanes = pl.ds(pl.multiple_of(step * 128, 128), 128)
        more = pl.ds(pl.multiple_of(width + step * 128, 128), 128)
        query = q_ref[:, lanes] * jnp.asarray(SCALE, LOW)
        out = out_ref[:, lanes]
        low_balance = jnp.concatenate([balance, balance], 0)
        product = (out.astype(F32) * att_ref[:, lanes].astype(F32)).T
        delta = jnp.concatenate([total(product[:HEAD]), total(product[HEAD:])], 1)
        query = two_heads(query)
        out = two_heads(out)
        keys = keys_ref[:, lanes]
        values = keys_ref[:, more]
        scores = jnp.minimum(dot_nt(keys, query), bound_ref[...])
        probs = jnp.exp(scores - lse_ref[pl.ds(step, 1), :])
        prob_grad = dot_nt(values, out)
        score_grad = (probs * (prob_grad - delta)).astype(LOW)
        qgrad_ref[:, lanes] = (pick_heads(dot_tn(keys, score_grad)) * SCALE).astype(LOW)
        query_share = (query.astype(F32) * low_balance).astype(LOW)
        out_share = (out.astype(F32) * low_balance).astype(LOW)
        kvgrad_ref[:, lanes] = dot(score_grad, query_share).astype(LOW)
        kvgrad_ref[:, more] = dot(probs.astype(LOW), out_share).astype(LOW)
        return carry

    lax.fori_loop(0, width // 128, pair, 0)
    z_low = z_ref[...].astype(LOW)
    put(0, dot_tn(z_low, (qgrad_ref[...].astype(F32) * balance).astype(LOW)))
    me = lax.axis_index("blk")
    for goal, place, other in ((keep_ref, 0, 0), (pass_ref, 0, 2), (send_ref, 0, 1), (send_ref, rows, 3)):
        rest = pl.ds(pl.multiple_of((me ^ other) * rows, rows), rows)
        goal[place : place + rows, :] = kvgrad_ref[rest, :]
    pass_ref[rows:, :] = kvgrad_ref[4 * rows :, :]
    send_ref[2 * rows :, :] = kvgrad_ref[4 * rows :, :]


def input_back_kernel(
    share, weight, put, rows_of, z_ref, joint_ref, qgrad_ref, keep_ref, near_ref, sent_ref, got_ref, *rest
):
    *small_refs, zgrad_ref, kvgrad_ref = rest
    full, width = z_ref.shape
    rows = full - PAD
    balance = jnp.where(lax.broadcasted_iota(jnp.int32, (full, 1), 0) < rows, 1.0, share)
    low = z_ref[...].astype(LOW)
    mine = keep_ref[...].astype(F32) + near_ref[:rows, :].astype(F32)
    kvgrad_ref[:rows, :] = (mine + got_ref[:rows, :].astype(F32)).astype(LOW)
    kvgrad_ref[rows:, :] = (sent_ref[rows:, :].astype(F32) + got_ref[rows:, :].astype(F32)).astype(LOW)
    grads = (qgrad_ref[...], kvgrad_ref[:, :width], kvgrad_ref[:, width:])
    grad = joint_ref[...]
    for part, value in enumerate(grads):
        if part > 0:
            put(part, dot_tn(low, (value.astype(F32) * balance).astype(LOW)))
        grad = grad + dot_nt(value, weight(part))
    zgrad_ref[...] = grad
    if small_refs:
        layers = [[ref[...] for ref in small_refs[k : k + 4]] for k in range(0, len(small_refs), 4)]
        lines = []
        for one, two, three, _ in layers:
            lines.extend([two[2:3] + three[0:1], two[0:1], one[3:4], one[0:1]])
        for one, two, three, _ in layers:
            lines.extend([two[3:4] + three[1:2], two[1:2], one[4:5], one[1:2], one[2:3]])
        lines.extend(bias for _, _, _, bias in layers)
        lines.append(grad[rows:] * share)
        small = jnp.concatenate(lines, 0)
        small = jnp.concatenate([small, jnp.zeros((width - small.shape[0], width), F32)], 0)
        put("small", small.T)


class Order:
    def __init__(self, stages):
        self.stages = stages

    def place(self, number):
        result = 0
        for stage in self.stages:
            result = 2 * result + ((number >> bit_place(stage)) & 1)
        return result

    def mine(self):
        result = 0
        for axis, bit in self.stages:
            result = 2 * result + ((lax.axis_index(axis) >> bit) & 1)
        return result


def call(kernel, name, cost, ins, outs, weights, scratch=(), grads=(), rows_of=None):
    sources, operands, begins = [], [], []
    for source, _, _ in weights.values():
        if not any(source is other for other in sources):
            sources.append(source)
            begins.append(len(operands))
            operands.extend(source[0])
    places, slots = {}, 0
    for key, (source, slot, count) in weights.items():
        which = [source is other for other in sources].index(True)
        places[key] = (which, slot, slots, count)
        slots = slots + count
    high, width = operands[0].shape[2:]
    shards = width // high
    groups, goals, aliases, shapes, made_shapes, grad_places = [], [], {}, [], [], {}
    for number, (keys, order, count, total_slots, into) in enumerate(grads):
        place = 0
        for key in keys:
            grad_places[key] = (number, place, count if key == "down" else 1)
            place += grad_places[key][2]
        halves = 1 if order is None else 2
        arrays, start = into or ((), 0)
        for half, array in enumerate(arrays):
            aliases[len(ins) + len(operands) + len(goals)] = len(shapes) + half
            goals.append(array)
        groups.append((order, halves, len(shapes), start))
        shapes += [jax.ShapeDtypeStruct((shards // halves, total_slots or place, high, width), LOW)] * halves
        made_shapes += [pltpu.VMEM((shards, place, high, width), LOW), pltpu.SemaphoreType.DMA((place, 2))]

    def body(*refs):
        in_refs, refs = refs[: len(ins)], refs[len(ins) :]
        operand_refs, refs = refs[: len(operands)], refs[len(operands) + len(goals) :]
        grad_refs, refs = refs[: len(shapes)], refs[len(shapes) :]
        refs, made_refs = refs[: len(refs) - len(made_shapes)], refs[len(refs) - len(made_shapes) :]
        *refs, buffer, sems = refs
        core = lax.axis_index("blk") % 2
        copies = {}
        for turn, (key, (which, slot, place, count)) in enumerate(places.items()):
            copies[key] = []
            arrays = len(sources[which][0])
            piece = shards // arrays
            for part in range(arrays):
                copy = pltpu.make_async_copy(
                    operand_refs[begins[which] + part].at[:, pl.ds(slot, count)],
                    buffer.at[pl.ds(part * piece, piece), pl.ds(place, count)],
                    sems.at[turn, part],
                )
                copy.start()
                copies[key].append(copy)
        arrived = set()
        offsets = [None if order is None else order.mine() for _, order in sources]
        goal_offsets = [None if order is None else order.mine() for order, _, _, _ in groups]

        def weight(key, part=None):
            if key not in arrived:
                for copy in copies[key]:
                    copy.wait()
                arrived.add(key)
            which, _, place, count = places[key]
            order = sources[which][1]
            span = range(shards) if part is None else range(part * (shards // count), (part + 1) * (shards // count))
            pieces = []
            for shard in span:
                if order is None:
                    at = shard
                else:
                    at = ((shard % 2) ^ core) * (shards // 2) + (order.place(shard) ^ offsets[which])
                pieces.extend(buffer[at, place + slot] for slot in range(count))
            return jnp.concatenate(pieces, 0)

        out = []

        def put(key, grad):
            low = grad.astype(LOW)
            down = isinstance(key, tuple) and key[0] == "down"
            number, slot, count = grad_places["down" if down else key]
            order, halves, begin, start = groups[number]
            made, made_sems = made_refs[2 * number], made_refs[2 * number + 1]
            first = key[1] * (shards // count) if down else 0
            for block in range(low.shape[0] // high):
                shard, inner = first + block // count, block % count
                at = shard
                if order is not None:
                    at = ((shard % 2) ^ core) * (shards // 2) + (order.place(shard) ^ goal_offsets[number])
                made[at, slot + inner] = low[block * high : (block + 1) * high]
            if not down or key[1] == count - 1:
                piece = shards // halves
                for half in range(halves):
                    copy = pltpu.make_async_copy(
                        made.at[pl.ds(half * piece, piece), pl.ds(slot, count)],
                        grad_refs[begin + half].at[:, pl.ds(start + slot, count)],
                        made_sems.at[slot, half],
                    )
                    copy.start()
                    out.append(copy)

        kernel(weight, put, rows_of, *in_refs, *refs)
        for copy in out:
            copy.wait()

    inside, anywhere = pl.BlockSpec(memory_space=pltpu.VMEM), pl.BlockSpec(memory_space=pl.ANY)
    results = pl.pallas_call(
        body,
        out_shape=shapes + [jax.ShapeDtypeStruct(shape, kind) for shape, kind in outs],
        in_specs=[inside] * len(ins) + [anywhere] * (len(operands) + len(goals)),
        out_specs=[anywhere] * len(shapes) + [inside] * len(outs),
        scratch_shapes=list(scratch)
        + [pltpu.VMEM((shards, slots, high, width), LOW), pltpu.SemaphoreType.DMA((len(weights), 2))]
        + made_shapes,
        input_output_aliases=aliases,
        compiler_params=pltpu.CompilerParams(vmem_limit_bytes=VMEM_LIMIT),
        cost_estimate=pl.CostEstimate(flops=int(cost * 3.3e8), bytes_accessed=0, transcendentals=0),
        name=name,
    )(*ins, *operands, *goals)
    made = [results[begin : begin + halves] for _, halves, begin, _ in groups]
    return made + list(results[len(shapes) :])


def flipped(value, bit):
    size = lax.axis_size("blk")
    return lax.ppermute(value, "blk", [(source, source ^ bit) for source in range(size)])


def fence(*arrays):
    return list(lax.optimization_barrier(tuple(arrays)))


def quartet(value):
    return both_chips(value, flipped(value, 2))


def both_chips(own, chip):
    return [own, flipped(own, 1), chip, flipped(chip, 1)]


def bits_of(axis):
    return lax.axis_size(axis).bit_length() - 1


def bit_place(stage):
    axis, bit = stage
    return bit if axis == "blk" else bits_of("blk") + bit


def pack_kernel(attn_ref, *refs):
    inputs, out_ref, (lines_ref, wide_ref, *held, sems) = refs[:5], refs[5], refs[6:]
    count, high, width = out_ref.shape
    origins = (attn_ref.at[0, pl.ds(0, count - 1)],) + inputs
    copies = [
        pltpu.make_async_copy(origin, goal, sems.at[place])
        for place, (origin, goal) in enumerate(zip(origins, [wide_ref] + held))
    ]
    for copy in copies:
        copy.start()
    lines_ref[...] = jnp.zeros(lines_ref.shape, F32)
    for copy in copies:
        copy.wait()
    gain_ref, shift_ref, bias_ref, memory_ref, seg_ref = held
    layers, rows, _ = gain_ref.shape
    place = layers * rows
    for layer in range(layers):
        lines_ref[layer * rows : (layer + 1) * rows, 0:high] = gain_ref[layer]
    rows = shift_ref.shape[0]
    for line in range(rows):
        for layer in range(layers):
            goal = place + layer * rows + line
            lines_ref[goal : goal + 1, 0:high] = shift_ref[line, layer : layer + 1]
    place += layers * rows
    layers, hidden = bias_ref.shape
    for layer in range(layers):
        for part in range(hidden // high):
            lines_ref[place : place + 1, 0:high] = bias_ref[layer : layer + 1, part * high : (part + 1) * high]
            place += 1
    columns = lines_ref[...].T
    lines_ref[...] = columns
    lines_ref[0:high, place : place + MEM] = memory_ref[...]
    out_ref[count - 1] = jnp.zeros((high, width), LOW)
    out_ref[count - 1, :, 0:128] = lines_ref[0:high, :].astype(LOW)
    lines_ref[...] = jnp.zeros(lines_ref.shape, F32)
    for line in range(seg_ref.shape[1] // 128):
        lines_ref[line : line + 1, :] = seg_ref[:, line * 128 : (line + 1) * 128].astype(F32)
    out_ref[count - 1, :, 128:256] = lines_ref[0:high, :].astype(LOW)
    out_ref[0 : count - 1] = wide_ref[...].astype(LOW)


def unpack_kernel(slot, sums_ref, gain_ref, shift_ref, bias_ref, memory_ref, lines_ref):
    high = sums_ref.shape[1]
    lines_ref[...] = jnp.zeros(lines_ref.shape, F32)
    columns = sums_ref[slot, :, 0:128]
    lines_ref[0:high, :] = columns
    lines = lines_ref[...].T
    layers, rows, _ = gain_ref.shape
    place = layers * rows
    for layer in range(layers):
        gain_ref[layer] = lines[layer * rows : (layer + 1) * rows, 0:high]
    rows = shift_ref.shape[0]
    for line in range(rows):
        for layer in range(layers):
            goal = place + layer * rows + line
            shift_ref[line, layer : layer + 1] = lines[goal : goal + 1, 0:high]
    place += layers * rows
    layers, hidden = bias_ref.shape
    for layer in range(layers):
        for part in range(hidden // high):
            bias_ref[layer : layer + 1, part * high : (part + 1) * high] = lines[place : place + 1, 0:high]
            place += 1
    memory_ref[...] = columns[:, place : place + MEM]


def flat(stages):
    return [bit for stage in stages for bit in (stage if isinstance(stage[0], tuple) else (stage,))]


def swapped(value, stage):
    if isinstance(stage[0], tuple):
        mask = sum(1 << bit_place(bit) for bit in stage)
        everyone = lax.axis_size("dp") * lax.axis_size("blk")
        return lax.ppermute(value, ALL, [(source, source ^ mask) for source in range(everyone)])
    axis, bit = stage
    return lax.ppermute(value, axis, [(source, source ^ (1 << bit)) for source in range(lax.axis_size(axis))])


class Gathering:
    def __init__(self, groups):
        self.groups = groups
        self.held = [shard[None] for shard, _, _ in groups]
        self.got, self.turn = {}, 0

    def begin(self):
        done = {}
        for number, (_, stages, first) in enumerate(self.groups):
            if first <= self.turn < first + len(stages) and stages[self.turn - first] is not None:
                self.got[number] = swapped(self.held[number], stages[self.turn - first])
                if self.turn - first + 1 == len(stages) and stages[-1] == ("blk", 0):
                    done[number] = ((self.held[number], self.got.pop(number)), Order([s for s in stages[-2::-1] if s]))
        return done

    def split(self, number, slots, stages):
        held, (shard, done, _) = self.held[number], self.groups[number]
        parts = (held[:, :slots], held[:, slots:])
        for place, part, more in zip((number, len(self.groups)), parts, stages):
            self.groups[place : place + 1] = [(shard, done + more, self.turn - len(done))]
            self.held[place : place + 1] = [part]

    def end(self, *others):
        numbers = list(self.got)
        bundle = fence(*self.got.values(), *others)
        for number, value in zip(numbers, bundle):
            self.held[number] = jnp.concatenate([self.held[number], value])
        self.got = {}
        self.turn += 1
        return bundle[len(numbers) :]


def joined(values):
    return values[0] if len(values) == 1 else jnp.concatenate(values, 1)


class Scattering:
    def __init__(self, arrays, stages):
        self.keeps = [keep for keep, _ in arrays]
        self.sends = [[send for _, send in arrays]]
        self.stages = list(stages)
        self.gots, self.result = None, None

    def begin(self):
        bits = flat([self.stages.pop(0)])
        self.gots = []
        for piece, sends in enumerate(self.sends):
            some = tuple(bit for place, bit in enumerate(bits) if (piece + 1) >> (len(bits) - 1 - place) & 1)
            self.gots.extend(swapped(send, some if len(some) > 1 else some[0]) for send in sends)

    def end(self):
        sums = []
        for place, keep in enumerate(self.keeps):
            value = keep.astype(F32)
            for got in self.gots[place :: len(self.keeps)]:
                value = value + got.astype(F32)
            sums.append(value)
        self.gots = None
        if not self.stages:
            self.result = joined(sums)[0]
            return
        pieces = 2 ** len(flat(self.stages[:1]))
        size = sums[0].shape[0] // pieces
        parts = [joined([value[k * size : (k + 1) * size] for value in sums]).astype(LOW) for k in range(pieces)]
        self.keeps, self.sends = parts[:1], [[part] for part in parts[1:]]


class Background:
    def __init__(self):
        self.sums, self.running, self.staying = {}, [], set()

    def add(self, name, arrays, stages):
        self.sums[name] = Scattering(arrays, stages)

    def begin(self, *names):
        self.staying = {name[1:] for name in names if name[0] == "~"}
        for name in names:
            short = name.rstrip("+")
            if short in self.sums:
                self.sums[short].begin()
                self.running.append(short)
                if short != name:
                    self.staying.add(short)

    def merge(self, name, other):
        one, two = self.sums[name], self.sums[other]
        if one.stages and one.stages == two.stages:
            one.keeps = [joined(one.keeps + two.keeps)]
            one.sends = [[joined(first + second)] for first, second in zip(one.sends, two.sends)]
            two.stages = []

    def end(self, *others):
        ending = [self.sums[name] for name in self.running if name not in self.staying]
        self.running = [name for name in self.running if name in self.staying]
        self.staying = set()
        gots = fence(*[got for run in ending for got in run.gots], *others)
        for run in ending:
            run.gots, gots = gots[: len(run.gots)], gots[len(run.gots) :]
            run.end()
        return gots


def local(
    tokens, segments, memory_init, attn_weights, ffn_in, ffn_out, ffn_bias, norm_gain, norm_shift, out_grad, memory_cot
):
    layers, count, rows, width = attn_weights.shape
    hidden = ffn_in.shape[2]
    per = hidden // width
    everyone = lax.axis_size("dp") * lax.axis_size("blk")
    direct = rows == 16
    core_bit, chip_bits = ("blk", 0), [("blk", bit) for bit in range(1, bits_of("blk"))]
    line_bits, near_bit = [("dp", bit) for bit in reversed(range(1, bits_of("dp")))], [("dp", 0)]

    small = [
        norm_gain.reshape(-1, rows), norm_shift.reshape(-1, rows), ffn_bias.reshape(-1, rows), memory_init
    ]
    starts = [sum(part.shape[0] for part in small[:k]) for k in range(5)]
    gain_rows, shift_rows = norm_gain.shape[1], norm_shift.shape[1]
    small = jnp.concatenate(small, 0).T.astype(LOW)
    numbers = jnp.pad(segments.reshape(-1, 128).astype(LOW), ((0, rows - segments.size // 128), (0, 0)))
    small = jnp.concatenate([jnp.pad(small, ((0, 0), (0, 128 - small.shape[1]))), numbers], 1)
    small = jnp.pad(small, ((0, 0), (0, width - small.shape[1])))[None]

    def rows_of(index):
        return dict(
            gain=starts[0] + index * gain_rows,
            shift=starts[1] + index * shift_rows,
            bias=64 + index * per,
            memory=starts[3],
            sizes=(rows, per, starts[2]),
        )

    def lowered(attn, up, down):
        up = up.astype(LOW).reshape(layers, rows, per, width).transpose(0, 2, 1, 3)
        return attn, up, down.astype(LOW).reshape(layers, per, rows, width)

    attn_low, up_low, down_low = lowered(attn_weights, ffn_in, ffn_out)
    early, middle, late = (0, 1, 2), (3, 8, 4, 5, 6), (7, 9, 10, 11)
    table = {}

    def listed(source, index, keys):
        place = 0
        for key in keys:
            size = per if key == "down" else 1
            table[index, key] = (source, place, size)
            place += size

    ups = tuple(("up", part) for part in range(per))
    if direct:

        def picked(index, keys):
            return [attn_low[index, key][None].astype(LOW) for key in keys]

        far, line = line_bits[:1], line_bits[1:]
        last = [core_bit]
        pause = [None]
        inside, anywhere = pl.BlockSpec(memory_space=pltpu.VMEM), pl.BlockSpec(memory_space=pl.ANY)
        packed_small = (norm_gain, norm_shift.transpose(1, 0, 2), ffn_bias, memory_init.T, segments)
        first_shard = pl.pallas_call(
            pack_kernel,
            out_shape=jax.ShapeDtypeStruct((len(early) + 1, rows, width), LOW),
            in_specs=[pl.BlockSpec(memory_space=pltpu.HBM)] * 6,
            out_specs=inside,
            scratch_shapes=[pltpu.VMEM((128, 128), F32), pltpu.VMEM((len(early), rows, width), F32)]
            + [
                pltpu.VMEM(part.shape, part.dtype)
                for part in packed_small
            ]
            + [pltpu.SemaphoreType.DMA((6,))],
            compiler_params=pltpu.CompilerParams(vmem_limit_bytes=3 * VMEM_LIMIT),
            name="pack",
        )(attn_weights, *packed_small)
        gathering = Gathering(
            [
                (first_shard, far + line + chip_bits + near_bit + last, 0),
                (jnp.concatenate(picked(0, middle)), far + line + near_bit + chip_bits + last, 0),
            ]
        )
        gathering.begin()
        attn_weights, ffn_in, ffn_out = gathering.end(attn_weights, ffn_in, ffn_out)
        attn_low, up_low, down_low = lowered(attn_weights, ffn_in, ffn_out)
        gathering.groups += [
            (
                jnp.concatenate(picked(0, late) + [up_low[0, :1]]),
                far + line + near_bit + chip_bits + last,
                2,
            ),
            (
                jnp.concatenate([down_low[0], up_low[0, 1:2]]),
                chip_bits + far + line + pause + near_bit + last,
                1,
            ),
            (
                jnp.concatenate([up_low[0, 2:]] + picked(1, early)),
                far + chip_bits + pause + near_bit + line + last,
                1,
            ),
            (jnp.concatenate(picked(1, middle)), far + line + pause + chip_bits + near_bit + last, 3),
            (jnp.concatenate(picked(1, late) + [up_low[1]]), far + line, 6),
            (down_low[1], near_bit + far + chip_bits + line + last, 6),
        ]
        gathering.held += [shard[None] for shard, _, _ in gathering.groups[2:]]
        gathering.begin()
        gathering.end()
        for turn in range(2, 4):
            gathering.begin()
            gathering.end()
        found = gathering.begin()
        arrived = fence(*[source[0][1] for source in (found[0], found[1])])
        for number, got in enumerate(arrived):
            found[number] = ((found[number][0][0], got), found[number][1])
        listed(found[0], 0, early + ("small",))
        listed(found[1], 0, middle)
    else:
        packed = jnp.concatenate(
            [attn_low.astype(LOW).reshape(-1, rows, width), up_low.reshape(-1, rows, width), small, down_low.reshape(-1, rows, width)]
        )
        whole = lax.all_gather(packed, ALL)
        split = layers * (count + per) + 1
        square = whole[:, :split].transpose(1, 0, 2, 3).reshape(split, -1, 16, width)
        downs = whole[:, split:].reshape(everyone, layers, per * rows, width).transpose(1, 0, 2, 3)
        downs = downs.reshape(layers, -1, per, 16, width).transpose(0, 2, 1, 3, 4).reshape(layers * per, -1, 16, width)
        source = ((jnp.concatenate([square, downs]).transpose(1, 0, 2, 3),), None)
        for index in range(layers):
            for key in range(count):
                table[index, key] = (source, index * count + key, 1)
            for part in range(per):
                table[index, ("up", part)] = (source, layers * count + index * per + part, 1)
            table[index, "down"] = (source, split + index * per, per)
        table[0, "small"] = (source, split - 1, 1)

    def attn(index, *keys):
        return {key: table[index, key] for key in keys}

    def feed(index):
        return attn(index, *ups, "down")

    length = tokens.shape[1]
    full = length + PAD
    size = lax.axis_size("blk")
    share = 1.0 / size
    me = lax.axis_index("blk")
    seg = segments[0].astype(F32)
    seg_row = jnp.concatenate([seg, jnp.full((PAD,), -1.0, F32)])
    seg_queries = jnp.concatenate([seg_row, seg_row]).reshape(1, -1)
    every = size * length + PAD
    keys_scratch = pltpu.VMEM((every, 2 * width), LOW)
    bound_scratch = pltpu.VMEM((every, 2 * full), F32)
    projected = [((full, width), LOW), ((length, 2 * width), LOW), ((PAD, 2 * width), LOW)]

    smalls, z, q, own, kvmem, *numbers = call(
        first_kernel,
        "first",
        4,
        [tokens[0]],
        [((128, width), F32), ((full, width), F32)] + projected + ([((size, length), F32)] if direct else []),
        attn(0, *early, "small"),
        [pltpu.VMEM((width, 128), F32)] if direct else [],
        rows_of=rows_of(0),
    )
    seg_all = numbers[0] if direct else jnp.concatenate(quartet(segments.astype(LOW))).astype(F32)
    kept = []
    for index in range(layers):
        chip = flipped(own, 2)
        if direct:
            own, chip = gathering.end(own, chip)
            if index > 0:
                gathering.split(6, len(late), [chip_bits + near_bit + [core_bit], near_bit + chip_bits + [core_bit]])
            found = gathering.begin()
            if index > 0:
                listed(found[5], index, middle)
        _, core, _, both = both_chips(own, chip)
        att, lse, pre, first, rq, rkv, wq, part = call(
            attend_kernel,
            f"attend_{index}",
            13,
            [z, q, own, core, chip, both, kvmem, seg_all, seg_queries, smalls],
            [
                ((full, width), LOW), ((width // 128, 2 * full), F32), ((full, width), F32), ((full, width), F32),
                ((PAD, width), LOW),
                ((length, 2 * width), LOW), ((length, width), LOW), ((PAD, width + 128), F32),
            ],
            attn(index, 3, 8, 4, 5, 6),
            [keys_scratch, bound_scratch],
            rows_of=rows_of(index),
        )
        if direct and index > 0:
            (part,) = gathering.end(part)
            gathering.begin()
        part_chip = flipped(part, 2)
        if direct:
            part, part_chip = gathering.end(part, part_chip)
            found = gathering.begin()
            if index == 0:
                listed(found[2], 0, late + ups[:1])
                listed(found[3], 0, ("down",) + ups[1:2])
                listed(found[4], 0, ups[2:])
                for key in early:
                    table[1, key] = (found[4], per - 2 + key, 1)
            else:
                listed(found[6], 1, late)
                listed(found[7], 1, ("down",))
                listed(found[8], 1, ups)
        parts = both_chips(part, part_chip)
        last = index + 1 == layers
        results = call(
            functools.partial(finish_kernel, last),
            f"finish_{index}",
            10,
            [first, *parts, wq, smalls],
            [((full, width), F32)]
            + ([] if last else projected)
            + [
                ((PAD, width), F32), ((PAD, width), F32), ((PAD, width), F32), ((full, width), F32),
                ((PAD, 2 * width), LOW), ((length, width), LOW), ((length, width), F32), ((full, width), LOW),
                ((full, width), F32),
            ],
            attn(index, 7, 9, 10, 11) | feed(index) | ({} if last else attn(index + 1, *early)),
            rows_of=rows_of(index),
        )
        rout, rlse, mempre, second, wkv, wlow, seqpre, x, feedpre = results[-9:]
        kept.append(
            dict(
                z=z, q=q, own=own, kvmem=kvmem, core=core, chip=chip, both=both, att=att, lse=lse, pre=pre, first=first,
                rq=rq, rkv=rkv, wq=wq, rout=rout, rlse=rlse, mempre=mempre, second=second, wkv=wkv, wlow=wlow,
                seqpre=seqpre, x=x, feedpre=feedpre,
            )
        )
        z = results[0]
        if not last:
            q, own, kvmem = results[1:4]
            if direct:
                q, own, kvmem = gathering.end(q, own, kvmem)
                gathering.begin()
    final = z
    grad = jnp.concatenate(
        [out_grad[0].astype(F32), jnp.pad(memory_cot[0].astype(F32), ((0, PAD - MEM), (0, 0)))]
    )
    background = Background()
    y, x, upward = near_bit, chip_bits, line_bits[::-1]
    orders = {
        "up_1": y + upward + x,
        "up_0": y + upward + x,
        "down_1": upward[:1] + y + upward[1:] + x,
        "down_0": upward[:1] + y + upward[1:] + x,
        "first_1": y + upward + x,
        "second_1": x + upward[:1] + y + upward[1:],
        "second_0": y + x + [tuple(upward)],
        "last": [tuple(y + x), tuple(upward)],
    }

    def order_of(name):
        return orders.get(name, y + x + upward)

    def group(name, keys, slots=None, into=None):
        if not direct:
            return (keys, None, per, None, None)
        return (keys, Order(flat(order_of(name))), per, slots, into)

    group_keys = [ups + (11,), ("down", 8), (9, 10, 7, 5, 6), (4, 3, 0), (1, 2)]
    made = [None] * layers
    for index in reversed(range(layers)):
        k = kept[index]
        names = {name: f"{name}_{index}" for name in ("up", "down", "first", "second")}
        end_name = names["second"] if index > 0 else "last"
        plan = iter(PLAN[index])

        def start(name, arrays):
            if direct:
                background.add(name, [arrays], [core_bit] + order_of(name))

        grads_up, grads_down, gbias, small_one, mem, seq, part = call(
            functools.partial(feed_back_kernel, share),
            f"feed_back_{index}",
            11,
            [grad, k["feedpre"], k["x"], k["seqpre"], k["wlow"], k["wq"], k["wkv"], k["first"], smalls],
            [
                ((per, width), F32),
                ((5, width), F32), ((PAD, width), F32), ((length, width), F32), ((2 * PAD, width), LOW),
            ],
            feed(index) | attn(index, 11, 8),
            grads=[
                group(names["up"], group_keys[0]),
                group(names["down"], group_keys[1]),
            ],
            rows_of=rows_of(index),
        )
        halves = len(grads_up)
        part, mem, seq, *both = background.end(part, mem, seq, *grads_up, *grads_down)
        grads_up, grads_down = both[:halves], both[halves:]
        start(names["up"], grads_up)
        start(names["down"], grads_down)
        if index + 1 < layers:
            start(*waiting)
        background.begin(*next(plan))
        part, chip = background.end(part, flipped(part, 2))
        background.begin(*next(plan))
        parts = both_chips(part, chip)
        grads_read, small_two, mem, seq, part = call(
            functools.partial(read_back_kernel, share),
            f"read_back_{index}",
            4,
            [*parts, mem, seq, k["second"], k["mempre"], k["rout"], k["rlse"], k["rq"], k["rkv"],
             k["first"], k["pre"], smalls],
            [((4, width), F32), ((PAD, width), F32), ((length, width), F32), ((PAD, width), LOW)],
            attn(index, 9, 10, 7, 5, 6),
            grads=[group(names["first"], group_keys[2])],
            rows_of=rows_of(index),
        )
        mem, seq, part, chip, *grads_read = background.end(mem, seq, part, flipped(part, 2), *grads_read)
        start(names["first"], grads_read)
        background.begin(*next(plan))
        parts = both_chips(part, chip)
        grads_attend, small_three, joint, qgrad, keep, pass_on, send = call(
            functools.partial(attend_back_kernel, share),
            f"attend_back_{index}",
            14,
            [k["z"], *parts, mem, seq, k["first"], k["pre"], k["att"], k["lse"], k["q"], k["own"], k["core"], k["chip"],
             k["both"], k["kvmem"], seg_all, seg_queries, smalls],
            [((2, width), F32), ((full, width), F32), ((full, width), LOW),
             ((length, 2 * width), LOW), ((length + PAD, 2 * width), LOW), ((2 * length + PAD, 2 * width), LOW)],
            attn(index, 4, 3),
            [keys_scratch, bound_scratch, pltpu.VMEM((full, width), LOW), keys_scratch],
            grads=[group(names["second"], group_keys[3], 5 if index > 0 else 3)],
            rows_of=rows_of(index),
        )
        pass_on, send, *grads_attend = background.end(pass_on, send, *grads_attend)
        if index == 0:
            start(names["second"], grads_attend)
        background.begin(*next(plan))
        near = flipped(send, 1)
        theirs = (pass_on.astype(F32) + near[length:].astype(F32)).astype(LOW)
        got = flipped(theirs, 2)
        got, theirs = background.end(got, theirs)
        background.begin(*next(plan))
        made[index] = dict(small=[small_one, small_two, small_three], bias=gbias)
        tiny = sum([m["small"] + [m["bias"]] for m in made], []) if index == 0 else []
        grads_last, grad = call(
            functools.partial(input_back_kernel, share),
            f"input_back_{index}",
            3,
            [k["z"], joint, qgrad, keep, near, theirs, got] + tiny,
            [((full, width), F32)],
            attn(index, 0, 1, 2),
            [pltpu.VMEM((full, 2 * width), LOW)],
            grads=[
                group(
                    end_name,
                    group_keys[4] + (("small",) if tiny else ()),
                    *((5, (grads_attend, 3)) if index > 0 else ()),
                )
            ],
            rows_of=rows_of(index),
        )
        waiting = (end_name, grads_last)
        made[index]["grads"] = (grads_up, grads_down, grads_read, grads_attend, grads_last)

    mine = [{} for _ in range(layers)]
    if direct:
        start("last", grads_last)
        background.begin(*next(plan))
        background.end()
        ffn_grads = ()
        for moves in plan:
            background.begin(*moves)
            ffn_grads = background.end(*ffn_grads)
            background.merge("last", "second_0")
            if not ffn_grads:
                ups_grads, down_grads = [], []
                for index in range(layers):
                    value = background.sums[f"up_{index}"].result
                    ups_grads.append(jnp.concatenate([value[part] for part in range(per)], -1))
                    down_grads.append(background.sums[f"down_{index}"].result[:per].reshape(per * rows, width))
                ffn_grads = [jnp.stack(ups_grads), jnp.stack(down_grads)]
        for index in range(layers):
            wanted = [f"{name}_{index}" for name in ("up", "down", "first", "second")] + (["last"] if index == 0 else [])
            if index == 0:
                both = last_sums = background.sums["last"].result
                background.sums["last"].result, background.sums["second_0"].result = both[:3], both[3:]
            results = [background.sums[name].result for name in wanted]
            keys = list(group_keys[:4])
            if index > 0:
                keys[3] = keys[3] + group_keys[4]
            else:
                keys.append(group_keys[4] + ("small",))
            for result, held in zip(results, keys):
                place = 0
                for key in held:
                    number = per if key == "down" else 1
                    mine[index][key] = result[place : place + number].reshape(number * rows, width)
                    place += number
    else:
        outgoing, order = [], []
        for index, m in enumerate(made):
            held = sum(group_keys, ()) + (("small",) if index == 0 else ())
            stack = jnp.concatenate([part[0] for part in m["grads"]], 1).transpose(1, 0, 2, 3)
            place = 0
            for key in held:
                if key == "down":
                    downs = stack[place : place + per].transpose(1, 0, 2, 3).reshape(everyone, per, rows, width)
                    outgoing.append(downs.transpose(1, 0, 2, 3).reshape(per, width, width))
                    order.extend((index, ("down", part)) for part in range(per))
                    place += per
                else:
                    outgoing.append(stack[place].reshape(1, width, width))
                    order.append((index, key))
                    place += 1
        result = lax.psum_scatter(jnp.concatenate(outgoing), ALL, scatter_dimension=1, tiled=True).astype(F32)
        for place, (index, key) in enumerate(order):
            mine[index][key] = result[place]
        for m in mine:
            m["down"] = jnp.concatenate([m["down", part] for part in range(per)])
    if not direct:
        ffn_grads = [
            jnp.stack([jnp.concatenate([m["up", part] for part in range(per)], -1) for m in mine]),
            jnp.stack([m["down"] for m in mine]),
        ]
    if direct:
        small_grads = pl.pallas_call(
            functools.partial(unpack_kernel, 2),
            out_shape=[
                jax.ShapeDtypeStruct(part.shape, F32) for part in packed_small[:4]
            ],
            in_specs=[inside],
            out_specs=[inside] * 4,
            scratch_shapes=[pltpu.VMEM((128, 128), F32)],
            compiler_params=pltpu.CompilerParams(vmem_limit_bytes=VMEM_LIMIT),
            name="unpack",
        )(last_sums)
        small_grads = [small_grads[0], small_grads[1].transpose(1, 0, 2), small_grads[2], small_grads[3].T]
    else:
        back = mine[0]["small"].T
        small_grads = [back[starts[k] : starts[k + 1]].reshape(part.shape) for k, part in enumerate(
            (norm_gain, norm_shift, ffn_bias, memory_init)
        )]
    return (
        final[:length].astype(LOW)[None],
        final[length : length + MEM][None],
        grad[:length][None],
        small_grads[3],
        jnp.stack([jnp.stack([m[key] for key in range(count)]) for m in mine]),
        *ffn_grads,
        small_grads[2],
        small_grads[0],
        small_grads[1],
    )


def solution(mesh):
    in_specs = (
        P("dp", "blk", None),
        P("dp", "blk"),
        P(None, ALL),
        P(None, None, ALL, None),
        P(None, ALL, None),
        P(None, ALL, None),
        P(None, ALL),
        P(None, None, ALL),
        P(None, None, ALL),
        P("dp", "blk", None),
        P("dp", None, None),
    )
    out_specs = (
        P("dp", "blk", None),
        P("dp", None, None),
        P("dp", "blk", None),
        P(None, ALL),
        P(None, None, ALL, None),
        P(None, ALL, None),
        P(None, ALL, None),
        P(None, ALL),
        P(None, None, ALL),
        P(None, None, ALL),
    )
    return jax.shard_map(local, mesh=mesh, in_specs=in_specs, out_specs=out_specs, check_vma=False)
```

```python
import functools

import jax
import jax.numpy as jnp
from jax import lax
from jax.experimental import pallas as pl
from jax.experimental.pallas import tpu as pltpu
from jax.sharding import PartitionSpec as P

HEADS = 8
HEAD = 64
MEM = 20
PAD = 32
NEG = -1000000000.0
BIG = 3.0e38
EPS = 1e-05
SCALE = HEAD**-0.5
ALL = ("dp", "blk")
LOW = jnp.bfloat16
F32 = jnp.float32
VMEM_LIMIT = 20 * 1024 * 1024
PLAN = {
    1: [
        ("up_1", "down_1"),
        ("up_1", "down_1"),
        ("up_1", "down_1", "first_1"),
        ("up_1", "down_1", "first_1"),
        ("up_1", "down_1", "first_1"),
    ],
    0: [
        ("up_0", "down_0", "second_1"),
        ("up_0", "down_0"),
        ("up_0", "down_0", "first_0", "second_1", "first_1"),
        ("up_0", "down_0", "first_0", "second_1", "second_0"),
        ("first_0", "second_0", "up_0", "first_1", "second_1"),
        ("last", "down_0"),
        ("last", "second_0", "first_0", "second_1"),
        ("last", "first_0"),
    ],
}


def dot(a, b):
    return jnp.dot(a, b, preferred_element_type=F32)


def dot_nt(a, b):
    return lax.dot_general(a, b, (((1,), (1,)), ((), ())), preferred_element_type=F32)


def dot_tn(a, b):
    return lax.dot_general(a, b, (((0,), (0,)), ((), ())), preferred_element_type=F32)


def hat(x):
    center = x - jnp.mean(x, -1, keepdims=True)
    spread = jnp.mean(center * center, -1, keepdims=True)
    inv = lax.rsqrt(spread + EPS)
    return center * inv, inv


def norm(x, gain, shift):
    return hat(x)[0] * gain + shift


def norm_back(x, gain, grad):
    unit, inv = hat(x)
    scaled = grad * gain
    mean_one = jnp.mean(scaled, -1, keepdims=True)
    mean_two = jnp.mean(scaled * unit, -1, keepdims=True)
    return inv * (scaled - mean_one - unit * mean_two), grad * unit


def row(small_ref, rows_of, name, which):
    place = rows_of[name] + which
    return small_ref[place : place + 1, :]


def total(x):
    return jnp.sum(x, 0, keepdims=True)


def gelu_parts(u):
    k = 0.7978845608028654
    t = jnp.tanh(k * (u + 0.044715 * u * u * u))
    half = 0.5 * (1.0 + t)
    slope = half + 0.5 * u * (1.0 - t * t) * (k * (1.0 + 0.134145 * u * u))
    return u * half, slope


def head_mask(width):
    lanes = lax.broadcasted_iota(jnp.int32, (HEADS, 1, width), 2) // HEAD
    return lanes == lax.broadcasted_iota(jnp.int32, (HEADS, 1, width), 0)


def spread_heads(x):
    rows, width = x.shape
    full = jnp.where(head_mask(width), x.astype(F32)[None], 0.0)
    return full.reshape(HEADS * rows, width).astype(x.dtype)


def fold_heads(x):
    rows, width = x.shape
    full = x.reshape(HEADS, rows // HEADS, width)
    return jnp.sum(jnp.where(head_mask(width), full, 0.0), 0)


def two_heads(x):
    first = lax.broadcasted_iota(jnp.int32, x.shape, 1) < HEAD
    zero = jnp.zeros_like(x)
    return jnp.concatenate([jnp.where(first, x, zero), jnp.where(first, zero, x)], 0)


def pick_heads(x):
    width, rows = x.shape
    mine = (lax.broadcasted_iota(jnp.int32, x.shape, 0) < HEAD) == (
        lax.broadcasted_iota(jnp.int32, x.shape, 1) < rows // 2
    )
    both = jnp.where(mine, x, 0.0).T
    return both[: rows // 2] + both[rows // 2 :]


def place_bounds(bound_ref, seg_ref, seg_queries):
    parts, rows = seg_ref.shape
    me = lax.axis_index("blk")
    for other in range(parts):
        numbers = jnp.broadcast_to(seg_ref[other : other + 1, :], (128, rows)).T[:, 0:1]
        allowed = (numbers == seg_queries) | (seg_queries == -1.0)
        place = pl.ds(pl.multiple_of((me ^ other) * rows, rows), rows)
        bound_ref[place, :] = jnp.where(allowed, BIG, NEG)
    memory = lax.broadcasted_iota(jnp.int32, (PAD, seg_queries.shape[1]), 0) < MEM
    bound_ref[4 * rows :, :] = jnp.where(memory, BIG, NEG)


def place_keys(keys_ref, own_ref, core_ref, chip_ref, both_ref, memory_ref):
    rows = core_ref.shape[0]
    me = lax.axis_index("blk")
    pieces = ((me, own_ref), (me ^ 1, core_ref), (me ^ 2, chip_ref), (me ^ 3, both_ref))
    for place, piece in pieces:
        keys_ref[pl.ds(pl.multiple_of(place * rows, rows), rows), :] = piece[0:rows, :]
    keys_ref[4 * rows :, :] = memory_ref[...]


def project(z, weight, q_ref, kv_ref, kvmem_ref):
    low = z.astype(LOW)
    rows, width = kv_ref.shape[0], low.shape[1]
    for part in (1, 2):
        lanes = pl.ds((part - 1) * width, width)
        value = dot(low, weight(part)).astype(LOW)
        kv_ref[:, lanes] = value[:rows]
        kvmem_ref[:, lanes] = value[rows:]
    q_ref[...] = dot(low, weight(0)).astype(LOW)


def bias_order(width, high, per):
    lanes = lax.broadcasted_iota(jnp.int32, (width, width), 0)
    shard, inner = lanes // (per * high), lanes % (per * high)
    goal = inner // high * (width // per) + shard * high + inner % high
    return (goal == lax.broadcasted_iota(jnp.int32, (width, width), 1)).astype(LOW)


def first_kernel(weight, put, rows_of, tokens_ref, small_ref, z_ref, q_ref, kv_ref, kvmem_ref, *seg_refs):
    rows = tokens_ref.shape[0]
    columns = weight("small")
    if seg_refs:
        seg_ref, number_ref = seg_refs
        number_ref[...] = columns[:, 128:256].astype(F32)
        high, size = rows_of["sizes"][0], lax.axis_size("blk")
        for other in range(size):
            shard = lax.axis_index("dp") * size + (lax.axis_index("blk") ^ other)
            numbers = number_ref[pl.ds(pl.multiple_of(shard * high, high), high), :]
            for line in range(rows // 128):
                seg_ref[other : other + 1, line * 128 : (line + 1) * 128] = numbers[line : line + 1]
    columns = columns[:, :128]
    small = columns.astype(F32).T
    width = small.shape[1]
    small_ref[...] = small
    high, per, start = rows_of["sizes"]
    order = bias_order(width, high, per)
    for layer in range((rows_of["memory"] - start) // per):
        lines = small[start + layer * per : start + (layer + 1) * per].astype(LOW)
        piece = width // per
        for part in range(per):
            line = jnp.concatenate([lines[j : j + 1, part * piece : (part + 1) * piece] for j in range(per)], 1)
            place = 64 + layer * per + part
            small_ref[place : place + 1, :] = dot_nt(line, order)
    z_ref[:rows, :] = tokens_ref[...].astype(F32)
    start = rows_of["memory"]
    z_ref[rows : rows + MEM, :] = small[start : start + MEM]
    z_ref[rows + MEM :, :] = jnp.zeros((PAD - MEM, small.shape[1]), F32)
    project(z_ref[...], weight, q_ref, kv_ref, kvmem_ref)


def attend_kernel(
    weight, put, rows_of, z_ref, q_ref, own_ref, core_ref, chip_ref, both_ref, kvmem_ref, segs_ref, segq_ref, small_ref,
    att_ref, lse_ref, pre_ref, one_ref, rq_ref, rkv_ref, wq_ref, part_ref,
    keys_ref, bound_ref,
):
    rows = core_ref.shape[0]
    width = z_ref.shape[1]
    place_keys(keys_ref, own_ref, core_ref, chip_ref, both_ref, kvmem_ref)
    place_bounds(bound_ref, segs_ref, segq_ref[...])

    def pair(step, carry):
        lanes = pl.ds(pl.multiple_of(step * 128, 128), 128)
        more = pl.ds(pl.multiple_of(width + step * 128, 128), 128)
        query = two_heads(q_ref[:, lanes]) * jnp.asarray(SCALE, LOW)
        keys = keys_ref[:, lanes]
        values = keys_ref[:, more]
        scores = jnp.minimum(dot_nt(keys, query), bound_ref[...])
        top = jnp.max(scores, 0, keepdims=True)
        expo = jnp.exp(scores - top)
        summed = jnp.sum(expo, 0, keepdims=True)
        att_ref[:, lanes] = pick_heads(dot_tn(values, expo.astype(LOW)) * (1.0 / summed)).astype(LOW)
        lse_ref[pl.ds(step, 1), :] = top + jnp.log(summed)
        return carry

    lax.fori_loop(0, width // 128, pair, 0)
    pre = z_ref[...] + dot(att_ref[...], weight(3))
    pre_ref[...] = pre
    one = norm(pre, row(small_ref, rows_of, "gain", 0), row(small_ref, rows_of, "shift", 0))
    one_ref[...] = one
    low = one.astype(LOW)
    seq_low, mem_low = low[:rows], low[rows:]
    wq_ref[...] = dot(seq_low, weight(8)).astype(LOW)
    rq = dot(mem_low, weight(4)).astype(LOW)
    rk = dot(seq_low, weight(5)).astype(LOW)
    rv = dot(seq_low, weight(6)).astype(LOW)
    rq_ref[...] = rq
    rkv_ref[:, :width] = rk
    rkv_ref[:, width:] = rv
    scores = dot_nt(spread_heads(rq * jnp.asarray(SCALE, LOW)), rk)
    top = jnp.max(scores, -1, keepdims=True)
    expo = jnp.exp(scores - top)
    summed = jnp.sum(expo, -1, keepdims=True)
    part_ref[:, :width] = fold_heads(dot(expo.astype(LOW), rv))
    lanes = lax.broadcasted_iota(jnp.int32, (HEADS, PAD, 128), 2)
    heads = lax.broadcasted_iota(jnp.int32, (HEADS, PAD, 128), 0)
    top = jnp.where(lanes == heads, top.reshape(HEADS, PAD, 1), 0.0)
    summed = jnp.where(lanes == heads + HEADS, summed.reshape(HEADS, PAD, 1), 0.0)
    part_ref[:, width:] = jnp.sum(top + summed, 0)


def in_pairs(values):
    own, core, chip, both = values
    return (own + core) + (chip + both)


def widened(stats, start, width):
    lanes = lax.broadcasted_iota(jnp.int32, (128, width), 0)
    heads = lax.broadcasted_iota(jnp.int32, (128, width), 1) // HEAD + start
    return jnp.dot(
        stats, (lanes == heads).astype(F32), precision=lax.Precision.HIGHEST, preferred_element_type=F32
    )


def write_probs(wk, wq):
    scores = dot_nt(spread_heads(wk * jnp.asarray(SCALE, LOW)), wq)
    scores = scores.reshape(HEADS, PAD, scores.shape[1])
    real = lax.broadcasted_iota(jnp.int32, scores.shape, 1) < MEM
    scores = jnp.where(real, scores, NEG)
    expo = jnp.exp(scores - jnp.max(scores, 1, keepdims=True))
    return expo * (1.0 / jnp.sum(expo, 1, keepdims=True))


def finish_kernel(
    last, weight, put, rows_of, one_ref, own_ref, core_ref, chip_ref, both_ref, wq_ref, small_ref, *rest
):
    if last:
        (z_ref, rout_ref, rlse_ref, mempre_ref, two_ref, wkv_ref, wlow_ref, seqpre_ref, x_ref, feedpre_ref) = rest
    else:
        (z_ref, q_ref, kv_ref, kvmem_ref,
         rout_ref, rlse_ref, mempre_ref, two_ref, wkv_ref, wlow_ref, seqpre_ref, x_ref, feedpre_ref) = rest
    rows, width = wq_ref.shape
    parts = (own_ref, core_ref, chip_ref, both_ref)
    tops = [widened(part[:, width:], 0, width) for part in parts]
    sums = [widened(part[:, width:], HEADS, width) for part in parts]
    top = jnp.maximum(jnp.maximum(tops[0], tops[1]), jnp.maximum(tops[2], tops[3]))
    fades = [jnp.exp(value - top) for value in tops]
    accum = in_pairs([fade * part[:, :width] for fade, part in zip(fades, parts)])
    summed = in_pairs([fade * value for fade, value in zip(fades, sums)])
    rout = accum / summed
    rout_ref[...] = rout
    rlse_ref[...] = top + jnp.log(summed)
    mempre = one_ref[rows:, :] + dot(rout.astype(LOW), weight(7))
    mempre_ref[...] = mempre
    memtwo = norm(mempre, row(small_ref, rows_of, "gain", 1), row(small_ref, rows_of, "shift", 1))
    memlow = memtwo.astype(LOW)
    wk = dot(memlow, weight(9)).astype(LOW)
    wv = dot(memlow, weight(10)).astype(LOW)
    wkv_ref[:, :width] = wk
    wkv_ref[:, width:] = wv
    probs = write_probs(wk, wq_ref[...]).reshape(HEADS * PAD, rows)
    wlow = dot_tn(probs.astype(LOW), spread_heads(wv)).astype(LOW)
    wlow_ref[...] = wlow
    seqpre = one_ref[:rows, :] + dot(wlow, weight(11))
    seqpre_ref[...] = seqpre
    seqtwo = norm(seqpre, row(small_ref, rows_of, "gain", 2), row(small_ref, rows_of, "shift", 2))
    two_ref[:rows, :] = seqtwo
    two_ref[rows:, :] = memtwo
    two = two_ref[...]
    x = two.astype(LOW)
    x_ref[...] = x
    feed = two + row(small_ref, rows_of, "shift", 4)
    for part in range(rows_of["sizes"][1]):
        u = dot(x, weight(("up", part))) + row(small_ref, rows_of, "bias", part)
        feed = feed + dot(gelu_parts(u)[0].astype(LOW), weight("down", part))
    feedpre_ref[...] = feed
    z_ref[...] = norm(feed, row(small_ref, rows_of, "gain", 3), row(small_ref, rows_of, "shift", 3))
    if not last:
        project(z_ref[...], weight, q_ref, kv_ref, kvmem_ref)


def feed_back_kernel(
    share, weight, put, rows_of, grad_ref, feedpre_ref, x_ref, seqpre_ref, wlow_ref, wq_ref, wkv_ref, one_ref,
    small_ref,
    gbias_ref, gsmall_ref, mem_ref, seq_ref, part_ref,
):
    rows, width = wq_ref.shape
    full = grad_ref.shape[0]
    balance = jnp.where(lax.broadcasted_iota(jnp.int32, (full, 1), 0) < rows, 1.0, share)
    grad = grad_ref[...]
    feed, by_unit = norm_back(feedpre_ref[...], row(small_ref, rows_of, "gain", 3), grad)
    gsmall_ref[0:1, :] = total(by_unit * balance)
    gsmall_ref[1:2, :] = total(grad * balance)
    low = feed.astype(LOW)
    low_share = (low.astype(F32) * balance).astype(LOW)
    gsmall_ref[2:3, :] = total(low_share.astype(F32))
    x = x_ref[...]
    two = feed
    high, parts, _ = rows_of["sizes"]
    order = bias_order(width, high, parts)
    piece = width // parts
    for part in range(parts):
        u = dot(x, weight(("up", part))) + row(small_ref, rows_of, "bias", part)
        value, slope = gelu_parts(u)
        put(("down", part), dot_tn(value.astype(LOW), low_share))
        pre = (dot_nt(low, weight("down", part)) * slope).astype(LOW)
        pre_share = (pre.astype(F32) * balance).astype(LOW)
        line = dot(total(pre_share.astype(F32)).astype(LOW), order)
        for j in range(parts):
            gbias_ref[j : j + 1, part * piece : (part + 1) * piece] = line[:, j * piece : (j + 1) * piece]
        put(("up", part), dot_tn(x, pre_share))
        two = two + dot_nt(pre, weight(("up", part)))
    mem_ref[...] = two[rows:]
    grad = two[:rows]
    seq, by_unit = norm_back(seqpre_ref[...], row(small_ref, rows_of, "gain", 2), grad)
    gsmall_ref[3:4, :] = total(by_unit)
    gsmall_ref[4:5, :] = total(grad)
    low = seq.astype(LOW)
    put(11, dot_tn(wlow_ref[...], low))
    out_low = dot_nt(low, weight(11)).astype(LOW)
    wk, wv = wkv_ref[:, :width], wkv_ref[:, width:]
    wq = wq_ref[...]
    probs = write_probs(wk, wq)
    prob_grad = dot_nt(spread_heads(wv), out_low).reshape(probs.shape)
    delta = jnp.sum(probs * prob_grad, 1, keepdims=True)
    score_grad = (probs * (prob_grad - delta)).reshape(HEADS * PAD, rows).astype(LOW)
    wq_low = (dot_tn(score_grad, spread_heads(wk)) * SCALE).astype(LOW)
    part_ref[:PAD, :] = (fold_heads(dot(score_grad, wq)) * SCALE).astype(LOW)
    part_ref[PAD:, :] = fold_heads(dot(probs.reshape(HEADS * PAD, rows).astype(LOW), out_low)).astype(LOW)
    put(8, dot_tn(one_ref[:rows, :].astype(LOW), wq_low))
    seq_ref[...] = seq + dot_nt(wq_low, weight(8))


def read_back_kernel(
    share, weight, put, rows_of, own_ref, core_ref, chip_ref, both_ref, mem_ref, seq_ref, two_ref, mempre_ref, rout_ref, rlse_ref, rq_ref, rkv_ref, one_ref,
    pre_ref, small_ref,
    gsmall_ref, memgrad_ref, seqjoint_ref, part_ref,
):
    rows, width = seq_ref.shape
    summed = in_pairs([part[...].astype(F32) for part in (own_ref, core_ref, chip_ref, both_ref)])
    k_low = summed[:PAD].astype(LOW)
    v_low = summed[PAD:].astype(LOW)
    mem_low = two_ref[rows:, :].astype(LOW)
    put(9, dot_tn(mem_low, k_low) * share)
    put(10, dot_tn(mem_low, v_low) * share)
    grad = mem_ref[...] + dot_nt(k_low, weight(9)) + dot_nt(v_low, weight(10))
    mem, by_unit = norm_back(mempre_ref[...], row(small_ref, rows_of, "gain", 1), grad)
    gsmall_ref[0:1, :] = total(by_unit) * share
    gsmall_ref[1:2, :] = total(grad) * share
    low = mem.astype(LOW)
    rout = rout_ref[...]
    put(7, dot_tn(rout.astype(LOW), low) * share)
    out_low = dot_nt(low, weight(7)).astype(LOW)
    memgrad_ref[...] = mem
    rk, rv = rkv_ref[:, :width], rkv_ref[:, width:]
    rq = spread_heads(rq_ref[...] * jnp.asarray(SCALE, LOW))
    out_wide = spread_heads(out_low)
    delta = jnp.sum(spread_heads(out_low.astype(F32) * rout), -1, keepdims=True)
    mask = head_mask(width)
    lse = jnp.max(jnp.where(mask, rlse_ref[...][None], -BIG).reshape(HEADS * PAD, width), -1, keepdims=True)
    probs = jnp.exp(dot_nt(rq, rk) - lse)
    score_grad = (probs * (dot_nt(out_wide, rv) - delta)).astype(LOW)
    part_ref[...] = (fold_heads(dot(score_grad, rk)) * SCALE).astype(LOW)
    key_low = dot_tn(score_grad, rq).astype(LOW)
    value_low = dot_tn(probs.astype(LOW), out_wide).astype(LOW)
    seq_low = one_ref[:rows, :].astype(LOW)
    put(5, dot_tn(seq_low, key_low))
    put(6, dot_tn(seq_low, value_low))
    grad = seq_ref[...] + dot_nt(key_low, weight(5)) + dot_nt(value_low, weight(6))
    joint, by_unit = norm_back(pre_ref[:rows, :], row(small_ref, rows_of, "gain", 0), grad)
    gsmall_ref[2:3, :] = total(by_unit)
    gsmall_ref[3:4, :] = total(grad)
    seqjoint_ref[...] = joint


def attend_back_kernel(
    share, weight, put, rows_of, z_ref, part_ref, corepart_ref, chippart_ref, bothpart_ref, memgrad_ref, seqjoint_ref, one_ref, pre_ref, att_ref, lse_ref,
    q_ref, own_ref, core_ref, chip_ref, both_ref, kvmem_ref, segs_ref, segq_ref, small_ref,
    gsmall_ref, joint_ref, qgrad_ref, keep_ref, pass_ref, send_ref,
    keys_ref, bound_ref, out_ref, kvgrad_ref,
):
    rows, width = seqjoint_ref.shape
    full = att_ref.shape[0]
    place_keys(keys_ref, own_ref, core_ref, chip_ref, both_ref, kvmem_ref)
    place_bounds(bound_ref, segs_ref, segq_ref[...])
    parts = (part_ref, corepart_ref, chippart_ref, bothpart_ref)
    q_low = in_pairs([part[...].astype(F32) for part in parts]).astype(LOW)
    put(4, dot_tn(one_ref[rows:, :].astype(LOW), q_low) * share)
    grad = memgrad_ref[...] + dot_nt(q_low, weight(4))
    mem, by_unit = norm_back(pre_ref[rows:, :], row(small_ref, rows_of, "gain", 0), grad)
    gsmall_ref[0:1, :] = total(by_unit) * share
    gsmall_ref[1:2, :] = total(grad) * share
    joint_ref[:rows, :] = seqjoint_ref[...]
    joint_ref[rows:, :] = mem
    low = joint_ref[...].astype(LOW)
    balance = jnp.where(lax.broadcasted_iota(jnp.int32, (full, 1), 0) < rows, 1.0, share)
    put(3, dot_tn(att_ref[...], (low.astype(F32) * balance).astype(LOW)))
    out_ref[...] = dot_nt(low, weight(3)).astype(LOW)

    def pair(step, carry):
        lanes = pl.ds(pl.multiple_of(step * 128, 128), 128)
        more = pl.ds(pl.multiple_of(width + step * 128, 128), 128)
        query = q_ref[:, lanes] * jnp.asarray(SCALE, LOW)
        out = out_ref[:, lanes]
        low_balance = jnp.concatenate([balance, balance], 0)
        product = (out.astype(F32) * att_ref[:, lanes].astype(F32)).T
        delta = jnp.concatenate([total(product[:HEAD]), total(product[HEAD:])], 1)
        query = two_heads(query)
        out = two_heads(out)
        keys = keys_ref[:, lanes]
        values = keys_ref[:, more]
        scores = jnp.minimum(dot_nt(keys, query), bound_ref[...])
        probs = jnp.exp(scores - lse_ref[pl.ds(step, 1), :])
        prob_grad = dot_nt(values, out)
        score_grad = (probs * (prob_grad - delta)).astype(LOW)
        qgrad_ref[:, lanes] = (pick_heads(dot_tn(keys, score_grad)) * SCALE).astype(LOW)
        query_share = (query.astype(F32) * low_balance).astype(LOW)
        out_share = (out.astype(F32) * low_balance).astype(LOW)
        kvgrad_ref[:, lanes] = dot(score_grad, query_share).astype(LOW)
        kvgrad_ref[:, more] = dot(probs.astype(LOW), out_share).astype(LOW)
        return carry

    lax.fori_loop(0, width // 128, pair, 0)
    z_low = z_ref[...].astype(LOW)
    put(0, dot_tn(z_low, (qgrad_ref[...].astype(F32) * balance).astype(LOW)))
    me = lax.axis_index("blk")
    for goal, place, other in ((keep_ref, 0, 0), (pass_ref, 0, 2), (send_ref, 0, 1), (send_ref, rows, 3)):
        rest = pl.ds(pl.multiple_of((me ^ other) * rows, rows), rows)
        goal[place : place + rows, :] = kvgrad_ref[rest, :]
    pass_ref[rows:, :] = kvgrad_ref[4 * rows :, :]
    send_ref[2 * rows :, :] = kvgrad_ref[4 * rows :, :]


def input_back_kernel(
    share, weight, put, rows_of, z_ref, joint_ref, qgrad_ref, keep_ref, near_ref, sent_ref, got_ref, *rest
):
    *small_refs, zgrad_ref, kvgrad_ref = rest
    full, width = z_ref.shape
    rows = full - PAD
    balance = jnp.where(lax.broadcasted_iota(jnp.int32, (full, 1), 0) < rows, 1.0, share)
    low = z_ref[...].astype(LOW)
    mine = keep_ref[...].astype(F32) + near_ref[:rows, :].astype(F32)
    kvgrad_ref[:rows, :] = (mine + got_ref[:rows, :].astype(F32)).astype(LOW)
    kvgrad_ref[rows:, :] = (sent_ref[rows:, :].astype(F32) + got_ref[rows:, :].astype(F32)).astype(LOW)
    grads = (qgrad_ref[...], kvgrad_ref[:, :width], kvgrad_ref[:, width:])
    grad = joint_ref[...]
    for part, value in enumerate(grads):
        if part > 0:
            put(part, dot_tn(low, (value.astype(F32) * balance).astype(LOW)))
        grad = grad + dot_nt(value, weight(part))
    zgrad_ref[...] = grad
    if small_refs:
        layers = [[ref[...] for ref in small_refs[k : k + 4]] for k in range(0, len(small_refs), 4)]
        lines = []
        for one, two, three, _ in layers:
            lines.extend([two[2:3] + three[0:1], two[0:1], one[3:4], one[0:1]])
        for one, two, three, _ in layers:
            lines.extend([two[3:4] + three[1:2], two[1:2], one[4:5], one[1:2], one[2:3]])
        lines.extend(bias for _, _, _, bias in layers)
        lines.append(grad[rows:] * share)
        small = jnp.concatenate(lines, 0)
        small = jnp.concatenate([small, jnp.zeros((width - small.shape[0], width), F32)], 0)
        put("small", small.T)


class Order:
    def __init__(self, stages):
        self.stages = stages

    def place(self, number):
        result = 0
        for stage in self.stages:
            result = 2 * result + ((number >> bit_place(stage)) & 1)
        return result

    def mine(self):
        result = 0
        for axis, bit in self.stages:
            result = 2 * result + ((lax.axis_index(axis) >> bit) & 1)
        return result


def call(kernel, name, cost, ins, outs, weights, scratch=(), grads=(), rows_of=None):
    sources, operands, begins = [], [], []
    for source, _, _ in weights.values():
        if not any(source is other for other in sources):
            sources.append(source)
            begins.append(len(operands))
            operands.extend(source[0])
    places, slots = {}, 0
    for key, (source, slot, count) in weights.items():
        which = [source is other for other in sources].index(True)
        places[key] = (which, slot, slots, count)
        slots = slots + count
    high, width = operands[0].shape[2:]
    shards = width // high
    groups, goals, aliases, shapes, made_shapes, grad_places = [], [], {}, [], [], {}
    for number, (keys, order, count, total_slots, into) in enumerate(grads):
        place = 0
        for key in keys:
            grad_places[key] = (number, place, count if key == "down" else 1)
            place += grad_places[key][2]
        halves = 1 if order is None else 2
        arrays, start = into or ((), 0)
        for half, array in enumerate(arrays):
            aliases[len(ins) + len(operands) + len(goals)] = len(shapes) + half
            goals.append(array)
        groups.append((order, halves, len(shapes), start))
        shapes += [jax.ShapeDtypeStruct((shards // halves, total_slots or place, high, width), LOW)] * halves
        made_shapes += [pltpu.VMEM((shards, place, high, width), LOW), pltpu.SemaphoreType.DMA((place, 2))]

    def body(*refs):
        in_refs, refs = refs[: len(ins)], refs[len(ins) :]
        operand_refs, refs = refs[: len(operands)], refs[len(operands) + len(goals) :]
        grad_refs, refs = refs[: len(shapes)], refs[len(shapes) :]
        refs, made_refs = refs[: len(refs) - len(made_shapes)], refs[len(refs) - len(made_shapes) :]
        *refs, buffer, sems = refs
        core = lax.axis_index("blk") % 2
        copies = {}
        for turn, (key, (which, slot, place, count)) in enumerate(places.items()):
            copies[key] = []
            arrays = len(sources[which][0])
            piece = shards // arrays
            for part in range(arrays):
                copy = pltpu.make_async_copy(
                    operand_refs[begins[which] + part].at[:, pl.ds(slot, count)],
                    buffer.at[pl.ds(part * piece, piece), pl.ds(place, count)],
                    sems.at[turn, part],
                )
                copy.start()
                copies[key].append(copy)
        arrived = set()
        offsets = [None if order is None else order.mine() for _, order in sources]
        goal_offsets = [None if order is None else order.mine() for order, _, _, _ in groups]

        def weight(key, part=None):
            if key not in arrived:
                for copy in copies[key]:
                    copy.wait()
                arrived.add(key)
            which, _, place, count = places[key]
            order = sources[which][1]
            span = range(shards) if part is None else range(part * (shards // count), (part + 1) * (shards // count))
            pieces = []
            for shard in span:
                if order is None:
                    at = shard
                else:
                    at = ((shard % 2) ^ core) * (shards // 2) + (order.place(shard) ^ offsets[which])
                pieces.extend(buffer[at, place + slot] for slot in range(count))
            return jnp.concatenate(pieces, 0)

        out = []

        def put(key, grad):
            low = grad.astype(LOW)
            down = isinstance(key, tuple) and key[0] == "down"
            number, slot, count = grad_places["down" if down else key]
            order, halves, begin, start = groups[number]
            made, made_sems = made_refs[2 * number], made_refs[2 * number + 1]
            first = key[1] * (shards // count) if down else 0
            for block in range(low.shape[0] // high):
                shard, inner = first + block // count, block % count
                at = shard
                if order is not None:
                    at = ((shard % 2) ^ core) * (shards // 2) + (order.place(shard) ^ goal_offsets[number])
                made[at, slot + inner] = low[block * high : (block + 1) * high]
            if not down or key[1] == count - 1:
                piece = shards // halves
                for half in range(halves):
                    copy = pltpu.make_async_copy(
                        made.at[pl.ds(half * piece, piece), pl.ds(slot, count)],
                        grad_refs[begin + half].at[:, pl.ds(start + slot, count)],
                        made_sems.at[slot, half],
                    )
                    copy.start()
                    out.append(copy)

        kernel(weight, put, rows_of, *in_refs, *refs)
        for copy in out:
            copy.wait()

    inside, anywhere = pl.BlockSpec(memory_space=pltpu.VMEM), pl.BlockSpec(memory_space=pl.ANY)
    results = pl.pallas_call(
        body,
        out_shape=shapes + [jax.ShapeDtypeStruct(shape, kind) for shape, kind in outs],
        in_specs=[inside] * len(ins) + [anywhere] * (len(operands) + len(goals)),
        out_specs=[anywhere] * len(shapes) + [inside] * len(outs),
        scratch_shapes=list(scratch)
        + [pltpu.VMEM((shards, slots, high, width), LOW), pltpu.SemaphoreType.DMA((len(weights), 2))]
        + made_shapes,
        input_output_aliases=aliases,
        compiler_params=pltpu.CompilerParams(vmem_limit_bytes=VMEM_LIMIT),
        cost_estimate=pl.CostEstimate(flops=int(cost * 1.1e9), bytes_accessed=0, transcendentals=0),
        name=name,
    )(*ins, *operands, *goals)
    made = [results[begin : begin + halves] for _, halves, begin, _ in groups]
    return made + list(results[len(shapes) :])


def flipped(value, bit):
    size = lax.axis_size("blk")
    return lax.ppermute(value, "blk", [(source, source ^ bit) for source in range(size)])


def fence(*arrays):
    return list(lax.optimization_barrier(tuple(arrays)))


def quartet(value):
    return both_chips(value, flipped(value, 2))


def both_chips(own, chip):
    return [own, flipped(own, 1), chip, flipped(chip, 1)]


def bits_of(axis):
    return lax.axis_size(axis).bit_length() - 1


def bit_place(stage):
    axis, bit = stage
    return bit if axis == "blk" else bits_of("blk") + bit


def pack_kernel(attn_ref, *refs):
    inputs, out_ref, (lines_ref, wide_ref, *held, sems) = refs[:5], refs[5], refs[6:]
    count, high, width = out_ref.shape
    origins = (attn_ref.at[0, pl.ds(0, count - 1)],) + inputs
    copies = [
        pltpu.make_async_copy(origin, goal, sems.at[place])
        for place, (origin, goal) in enumerate(zip(origins, [wide_ref] + held))
    ]
    for copy in copies:
        copy.start()
    lines_ref[...] = jnp.zeros(lines_ref.shape, F32)
    for copy in copies:
        copy.wait()
    gain_ref, shift_ref, bias_ref, memory_ref, seg_ref = held
    layers, rows, _ = gain_ref.shape
    place = layers * rows
    for layer in range(layers):
        lines_ref[layer * rows : (layer + 1) * rows, 0:high] = gain_ref[layer]
    rows = shift_ref.shape[0]
    for line in range(rows):
        for layer in range(layers):
            goal = place + layer * rows + line
            lines_ref[goal : goal + 1, 0:high] = shift_ref[line, layer : layer + 1]
    place += layers * rows
    layers, hidden = bias_ref.shape
    for layer in range(layers):
        for part in range(hidden // high):
            lines_ref[place : place + 1, 0:high] = bias_ref[layer : layer + 1, part * high : (part + 1) * high]
            place += 1
    columns = lines_ref[...].T
    lines_ref[...] = columns
    lines_ref[0:high, place : place + MEM] = memory_ref[...]
    out_ref[count - 1] = jnp.zeros((high, width), LOW)
    out_ref[count - 1, :, 0:128] = lines_ref[0:high, :].astype(LOW)
    lines_ref[...] = jnp.zeros(lines_ref.shape, F32)
    for line in range(seg_ref.shape[1] // 128):
        lines_ref[line : line + 1, :] = seg_ref[:, line * 128 : (line + 1) * 128].astype(F32)
    out_ref[count - 1, :, 128:256] = lines_ref[0:high, :].astype(LOW)
    out_ref[0 : count - 1] = wide_ref[...].astype(LOW)


def unpack_kernel(slot, sums_ref, gain_ref, shift_ref, bias_ref, memory_ref, lines_ref):
    high = sums_ref.shape[1]
    lines_ref[...] = jnp.zeros(lines_ref.shape, F32)
    columns = sums_ref[slot, :, 0:128]
    lines_ref[0:high, :] = columns
    lines = lines_ref[...].T
    layers, rows, _ = gain_ref.shape
    place = layers * rows
    for layer in range(layers):
        gain_ref[layer] = lines[layer * rows : (layer + 1) * rows, 0:high]
    rows = shift_ref.shape[0]
    for line in range(rows):
        for layer in range(layers):
            goal = place + layer * rows + line
            shift_ref[line, layer : layer + 1] = lines[goal : goal + 1, 0:high]
    place += layers * rows
    layers, hidden = bias_ref.shape
    for layer in range(layers):
        for part in range(hidden // high):
            bias_ref[layer : layer + 1, part * high : (part + 1) * high] = lines[place : place + 1, 0:high]
            place += 1
    memory_ref[...] = columns[:, place : place + MEM]


def flat(stages):
    return [bit for stage in stages for bit in (stage if isinstance(stage[0], tuple) else (stage,))]


def swapped(value, stage):
    if isinstance(stage[0], tuple):
        mask = sum(1 << bit_place(bit) for bit in stage)
        everyone = lax.axis_size("dp") * lax.axis_size("blk")
        return lax.ppermute(value, ALL, [(source, source ^ mask) for source in range(everyone)])
    axis, bit = stage
    return lax.ppermute(value, axis, [(source, source ^ (1 << bit)) for source in range(lax.axis_size(axis))])


class Gathering:
    def __init__(self, groups):
        self.groups = groups
        self.held = [shard[None] for shard, _, _ in groups]
        self.got, self.turn = {}, 0

    def begin(self):
        done = {}
        for number, (_, stages, first) in enumerate(self.groups):
            if first <= self.turn < first + len(stages) and stages[self.turn - first] is not None:
                self.got[number] = swapped(self.held[number], stages[self.turn - first])
                if self.turn - first + 1 == len(stages) and stages[-1] == ("blk", 0):
                    done[number] = ((self.held[number], self.got.pop(number)), Order([s for s in stages[-2::-1] if s]))
        return done

    def split(self, number, slots, stages):
        held, (shard, done, _) = self.held[number], self.groups[number]
        parts = (held[:, :slots], held[:, slots:])
        for place, part, more in zip((number, len(self.groups)), parts, stages):
            self.groups[place : place + 1] = [(shard, done + more, self.turn - len(done))]
            self.held[place : place + 1] = [part]

    def end(self, *others):
        numbers = list(self.got)
        bundle = fence(*self.got.values(), *others)
        for number, value in zip(numbers, bundle):
            self.held[number] = jnp.concatenate([self.held[number], value])
        self.got = {}
        self.turn += 1
        return bundle[len(numbers) :]


def joined(values):
    return values[0] if len(values) == 1 else jnp.concatenate(values, 1)


class Scattering:
    def __init__(self, arrays, stages):
        self.keeps = [keep for keep, _ in arrays]
        self.sends = [[send for _, send in arrays]]
        self.stages = list(stages)
        self.gots, self.result = None, None

    def begin(self):
        bits = flat([self.stages.pop(0)])
        self.gots = []
        for piece, sends in enumerate(self.sends):
            some = tuple(bit for place, bit in enumerate(bits) if (piece + 1) >> (len(bits) - 1 - place) & 1)
            self.gots.extend(swapped(send, some if len(some) > 1 else some[0]) for send in sends)

    def end(self):
        sums = []
        for place, keep in enumerate(self.keeps):
            value = keep.astype(F32)
            for got in self.gots[place :: len(self.keeps)]:
                value = value + got.astype(F32)
            sums.append(value)
        self.gots = None
        if not self.stages:
            self.result = joined(sums)[0]
            return
        pieces = 2 ** len(flat(self.stages[:1]))
        size = sums[0].shape[0] // pieces
        parts = [joined([value[k * size : (k + 1) * size] for value in sums]).astype(LOW) for k in range(pieces)]
        self.keeps, self.sends = parts[:1], [[part] for part in parts[1:]]


class Background:
    def __init__(self):
        self.sums, self.running, self.staying = {}, [], set()

    def add(self, name, arrays, stages):
        self.sums[name] = Scattering(arrays, stages)

    def begin(self, *names):
        self.staying = {name[1:] for name in names if name[0] == "~"}
        for name in names:
            short = name.rstrip("+")
            if short in self.sums:
                self.sums[short].begin()
                self.running.append(short)
                if short != name:
                    self.staying.add(short)

    def merge(self, name, other):
        one, two = self.sums[name], self.sums[other]
        if one.stages and one.stages == two.stages:
            one.keeps = [joined(one.keeps + two.keeps)]
            one.sends = [[joined(first + second)] for first, second in zip(one.sends, two.sends)]
            two.stages = []

    def end(self, *others):
        ending = [self.sums[name] for name in self.running if name not in self.staying]
        self.running = [name for name in self.running if name in self.staying]
        self.staying = set()
        gots = fence(*[got for run in ending for got in run.gots], *others)
        for run in ending:
            run.gots, gots = gots[: len(run.gots)], gots[len(run.gots) :]
            run.end()
        return gots


def local(
    tokens, segments, memory_init, attn_weights, ffn_in, ffn_out, ffn_bias, norm_gain, norm_shift, out_grad, memory_cot
):
    layers, count, rows, width = attn_weights.shape
    hidden = ffn_in.shape[2]
    per = hidden // width
    everyone = lax.axis_size("dp") * lax.axis_size("blk")
    direct = rows == 16
    core_bit, chip_bits = ("blk", 0), [("blk", bit) for bit in range(1, bits_of("blk"))]
    line_bits, near_bit = [("dp", bit) for bit in reversed(range(1, bits_of("dp")))], [("dp", 0)]

    small = [
        norm_gain.reshape(-1, rows), norm_shift.reshape(-1, rows), ffn_bias.reshape(-1, rows), memory_init
    ]
    starts = [sum(part.shape[0] for part in small[:k]) for k in range(5)]
    gain_rows, shift_rows = norm_gain.shape[1], norm_shift.shape[1]
    small = jnp.concatenate(small, 0).T.astype(LOW)
    numbers = jnp.pad(segments.reshape(-1, 128).astype(LOW), ((0, rows - segments.size // 128), (0, 0)))
    small = jnp.concatenate([jnp.pad(small, ((0, 0), (0, 128 - small.shape[1]))), numbers], 1)
    small = jnp.pad(small, ((0, 0), (0, width - small.shape[1])))[None]

    def rows_of(index):
        return dict(
            gain=starts[0] + index * gain_rows,
            shift=starts[1] + index * shift_rows,
            bias=64 + index * per,
            memory=starts[3],
            sizes=(rows, per, starts[2]),
        )

    def lowered(attn, up, down):
        up = up.astype(LOW).reshape(layers, rows, per, width).transpose(0, 2, 1, 3)
        return attn, up, down.astype(LOW).reshape(layers, per, rows, width)

    attn_low, up_low, down_low = lowered(attn_weights, ffn_in, ffn_out)
    early, middle, late = (0, 1, 2), (3, 8, 4, 5, 6), (7, 9, 10, 11)
    table = {}

    def listed(source, index, keys):
        place = 0
        for key in keys:
            size = per if key == "down" else 1
            table[index, key] = (source, place, size)
            place += size

    ups = tuple(("up", part) for part in range(per))
    if direct:

        def picked(index, keys):
            return [attn_low[index, key][None].astype(LOW) for key in keys]

        far, line = line_bits[:1], line_bits[1:]
        last = [core_bit]
        pause = [None]
        inside, anywhere = pl.BlockSpec(memory_space=pltpu.VMEM), pl.BlockSpec(memory_space=pl.ANY)
        packed_small = (norm_gain, norm_shift.transpose(1, 0, 2), ffn_bias, memory_init.T, segments)
        first_shard = pl.pallas_call(
            pack_kernel,
            out_shape=jax.ShapeDtypeStruct((len(early) + 1, rows, width), LOW),
            in_specs=[pl.BlockSpec(memory_space=pltpu.HBM)] * 6,
            out_specs=inside,
            scratch_shapes=[pltpu.VMEM((128, 128), F32), pltpu.VMEM((len(early), rows, width), F32)]
            + [
                pltpu.VMEM(part.shape, part.dtype)
                for part in packed_small
            ]
            + [pltpu.SemaphoreType.DMA((6,))],
            compiler_params=pltpu.CompilerParams(vmem_limit_bytes=3 * VMEM_LIMIT),
            name="pack",
        )(attn_weights, *packed_small)
        gathering = Gathering(
            [
                (first_shard, far + line + chip_bits + near_bit + last, 0),
                (jnp.concatenate(picked(0, middle)), far + line + near_bit + chip_bits + last, 0),
            ]
        )
        gathering.begin()
        attn_weights, ffn_in, ffn_out = gathering.end(attn_weights, ffn_in, ffn_out)
        attn_low, up_low, down_low = lowered(attn_weights, ffn_in, ffn_out)
        gathering.groups += [
            (
                jnp.concatenate(picked(0, late) + [up_low[0, :1]]),
                far + line + near_bit + chip_bits + last,
                2,
            ),
            (
                jnp.concatenate([down_low[0], up_low[0, 1:2]]),
                chip_bits + far + line + pause + near_bit + last,
                1,
            ),
            (
                jnp.concatenate([up_low[0, 2:]] + picked(1, early)),
                far + chip_bits + pause + near_bit + line + last,
                1,
            ),
            (jnp.concatenate(picked(1, middle)), far + line + pause + chip_bits + near_bit + last, 3),
            (jnp.concatenate(picked(1, late) + [up_low[1]]), far + line, 6),
            (down_low[1], near_bit + far + chip_bits + line + last, 6),
        ]
        gathering.held += [shard[None] for shard, _, _ in gathering.groups[2:]]
        gathering.begin()
        gathering.end()
        for turn in range(2, 4):
            gathering.begin()
            gathering.end()
        found = gathering.begin()
        arrived = fence(*[source[0][1] for source in (found[0], found[1])])
        for number, got in enumerate(arrived):
            found[number] = ((found[number][0][0], got), found[number][1])
        listed(found[0], 0, early + ("small",))
        listed(found[1], 0, middle)
    else:
        packed = jnp.concatenate(
            [attn_low.astype(LOW).reshape(-1, rows, width), up_low.reshape(-1, rows, width), small, down_low.reshape(-1, rows, width)]
        )
        whole = lax.all_gather(packed, ALL)
        split = layers * (count + per) + 1
        square = whole[:, :split].transpose(1, 0, 2, 3).reshape(split, -1, 16, width)
        downs = whole[:, split:].reshape(everyone, layers, per * rows, width).transpose(1, 0, 2, 3)
        downs = downs.reshape(layers, -1, per, 16, width).transpose(0, 2, 1, 3, 4).reshape(layers * per, -1, 16, width)
        source = ((jnp.concatenate([square, downs]).transpose(1, 0, 2, 3),), None)
        for index in range(layers):
            for key in range(count):
                table[index, key] = (source, index * count + key, 1)
            for part in range(per):
                table[index, ("up", part)] = (source, layers * count + index * per + part, 1)
            table[index, "down"] = (source, split + index * per, per)
        table[0, "small"] = (source, split - 1, 1)

    def attn(index, *keys):
        return {key: table[index, key] for key in keys}

    def feed(index):
        return attn(index, *ups, "down")

    length = tokens.shape[1]
    full = length + PAD
    size = lax.axis_size("blk")
    share = 1.0 / size
    me = lax.axis_index("blk")
    seg = segments[0].astype(F32)
    seg_row = jnp.concatenate([seg, jnp.full((PAD,), -1.0, F32)])
    seg_queries = jnp.concatenate([seg_row, seg_row]).reshape(1, -1)
    every = size * length + PAD
    keys_scratch = pltpu.VMEM((every, 2 * width), LOW)
    bound_scratch = pltpu.VMEM((every, 2 * full), F32)
    projected = [((full, width), LOW), ((length, 2 * width), LOW), ((PAD, 2 * width), LOW)]

    smalls, z, q, own, kvmem, *numbers = call(
        first_kernel,
        "first",
        4,
        [tokens[0]],
        [((128, width), F32), ((full, width), F32)] + projected + ([((size, length), F32)] if direct else []),
        attn(0, *early, "small"),
        [pltpu.VMEM((width, 128), F32)] if direct else [],
        rows_of=rows_of(0),
    )
    seg_all = numbers[0] if direct else jnp.concatenate(quartet(segments.astype(LOW))).astype(F32)
    kept = []
    for index in range(layers):
        chip = flipped(own, 2)
        if direct:
            own, chip = gathering.end(own, chip)
            if index > 0:
                gathering.split(6, len(late), [chip_bits + near_bit + [core_bit], near_bit + chip_bits + [core_bit]])
            found = gathering.begin()
            if index > 0:
                listed(found[5], index, middle)
        _, core, _, both = both_chips(own, chip)
        att, lse, pre, first, rq, rkv, wq, part = call(
            attend_kernel,
            f"attend_{index}",
            13,
            [z, q, own, core, chip, both, kvmem, seg_all, seg_queries, smalls],
            [
                ((full, width), LOW), ((width // 128, 2 * full), F32), ((full, width), F32), ((full, width), F32),
                ((PAD, width), LOW),
                ((length, 2 * width), LOW), ((length, width), LOW), ((PAD, width + 128), F32),
            ],
            attn(index, 3, 8, 4, 5, 6),
            [keys_scratch, bound_scratch],
            rows_of=rows_of(index),
        )
        if direct and index > 0:
            (part,) = gathering.end(part)
            gathering.begin()
        part_chip = flipped(part, 2)
        if direct:
            part, part_chip = gathering.end(part, part_chip)
            found = gathering.begin()
            if index == 0:
                listed(found[2], 0, late + ups[:1])
                listed(found[3], 0, ("down",) + ups[1:2])
                listed(found[4], 0, ups[2:])
                for key in early:
                    table[1, key] = (found[4], per - 2 + key, 1)
            else:
                listed(found[6], 1, late)
                listed(found[7], 1, ("down",))
                listed(found[8], 1, ups)
        parts = both_chips(part, part_chip)
        last = index + 1 == layers
        results = call(
            functools.partial(finish_kernel, last),
            f"finish_{index}",
            10,
            [first, *parts, wq, smalls],
            [((full, width), F32)]
            + ([] if last else projected)
            + [
                ((PAD, width), F32), ((PAD, width), F32), ((PAD, width), F32), ((full, width), F32),
                ((PAD, 2 * width), LOW), ((length, width), LOW), ((length, width), F32), ((full, width), LOW),
                ((full, width), F32),
            ],
            attn(index, 7, 9, 10, 11) | feed(index) | ({} if last else attn(index + 1, *early)),
            rows_of=rows_of(index),
        )
        rout, rlse, mempre, second, wkv, wlow, seqpre, x, feedpre = results[-9:]
        kept.append(
            dict(
                z=z, q=q, own=own, kvmem=kvmem, core=core, chip=chip, both=both, att=att, lse=lse, pre=pre, first=first,
                rq=rq, rkv=rkv, wq=wq, rout=rout, rlse=rlse, mempre=mempre, second=second, wkv=wkv, wlow=wlow,
                seqpre=seqpre, x=x, feedpre=feedpre,
            )
        )
        z = results[0]
        if not last:
            q, own, kvmem = results[1:4]
            if direct:
                q, own, kvmem = gathering.end(q, own, kvmem)
                gathering.begin()
    final = z
    grad = jnp.concatenate(
        [out_grad[0].astype(F32), jnp.pad(memory_cot[0].astype(F32), ((0, PAD - MEM), (0, 0)))]
    )
    background = Background()
    y, x, upward = near_bit, chip_bits, line_bits[::-1]
    orders = {
        "up_1": y + upward + x,
        "up_0": y + upward + x,
        "down_1": upward[:1] + y + upward[1:] + x,
        "down_0": upward[:1] + y + upward[1:] + x,
        "first_1": y + upward + x,
        "second_1": x + upward[:1] + y + upward[1:],
        "second_0": y + x + [tuple(upward)],
        "last": [tuple(y + x), tuple(upward)],
    }

    def order_of(name):
        return orders.get(name, y + x + upward)

    def group(name, keys, slots=None, into=None):
        if not direct:
            return (keys, None, per, None, None)
        return (keys, Order(flat(order_of(name))), per, slots, into)

    group_keys = [ups + (11,), ("down", 8), (9, 10, 7, 5, 6), (4, 3, 0), (1, 2)]
    made = [None] * layers
    for index in reversed(range(layers)):
        k = kept[index]
        names = {name: f"{name}_{index}" for name in ("up", "down", "first", "second")}
        end_name = names["second"] if index > 0 else "last"
        plan = iter(PLAN[index])

        def start(name, arrays):
            if direct:
                background.add(name, [arrays], [core_bit] + order_of(name))

        grads_up, grads_down, gbias, small_one, mem, seq, part = call(
            functools.partial(feed_back_kernel, share),
            f"feed_back_{index}",
            11,
            [grad, k["feedpre"], k["x"], k["seqpre"], k["wlow"], k["wq"], k["wkv"], k["first"], smalls],
            [
                ((per, width), F32),
                ((5, width), F32), ((PAD, width), F32), ((length, width), F32), ((2 * PAD, width), LOW),
            ],
            feed(index) | attn(index, 11, 8),
            grads=[
                group(names["up"], group_keys[0]),
                group(names["down"], group_keys[1]),
            ],
            rows_of=rows_of(index),
        )
        halves = len(grads_up)
        part, mem, seq, *both = background.end(part, mem, seq, *grads_up, *grads_down)
        grads_up, grads_down = both[:halves], both[halves:]
        start(names["up"], grads_up)
        start(names["down"], grads_down)
        if index + 1 < layers:
            start(*waiting)
        background.begin(*next(plan))
        part, chip = background.end(part, flipped(part, 2))
        background.begin(*next(plan))
        parts = both_chips(part, chip)
        grads_read, small_two, mem, seq, part = call(
            functools.partial(read_back_kernel, share),
            f"read_back_{index}",
            4,
            [*parts, mem, seq, k["second"], k["mempre"], k["rout"], k["rlse"], k["rq"], k["rkv"],
             k["first"], k["pre"], smalls],
            [((4, width), F32), ((PAD, width), F32), ((length, width), F32), ((PAD, width), LOW)],
            attn(index, 9, 10, 7, 5, 6),
            grads=[group(names["first"], group_keys[2])],
            rows_of=rows_of(index),
        )
        mem, seq, part, chip, *grads_read = background.end(mem, seq, part, flipped(part, 2), *grads_read)
        start(names["first"], grads_read)
        background.begin(*next(plan))
        parts = both_chips(part, chip)
        grads_attend, small_three, joint, qgrad, keep, pass_on, send = call(
            functools.partial(attend_back_kernel, share),
            f"attend_back_{index}",
            14,
            [k["z"], *parts, mem, seq, k["first"], k["pre"], k["att"], k["lse"], k["q"], k["own"], k["core"], k["chip"],
             k["both"], k["kvmem"], seg_all, seg_queries, smalls],
            [((2, width), F32), ((full, width), F32), ((full, width), LOW),
             ((length, 2 * width), LOW), ((length + PAD, 2 * width), LOW), ((2 * length + PAD, 2 * width), LOW)],
            attn(index, 4, 3),
            [keys_scratch, bound_scratch, pltpu.VMEM((full, width), LOW), keys_scratch],
            grads=[group(names["second"], group_keys[3], 5 if index > 0 else 3)],
            rows_of=rows_of(index),
        )
        pass_on, send, *grads_attend = background.end(pass_on, send, *grads_attend)
        if index == 0:
            start(names["second"], grads_attend)
        background.begin(*next(plan))
        near = flipped(send, 1)
        theirs = (pass_on.astype(F32) + near[length:].astype(F32)).astype(LOW)
        got = flipped(theirs, 2)
        got, theirs = background.end(got, theirs)
        background.begin(*next(plan))
        made[index] = dict(small=[small_one, small_two, small_three], bias=gbias)
        tiny = sum([m["small"] + [m["bias"]] for m in made], []) if index == 0 else []
        grads_last, grad = call(
            functools.partial(input_back_kernel, share),
            f"input_back_{index}",
            3,
            [k["z"], joint, qgrad, keep, near, theirs, got] + tiny,
            [((full, width), F32)],
            attn(index, 0, 1, 2),
            [pltpu.VMEM((full, 2 * width), LOW)],
            grads=[
                group(
                    end_name,
                    group_keys[4] + (("small",) if tiny else ()),
                    *((5, (grads_attend, 3)) if index > 0 else ()),
                )
            ],
            rows_of=rows_of(index),
        )
        waiting = (end_name, grads_last)
        made[index]["grads"] = (grads_up, grads_down, grads_read, grads_attend, grads_last)

    mine = [{} for _ in range(layers)]
    if direct:
        start("last", grads_last)
        background.begin(*next(plan))
        background.end()
        ffn_grads = ()
        for moves in plan:
            background.begin(*moves)
            ffn_grads = background.end(*ffn_grads)
            background.merge("last", "second_0")
            if not ffn_grads:
                ups_grads, down_grads = [], []
                for index in range(layers):
                    value = background.sums[f"up_{index}"].result
                    ups_grads.append(jnp.concatenate([value[part] for part in range(per)], -1))
                    down_grads.append(background.sums[f"down_{index}"].result[:per].reshape(per * rows, width))
                ffn_grads = [jnp.stack(ups_grads), jnp.stack(down_grads)]
        for index in range(layers):
            wanted = [f"{name}_{index}" for name in ("up", "down", "first", "second")] + (["last"] if index == 0 else [])
            if index == 0:
                both = last_sums = background.sums["last"].result
                background.sums["last"].result, background.sums["second_0"].result = both[:3], both[3:]
            results = [background.sums[name].result for name in wanted]
            keys = list(group_keys[:4])
            if index > 0:
                keys[3] = keys[3] + group_keys[4]
            else:
                keys.append(group_keys[4] + ("small",))
            for result, held in zip(results, keys):
                place = 0
                for key in held:
                    number = per if key == "down" else 1
                    mine[index][key] = result[place : place + number].reshape(number * rows, width)
                    place += number
    else:
        outgoing, order = [], []
        for index, m in enumerate(made):
            held = sum(group_keys, ()) + (("small",) if index == 0 else ())
            stack = jnp.concatenate([part[0] for part in m["grads"]], 1).transpose(1, 0, 2, 3)
            place = 0
            for key in held:
                if key == "down":
                    downs = stack[place : place + per].transpose(1, 0, 2, 3).reshape(everyone, per, rows, width)
                    outgoing.append(downs.transpose(1, 0, 2, 3).reshape(per, width, width))
                    order.extend((index, ("down", part)) for part in range(per))
                    place += per
                else:
                    outgoing.append(stack[place].reshape(1, width, width))
                    order.append((index, key))
                    place += 1
        result = lax.psum_scatter(jnp.concatenate(outgoing), ALL, scatter_dimension=1, tiled=True).astype(F32)
        for place, (index, key) in enumerate(order):
            mine[index][key] = result[place]
        for m in mine:
            m["down"] = jnp.concatenate([m["down", part] for part in range(per)])
    if not direct:
        ffn_grads = [
            jnp.stack([jnp.concatenate([m["up", part] for part in range(per)], -1) for m in mine]),
            jnp.stack([m["down"] for m in mine]),
        ]
    if direct:
        small_grads = pl.pallas_call(
            functools.partial(unpack_kernel, 2),
            out_shape=[
                jax.ShapeDtypeStruct(part.shape, F32) for part in packed_small[:4]
            ],
            in_specs=[inside],
            out_specs=[inside] * 4,
            scratch_shapes=[pltpu.VMEM((128, 128), F32)],
            compiler_params=pltpu.CompilerParams(vmem_limit_bytes=VMEM_LIMIT),
            name="unpack",
        )(last_sums)
        small_grads = [small_grads[0], small_grads[1].transpose(1, 0, 2), small_grads[2], small_grads[3].T]
    else:
        back = mine[0]["small"].T
        small_grads = [back[starts[k] : starts[k + 1]].reshape(part.shape) for k, part in enumerate(
            (norm_gain, norm_shift, ffn_bias, memory_init)
        )]
    return (
        final[:length].astype(LOW)[None],
        final[length : length + MEM][None],
        grad[:length][None],
        small_grads[3],
        jnp.stack([jnp.stack([m[key] for key in range(count)]) for m in mine]),
        *ffn_grads,
        small_grads[2],
        small_grads[0],
        small_grads[1],
    )


def solution(mesh):
    in_specs = (
        P("dp", "blk", None),
        P("dp", "blk"),
        P(None, ALL),
        P(None, None, ALL, None),
        P(None, ALL, None),
        P(None, ALL, None),
        P(None, ALL),
        P(None, None, ALL),
        P(None, None, ALL),
        P("dp", "blk", None),
        P("dp", None, None),
    )
    out_specs = (
        P("dp", "blk", None),
        P("dp", None, None),
        P("dp", "blk", None),
        P(None, ALL),
        P(None, None, ALL, None),
        P(None, ALL, None),
        P(None, ALL, None),
        P(None, ALL),
        P(None, None, ALL),
        P(None, None, ALL),
    )
    return jax.shard_map(local, mesh=mesh, in_specs=in_specs, out_specs=out_specs, check_vma=False)
```
